32 devices in a mesh: region: 8 (over z, x), mode: 4 (over y, core).
Axes of the slice: x: 2, y: 2, z: 4, core: 2. Of those that a mesh axis runs over, the one named last changes fastest.
Arguments:
- measured: float32 [8, 256, 256], P('region'), may hold values from 0.05 to 20
- probe_modes: float32 [2, 4, 256, 256], P(None, 'mode'), may hold values from -1.5 to 1.5
- object_bands: float32 [2, 1024, 512], P(None, 'region'), may hold values from -4.2 to 4.2
- scan_offsets: int32 [8, 2], replicated, may hold values from 0 to 767, as said below
- band_owner: int32 [8], replicated, may hold values from 0 to 7, each once
Outputs:
- probe_out: float32 [2, 4, 256, 256], P(None, 'mode')
- object_out: float32 [2, 1024, 512], P(None, 'region')
The draws below stay inside these ranges and needn't reach their ends.
Inputs may be any that keep to these rules, and one draw needn't show every extreme that they name: `scan_offsets`: every frame covers rows r to r + 255 within the bands r // 128 to r // 128 + 2; no band is covered by two frames of one region (frames f * 1 to f + 1 - 1 form region f).
All inputs are finite; a program needn't handle non-finite values.
Results may differ from the reference program's by a relative error of at most 0.0001.
Values sent between devices are 32-bit elements; how exact they have to be, the bound alone decides.
No kernel may reach another device: no remote copies, remote signals or barrier semaphores. Data moves between devices by JAX's collectives and lax.ppermute only.
A program may use at most 64 MiB of HBM per device.

```python
import math
import jax
import jax.numpy as jnp
from jax import lax

N = 256
ITERS = 1
OBJ_X = 512
F_DEV = 1
MODES = 4
FRAMES = 8
OBJ_Y = 1024
N_REGION = 8


def draw_scan_offsets(key, part):
    region_keys = jax.random.split(jax.random.fold_in(key, 11), N_REGION)
    spots = N_REGION - 2 * F_DEV

    def one_region(region_key):
        first_key, second_key, third_key, fourth_key = jax.random.split(region_key, 4)
        chosen = jnp.sort(jax.random.permutation(first_key, spots)[:F_DEV])
        anchors = chosen + 2 * jnp.arange(F_DEV, dtype=jnp.int32)
        anchors = jax.random.permutation(fourth_key, anchors)
        lead_rows = jax.random.randint(second_key, (F_DEV,), 0, N // 2)
        columns = jax.random.randint(third_key, (F_DEV,), 0, OBJ_X - N + 1)
        return jnp.stack([anchors * (N // 2) + lead_rows, columns], axis=1)
    return jax.vmap(one_region)(region_keys).reshape(N_REGION * F_DEV, 2).astype(jnp.int32)


def shard_levels(stream_key, dims, pieces, low, largest):
    gain = 1.0
    for position, shards_of in pieces:
        steps = jax.random.uniform(jax.random.fold_in(jax.random.fold_in(stream_key, 6), position), (shards_of,), jnp.float32, low / len(pieces), largest / len(pieces))
        gain = gain * jnp.repeat(jnp.exp(steps), dims[position] // shards_of).reshape((-1,) + (1,) * (len(dims) - 1 - position))
    return gain


def scatter_about(rng, extent, width, limit, cuts=(), kind=jnp.bfloat16):
    gain = shard_levels(rng, extent, cuts, -0.22, 0.18) if cuts else 1.0
    result = jax.random.normal(rng, extent, jnp.float32) * width * gain
    return jnp.minimum(jnp.maximum(result, -limit), limit).astype(kind)


def setup_inputs(seed: int = 0) -> dict:
    splits = jax.random.split(jax.random.key(seed), 6)
    return {
        "measured": jnp.clip(jnp.exp(math.log(20.0) - 5.9914645 * jax.random.uniform(splits[0], (FRAMES, N, N), jnp.float32) ** shard_levels(splits[0], (FRAMES, N, N), ((0, 8),), -0.2, 0.2)), 0.05, 20.0),
        "probe_modes": scatter_about(splits[1], (2, MODES, N, N), 0.25, 1.5, ((1, 4),), jnp.float32),
        "object_bands": scatter_about(splits[2], (2, OBJ_Y, OBJ_X), 0.7, 4.2, ((1, 8),), jnp.float32),
        "scan_offsets": draw_scan_offsets(jax.random.fold_in(splits[5], 71), 0),
        "band_owner": jax.random.permutation(splits[4], N_REGION).astype(jnp.int32),
    }


intensity_offset = 0.1
probe_damping = 1.0
object_damping = 1.0

def to_complex(planes):
    return lax.complex(planes[0], planes[1])

def wave_change(probe_wave, window_wave, measured_frame):
    exit_waves = probe_wave * window_wave[None]
    far_field = jnp.fft.fft2(exit_waves, norm='ortho')
    intensity = lax.optimization_barrier(jnp.sum(jnp.real(far_field) ** 2 + jnp.imag(far_field) ** 2, axis=0))
    factor = jnp.sqrt(measured_frame) / jnp.sqrt(intensity + intensity_offset) - 1.0
    return jnp.fft.ifft2(far_field * factor[None], norm='ortho')

def reference(measured, probe_modes, object_bands, scan_offsets, band_owner):
    band_rows = N // 2
    stored = object_bands.reshape(2, N_REGION, band_rows, OBJ_X)
    ordered = jnp.take(stored, band_owner, axis=1).reshape(2, N_REGION * band_rows, OBJ_X)
    object_image = to_complex(ordered)
    probe_wave = to_complex(probe_modes)

    def window_of(offset):
        return lax.dynamic_slice(object_image, (offset[0], offset[1]), (N, N))

    def add_power(summed, offset):
        window_wave = window_of(offset)
        return (summed + jnp.real(window_wave) ** 2 + jnp.imag(window_wave) ** 2, None)
    object_power, unused = lax.scan(add_power, jnp.zeros((N, N), jnp.float32), scan_offsets)
    for iteration in range(ITERS):

        def add_gradient(summed, inputs):
            offset, measured_frame = inputs
            window_wave = window_of(offset)
            change = wave_change(probe_wave, window_wave, measured_frame)
            return (summed + jnp.conj(window_wave)[None] * change, None)
        gradient, unused = lax.scan(add_gradient, jnp.zeros_like(probe_wave), (scan_offsets, measured))
        probe_wave = probe_wave + gradient / (object_power + probe_damping)
    density_frame = lax.optimization_barrier(jnp.sum(jnp.real(probe_wave) ** 2 + jnp.imag(probe_wave) ** 2, axis=0))

    def add_update(totals, inputs):
        numerator, density = totals
        offset, measured_frame = inputs
        window_wave = window_of(offset)
        change = wave_change(probe_wave, window_wave, measured_frame)
        update_term = lax.optimization_barrier(jnp.sum(jnp.conj(probe_wave) * change, axis=0))
        corner = (offset[0], offset[1])
        numerator = lax.dynamic_update_slice(numerator, lax.dynamic_slice(numerator, corner, (N, N)) + update_term, corner)
        density = lax.dynamic_update_slice(density, lax.dynamic_slice(density, corner, (N, N)) + density_frame, corner)
        return ((numerator, density), None)
    start_totals = (jnp.zeros_like(object_image), jnp.zeros(object_image.shape, jnp.float32))
    (numerator, density), unused = lax.scan(add_update, start_totals, (scan_offsets, measured))
    updated = object_image + numerator / (density + object_damping)
    planes = jnp.stack([jnp.real(updated), jnp.imag(updated)])
    restored = jnp.zeros_like(stored).at[:, band_owner].set(planes.reshape(2, N_REGION, band_rows, OBJ_X))
    probe_planes = jnp.stack([jnp.real(probe_wave), jnp.imag(probe_wave)])
    return (probe_planes, restored.reshape(2, N_REGION * band_rows, OBJ_X))
```

```python
import functools
import math

import jax
import jax.numpy as jnp
import ml_dtypes
import numpy as np
from jax import lax
from jax.experimental import pallas as pl
from jax.experimental.pallas import tpu as pltpu
from jax.sharding import PartitionSpec as P

intensity_offset = 0.1
probe_damping = 1.0
object_damping = 1.0
half = jnp.bfloat16
single = jnp.float32
axes = ("region", "mode")
on_chip = pl.BlockSpec(memory_space=pltpu.VMEM)
scalars = pl.BlockSpec(memory_space=pltpu.SMEM)


class Layout:
    def __init__(self, regions, helpers, length, frames, modes, width):
        self.regions, self.helpers = regions, helpers
        self.length, self.frames, self.modes, self.width = length, frames, modes, width
        self.halves = 2 if regions % 2 == 0 and helpers % 2 == 0 else 1
        self.lowers, self.cores = regions // self.halves, helpers // self.halves
        self.local_modes = modes // helpers
        self.band = length // 2
        self.share = self.band // helpers
        self.piece = length // regions
        self.part = length // self.cores

    def place(self):
        region, helper = lax.axis_index("region"), lax.axis_index("mode")
        upper, lower = region // self.lowers, region % self.lowers
        twin, core = helper // self.cores, helper % self.cores
        return upper, lower, twin, core

    def device(self, upper, lower, twin, core):
        return (upper * self.lowers + lower) * self.helpers + twin * self.cores + core

    def everyone(self):
        for upper in range(self.halves):
            for lower in range(self.lowers):
                for twin in range(self.halves):
                    for core in range(self.cores):
                        yield upper, lower, twin, core

    def cubes(self):
        return [
            [
                self.device(upper, lower, twin, core)
                for twin in range(self.halves)
                for lower in range(self.lowers)
            ]
            for upper in range(self.halves)
            for core in range(self.cores)
        ]

    def from_upper(self, array, step):
        pairs = [
            (self.device((u + step) % self.halves, l, t, c), self.device(u, l, t, c))
            for u, l, t, c in self.everyone()
        ]
        return lax.ppermute(array, axes, pairs)

    def from_core(self, array, step):
        pairs = [
            (self.device(u, l, t, (c + step) % self.cores), self.device(u, l, t, c))
            for u, l, t, c in self.everyone()
        ]
        return lax.ppermute(array, axes, pairs)

    def within_cube(self, array):
        return lax.all_to_all(
            array, axes, split_axis=0, concat_axis=0, tiled=True, axis_index_groups=self.cubes()
        )


def fourier_tables(length, cores):
    positions = np.arange(length)
    angles = (positions[:, None] * positions[None, :] % length) * (2.0 * math.pi / length)
    cosine, sine = np.cos(angles) / math.sqrt(length), np.sin(angles) / math.sqrt(length)
    plus = np.block([[cosine, -sine], [sine, cosine]])
    minus = np.block([[cosine, sine], [-sine, cosine]])
    rows = [
        np.concatenate([block, length + block]) for block in np.split(positions, cores)
    ]
    minus_parts = np.stack([minus[taken] for taken in rows])
    plus_parts = np.stack([plus[:, taken] for taken in rows])

    def pair(table):
        lead = table.astype(ml_dtypes.bfloat16)
        return np.stack([lead, (table - lead.astype(np.float64)).astype(ml_dtypes.bfloat16)])

    return pair(plus), pair(minus), pair(plus_parts), pair(minus_parts)


def split(values):
    lead = values.astype(half)
    return lead, (values - lead.astype(single)).astype(half)


def dot(left, right):
    return jnp.dot(left, right, preferred_element_type=single)


def from_left(table, values):
    lead, trail = split(values)
    return dot(table[0], lead) + dot(table[1], lead) + dot(table[0], trail)


def from_right(values, table):
    lead, trail = split(values)
    return dot(lead, table[0]) + dot(lead, table[1]) + dot(trail, table[0])


def beside(stacked):
    rows = stacked.shape[0] // 2
    return jnp.concatenate([stacked[:rows], stacked[rows:]], axis=1)


def above(planes):
    columns = planes.shape[1] // 2
    return jnp.concatenate([planes[:, :columns], planes[:, columns:]], axis=0)


def band_of_block(owner, block, layout):
    band = jnp.int32(0)
    for candidate in range(layout.regions):
        band = jnp.where(owner[candidate] == block, candidate, band)
    return band


def frame_over(offsets, region, band, layout):
    row, column = offsets[region * layout.frames, 0], offsets[region * layout.frames, 1]
    for extra in range(1, layout.frames):
        index = region * layout.frames + extra
        anchor = offsets[index, 0] // layout.band
        over = (anchor <= band) & (band <= anchor + 2)
        row = jnp.where(over, offsets[index, 0], row)
        column = jnp.where(over, offsets[index, 1], column)
    return row, column


def cut_kernel(layout, offsets, owner, *refs):
    blocks, out = refs[:-1], refs[-1]
    upper, lower, _, _ = layout.place()
    rows = 2 * layout.share
    for entry, block in enumerate(blocks):
        number = (upper + entry) % layout.halves * layout.lowers + lower
        band = band_of_block(owner, number, layout)
        values = block[...].reshape(rows, layout.width)
        for region in range(layout.regions):
            _, column = frame_over(offsets, region, band, layout)
            shift = (layout.width - column) % layout.width
            moved = pltpu.roll(values, shift, 1)[:, : layout.length]
            out[region, entry] = moved.reshape(2, layout.share, layout.length)


def choose_kernel(layout, offsets, owner, arrived, out):
    upper, lower, twin, core = layout.place()
    rows = lax.broadcasted_iota(jnp.int32, (layout.share, layout.length), 0)
    for frame in range(layout.frames):
        row = offsets[(twin * layout.lowers + lower) * layout.frames + frame, 0]
        anchor = row // layout.band
        lead = row - anchor * layout.band
        found = []
        for step in range(3):
            block = owner[anchor + step]
            entry = (block // layout.lowers + layout.halves - upper) % layout.halves
            found.append((block % layout.lowers, entry))
        for source in range(layout.halves):
            first = (source * layout.cores + core) * layout.share
            for plane in range(2):
                top, middle, bottom = (
                    arrived[source * layout.lowers + low, entry, plane] for low, entry in found
                )
                out[frame, plane, 0, source] = jnp.where(rows + first >= lead, top, bottom)
                out[frame, plane, 1, source] = middle


def first_kernel(layout, offsets, *refs):
    cores, frames, length = layout.cores, layout.frames, layout.length
    shares = refs[:cores]
    own_measured, other_measured, probes, plus, minus = refs[cores : cores + 5]
    windows, pieces, old_piece, inner, intensity, far = refs[cores + 5 :]
    upper, lower, twin, core = layout.place()
    region = twin * layout.lowers + lower
    plus_table, minus_table = (plus[0], plus[1]), (minus[0], minus[1])
    local = layout.local_modes
    first_mode = (upper * cores + core) * local
    own_frames = upper == twin
    for frame in range(frames):
        row = offsets[region * frames + frame, 0]
        lead = row % layout.band
        for step, share in enumerate(shares):
            inner[:, :, :, (core + step) % cores] = share[frame]
        for plane in range(2):
            wrapped = inner[plane].reshape(length, length)
            windows[frame, plane] = pltpu.roll(wrapped, (length - lead) % length, 0)
        window_real, window_imag = windows[frame, 0], windows[frame, 1]
        intensity[...] = jnp.zeros_like(intensity)

        def forward(mode):
            probe_real, probe_imag = probes[0, mode], probes[1, mode]
            leaving = jnp.concatenate(
                [
                    probe_real * window_real - probe_imag * window_imag,
                    probe_real * window_imag + probe_imag * window_real,
                ],
                axis=0,
            )
            return from_right(beside(from_left(minus_table, leaving)), plus_table)

        def add_mode(step, unused):
            mode = (first_mode + local + step) % layout.modes
            wave = forward(mode)
            intensity[...] += wave[:, :length] ** 2 + wave[:, length:] ** 2
            kept = jnp.maximum(step - (layout.modes - local), 0)
            far[kept] = wave
            return unused

        lax.fori_loop(0, layout.modes, add_mode, 0)
        measured = jnp.where(own_frames, own_measured[frame], other_measured[frame])
        factor = jnp.sqrt(measured) / jnp.sqrt(intensity[...] + intensity_offset) - 1.0
        factors = jnp.concatenate([factor, factor], axis=1)
        power = window_real**2 + window_imag**2
        cut = (layout.regions, layout.piece, length)
        pieces_here = [power]
        for kept in range(local):
            wave = far[kept] * factors
            change = from_left(plus_table, above(from_right(wave, minus_table)))
            change_real, change_imag = change[:length], change[length:]
            pieces_here.append(window_real * change_real + window_imag * change_imag)
            pieces_here.append(window_real * change_imag - window_imag * change_real)
        for channel, values in enumerate(pieces_here):
            if frame == 0:
                pieces[:, channel] = values.reshape(cut)
            else:
                pieces[:, channel] += values.reshape(cut)
    for kept in range(local):
        rows = pl.ds(region * layout.piece, layout.piece)
        for plane in range(2):
            old_piece[kept, plane] = probes[plane, first_mode + kept, rows, :]


def step_kernel(layout, arrived, old_piece, new_piece):
    total = jnp.sum(arrived[...], axis=0)
    damped = total[0] + probe_damping
    for kept in range(layout.local_modes):
        for plane in range(2):
            gradient = total[1 + 2 * kept + plane]
            new_piece[kept, plane] = old_piece[kept, plane] + gradient / damped


def second_kernel(layout, offsets, *refs):
    cores, frames, length = layout.cores, layout.frames, layout.length
    probes = refs[:cores]
    windows, own_measured, other_measured, plus, minus, left_plus, left_minus = refs[
        cores : cores + 7
    ]
    probe_out, probe_power, *others = refs[cores + 7 :]
    shares, (far, inner) = others[:cores], others[cores:]
    upper, lower, twin, core = layout.place()
    region = twin * layout.lowers + lower
    plus_table, minus_table = (plus[0], plus[1]), (minus[0], minus[1])
    part_minus = (left_minus[0, core], left_minus[1, core])
    part_plus = (left_plus[0, core], left_plus[1, core])
    local = layout.local_modes
    part = layout.part
    rows = pl.ds(pl.multiple_of(core * part, part), part)
    listed = [
        (step, entry, kept)
        for step in range(cores)
        for entry in range(layout.halves)
        for kept in range(local)
    ]

    def probe(step, entry, kept, plane):
        return probes[step][:, entry, kept, plane].reshape(length, length)

    own_entry = (twin + layout.halves - upper) % layout.halves
    for kept in range(local):
        for plane in range(2):
            probe_out[plane, kept] = probes[0][:, own_entry, kept, plane].reshape(length, length)
    power = jnp.zeros((length, length), single)
    for place in listed:
        power += probe(*place, 0) ** 2 + probe(*place, 1) ** 2
    probe_power[...] = power
    for frame in range(frames):
        window_real, window_imag = windows[frame, 0], windows[frame, 1]
        intensity = jnp.zeros((part, length), single)
        for number, place in enumerate(listed):
            probe_real, probe_imag = probe(*place, 0), probe(*place, 1)
            leaving = jnp.concatenate(
                [
                    probe_real * window_real - probe_imag * window_imag,
                    probe_real * window_imag + probe_imag * window_real,
                ],
                axis=0,
            )
            wave = from_right(beside(from_left(part_minus, leaving)), plus_table)
            intensity += wave[:, :length] ** 2 + wave[:, length:] ** 2
            far[number] = wave
        measured = jnp.where(upper == twin, own_measured[frame, rows, :], other_measured[frame, rows, :])
        factor = jnp.sqrt(measured) / jnp.sqrt(intensity + intensity_offset) - 1.0
        factors = jnp.concatenate([factor, factor], axis=1)
        numer_real = jnp.zeros((length, length), single)
        numer_imag = jnp.zeros((length, length), single)
        for number, place in enumerate(listed):
            change = from_left(part_plus, above(from_right(far[number] * factors, minus_table)))
            change_real, change_imag = change[:length], change[length:]
            probe_real, probe_imag = probe(*place, 0), probe(*place, 1)
            numer_real += probe_real * change_real + probe_imag * change_imag
            numer_imag += probe_real * change_imag - probe_imag * change_real
        lead = offsets[region * frames + frame, 0] % layout.band
        for plane, values in enumerate((numer_real, numer_imag)):
            turned = pltpu.roll(values, lead, 0)
            inner[plane] = turned.reshape(2, layout.halves, cores, layout.share, length)
        for step, share in enumerate(shares):
            share[frame] = inner[:, :, :, (core + cores - step) % cores]


def post_kernel(layout, offsets, owner, *refs):
    shares, out = refs[:-1], refs[-1]
    upper, lower, twin, _ = layout.place()
    region = twin * layout.lowers + lower
    for low in range(layout.lowers):
        band = band_of_block(owner, upper * layout.lowers + low, layout)
        frame, row = jnp.int32(0), offsets[region * layout.frames, 0]
        for extra in range(1, layout.frames):
            candidate = offsets[region * layout.frames + extra, 0]
            anchor = candidate // layout.band
            over = (anchor <= band) & (band <= anchor + 2)
            frame, row = jnp.where(over, extra, frame), jnp.where(over, candidate, row)
        slot = (band - row // layout.band == 1).astype(jnp.int32)
        for target in range(layout.halves):
            for plane in range(2):
                total = shares[0][frame, plane, slot, target]
                for share in shares[1:]:
                    total += share[frame, plane, slot, target]
                out[target * layout.lowers + low, plane] = total


def update_kernel(layout, offsets, owner, arrived, probe_power, rows_in, rows_out, doubled):
    upper, lower, twin, core = layout.place()
    length, share = layout.length, layout.share
    band = band_of_block(owner, upper * layout.lowers + lower, layout)
    first = (twin * layout.cores + core) * share
    rows = lax.broadcasted_iota(jnp.int32, (share, length), 0) + first
    doubled[0] = probe_power[...]
    doubled[1] = probe_power[...]
    powers = doubled.reshape(2 * length, length)
    total = jnp.zeros((3 * share, layout.width), single)
    blank = jnp.zeros((3 * share, layout.width - length), single)
    for region in range(layout.regions):
        row, column = frame_over(offsets, region, band, layout)
        anchor = row // layout.band
        lead = row - anchor * layout.band
        step = band - anchor
        begin = jnp.where(step == 0, lead, jnp.where((step == 1) | (step == 2), 0, layout.band))
        end = jnp.where(step == 2, lead, layout.band)
        inside = (rows >= begin) & (rows < end)
        slot = (step == 1).astype(jnp.int32)
        start = (slot * layout.band + first + length - lead) % length
        near = powers[pl.ds(pl.multiple_of(start // 8 * 8, 8), share + 8), :]
        near = pltpu.roll(near, (share + 8 - start % 8) % (share + 8), 0)[:share]
        terms = jnp.concatenate([arrived[region, 0], arrived[region, 1], near], axis=0)
        kept = jnp.where(jnp.concatenate([inside] * 3, axis=0), terms, 0.0)
        total += pltpu.roll(jnp.concatenate([kept, blank], axis=1), column, 1)
    damped = total[2 * share :] + object_damping
    for plane in range(2):
        rows_out[plane] = rows_in[plane] + total[plane * share : (plane + 1) * share] / damped


def call(kernel, name, operands, outputs, scratch=(), scalar_count=0):
    shapes = [jax.ShapeDtypeStruct(shape, single) for shape in outputs]
    return pl.pallas_call(
        kernel,
        name=name,
        out_shape=shapes,
        in_specs=[scalars] * scalar_count + [on_chip] * (len(operands) - scalar_count),
        out_specs=[on_chip] * len(shapes),
        scratch_shapes=[pltpu.VMEM(shape, single) for shape in scratch],
        compiler_params=pltpu.CompilerParams(vmem_limit_bytes=50 * 2**20),
    )(*operands)


def body(measured, probe_modes, object_bands, scan_offsets, band_owner):
    layout = Layout(
        lax.axis_size("region"),
        lax.axis_size("mode"),
        measured.shape[1],
        measured.shape[0],
        probe_modes.shape[1] * lax.axis_size("mode"),
        object_bands.shape[2],
    )
    regions, halves, cores = layout.regions, layout.halves, layout.cores
    length, share, piece, frames = layout.length, layout.share, layout.piece, layout.frames
    local = layout.local_modes
    plus, minus, left_plus, left_minus = fourier_tables(length, cores)
    helper = lax.axis_index("mode")

    own_rows = lax.dynamic_slice_in_dim(object_bands, helper * share, share, 1)
    blocks = [own_rows] + [layout.from_upper(own_rows, step) for step in range(1, halves)]
    probes = lax.all_gather(probe_modes, "mode", axis=1, tiled=True)
    other_measured = measured
    if halves > 1:
        pairs = [
            (layout.device(t, l, t, c), layout.device(u, l, t, c))
            for u, l, t, c in layout.everyone()
            if u != t
        ]
        other_measured = lax.ppermute(measured, axes, pairs)

    (cuts,) = call(
        functools.partial(cut_kernel, layout),
        "cut",
        (scan_offsets, band_owner, *blocks),
        [(regions, halves, 2, share, length)],
        scalar_count=2,
    )
    cuts = layout.within_cube(cuts)
    strip = (frames, 2, 2, halves, share, length)
    (chosen,) = call(
        functools.partial(choose_kernel, layout),
        "choose",
        (scan_offsets, band_owner, cuts),
        [strip],
        scalar_count=2,
    )
    strips = [chosen] + [layout.from_core(chosen, step) for step in range(1, cores)]
    inner = (2, 2, halves, cores, share, length)
    windows, pieces, old_piece = call(
        functools.partial(first_kernel, layout),
        "first",
        (scan_offsets, *strips, measured, other_measured, probes, plus, minus),
        [
            (frames, 2, length, length),
            (regions, 1 + 2 * local, piece, length),
            (local, 2, piece, length),
        ],
        scratch=[
            inner,
            (length, length),
            (local, length, 2 * length),
        ],
        scalar_count=1,
    )
    pieces = layout.within_cube(pieces)
    (new_piece,) = call(
        functools.partial(step_kernel, layout),
        "step",
        (pieces, old_piece),
        [(local, 2, piece, length)],
    )
    entries = [new_piece] + [layout.from_upper(new_piece, step) for step in range(1, halves)]
    spread = jnp.broadcast_to(jnp.stack(entries)[None], (regions, halves, local, 2, piece, length))
    gathered = layout.within_cube(spread)
    new_probes = [gathered] + [layout.from_core(gathered, step) for step in range(1, cores)]
    probe_out, probe_power, *shares = call(
        functools.partial(second_kernel, layout),
        "second",
        (
            scan_offsets,
            *new_probes,
            windows,
            measured,
            other_measured,
            plus,
            minus,
            left_plus,
            left_minus,
        ),
        [(2, local, length, length), (length, length)] + [strip] * cores,
        scratch=[
            (layout.modes, layout.part, 2 * length),
            inner,
        ],
        scalar_count=1,
    )
    shares = shares[:1] + [
        layout.from_core(sent, step) for step, sent in enumerate(shares[1:], start=1)
    ]
    (posted,) = call(
        functools.partial(post_kernel, layout),
        "post",
        (scan_offsets, band_owner, *shares),
        [(regions, 2, share, length)],
        scalar_count=2,
    )
    posted = layout.within_cube(posted)
    (new_rows,) = call(
        functools.partial(update_kernel, layout),
        "update",
        (scan_offsets, band_owner, posted, probe_power, own_rows),
        [(2, share, layout.width)],
        scratch=[(2, length, length)],
        scalar_count=2,
    )
    object_out = lax.all_gather(new_rows, "mode", axis=1, tiled=True)
    return probe_out, object_out


def solution(mesh):
    in_specs = (
        P("region", None, None),
        P(None, "mode", None, None),
        P(None, "region", None),
        P(),
        P(),
    )
    out_specs = (P(None, "mode", None, None), P(None, "region", None))
    return jax.shard_map(body, mesh=mesh, in_specs=in_specs, out_specs=out_specs, check_vma=False)
```

```python
import functools
import math

import jax
import jax.numpy as jnp
import ml_dtypes
import numpy as np
from jax import lax
from jax.experimental import pallas as pl
from jax.experimental.pallas import tpu as pltpu
from jax.sharding import PartitionSpec as P

intensity_offset = 0.1
probe_damping = 1.0
object_damping = 1.0
half = jnp.bfloat16
single = jnp.float32
axes = ("region", "mode")
on_chip = pl.BlockSpec(memory_space=pltpu.VMEM)
scalars = pl.BlockSpec(memory_space=pltpu.SMEM)


class Layout:
    def __init__(self, regions, helpers, length, frames, modes, width):
        self.regions, self.helpers = regions, helpers
        self.length, self.frames, self.modes, self.width = length, frames, modes, width
        self.halves = 2 if regions % 2 == 0 and helpers % 2 == 0 else 1
        self.lowers, self.cores = regions // self.halves, helpers // self.halves
        self.local_modes = modes // helpers
        self.band = length // 2
        self.share = self.band // helpers
        self.strip = self.band // self.cores
        self.piece = length // regions
        self.part = length // self.cores

    def place(self):
        region, helper = lax.axis_index("region"), lax.axis_index("mode")
        upper, lower = region // self.lowers, region % self.lowers
        twin, core = helper // self.cores, helper % self.cores
        return upper, lower, twin, core

    def device(self, upper, lower, twin, core):
        return (upper * self.lowers + lower) * self.helpers + twin * self.cores + core

    def everyone(self):
        for upper in range(self.halves):
            for lower in range(self.lowers):
                for twin in range(self.halves):
                    for core in range(self.cores):
                        yield upper, lower, twin, core

    def cubes(self):
        return [
            [
                self.device(upper, lower, twin, core)
                for twin in range(self.halves)
                for lower in range(self.lowers)
            ]
            for upper in range(self.halves)
            for core in range(self.cores)
        ]

    def from_upper(self, array, step):
        pairs = [
            (self.device((u + step) % self.halves, l, t, c), self.device(u, l, t, c))
            for u, l, t, c in self.everyone()
        ]
        return lax.ppermute(array, axes, pairs)

    def from_core(self, array, step):
        pairs = [
            (self.device(u, l, t, (c + step) % self.cores), self.device(u, l, t, c))
            for u, l, t, c in self.everyone()
        ]
        return lax.ppermute(array, axes, pairs)

    def from_twin(self, array, step):
        pairs = [
            (self.device(u, l, (t + step) % self.halves, c), self.device(u, l, t, c))
            for u, l, t, c in self.everyone()
        ]
        return lax.ppermute(array, axes, pairs)

    def within_row(self, array):
        rows = [
            [self.device(upper, lower, twin, core) for lower in range(self.lowers)]
            for upper in range(self.halves)
            for twin in range(self.halves)
            for core in range(self.cores)
        ]
        return lax.all_to_all(
            array, axes, split_axis=0, concat_axis=0, tiled=True, axis_index_groups=rows
        )

    def within_cube(self, array):
        return lax.all_to_all(
            array, axes, split_axis=0, concat_axis=0, tiled=True, axis_index_groups=self.cubes()
        )


def fourier_tables(length, cores):
    positions = np.arange(length)
    angles = (positions[:, None] * positions[None, :] % length) * (2.0 * math.pi / length)
    cosine, sine = np.cos(angles) / math.sqrt(length), np.sin(angles) / math.sqrt(length)
    plus = np.block([[cosine, -sine], [sine, cosine]])
    minus = np.block([[cosine, sine], [-sine, cosine]])
    rows = [
        np.concatenate([block, length + block]) for block in np.split(positions, cores)
    ]
    minus_parts = np.stack([minus[taken] for taken in rows])
    plus_parts = np.stack([plus[:, taken] for taken in rows])

    def pair(table):
        lead = table.astype(ml_dtypes.bfloat16)
        return np.stack([lead, (table - lead.astype(np.float64)).astype(ml_dtypes.bfloat16)])

    return pair(plus), pair(minus), pair(plus_parts), pair(minus_parts)


def split(values):
    lead = values.astype(half)
    return lead, (values - lead.astype(single)).astype(half)


def dot(left, right):
    return jnp.dot(left, right, preferred_element_type=single)


def from_left(table, values):
    lead, trail = split(values)
    return dot(table[0], lead) + dot(table[1], lead) + dot(table[0], trail)


def from_right(values, table):
    lead, trail = split(values)
    return dot(lead, table[0]) + dot(lead, table[1]) + dot(trail, table[0])


def beside(stacked):
    rows = stacked.shape[0] // 2
    return jnp.concatenate([stacked[:rows], stacked[rows:]], axis=1)


def above(planes):
    columns = planes.shape[1] // 2
    return jnp.concatenate([planes[:, :columns], planes[:, columns:]], axis=0)


def band_of_block(owner, block, layout):
    band = jnp.int32(0)
    for candidate in range(layout.regions):
        band = jnp.where(owner[candidate] == block, candidate, band)
    return band


def frame_over(offsets, region, band, layout):
    row, column = offsets[region * layout.frames, 0], offsets[region * layout.frames, 1]
    for extra in range(1, layout.frames):
        index = region * layout.frames + extra
        anchor = offsets[index, 0] // layout.band
        over = (anchor <= band) & (band <= anchor + 2)
        row = jnp.where(over, offsets[index, 0], row)
        column = jnp.where(over, offsets[index, 1], column)
    return row, column


def cut_kernel(layout, offsets, owner, block, measured, out, sent):
    upper, lower, twin, core = layout.place()
    sent[...] = measured[:, pl.ds(pl.multiple_of(core * layout.part, layout.part), layout.part), :]
    band = band_of_block(owner, upper * layout.lowers + lower, layout)
    values = block[...].reshape(2 * layout.strip, layout.width)
    for target in range(layout.lowers):
        _, column = frame_over(offsets, twin * layout.lowers + target, band, layout)
        shift = (layout.width - column) % layout.width
        moved = pltpu.roll(values, shift, 1)[:, : layout.length]
        out[target] = moved.reshape(2, layout.strip, layout.length)


def choose_kernel(layout, offsets, owner, arrived, out):
    upper, lower, twin, core = layout.place()
    rows = lax.broadcasted_iota(jnp.int32, (layout.strip, layout.length), 0) + core * layout.strip
    for frame in range(layout.frames):
        row = offsets[(twin * layout.lowers + lower) * layout.frames + frame, 0]
        anchor = row // layout.band
        lead = row - anchor * layout.band
        blocks = [owner[anchor + step] for step in range(3)]
        lows = [block % layout.lowers for block in blocks]
        here = [block // layout.lowers == upper for block in blocks]
        for plane in range(2):
            top, middle, bottom = (arrived[low, plane] for low in lows)
            first = jnp.where((rows >= lead) & here[0], top, 0.0)
            out[frame, plane, 0] = jnp.where((rows < lead) & here[2], bottom, first)
            out[frame, plane, 1] = jnp.where(here[1], middle, 0.0)


def far_kernel(layout, offsets, *refs):
    cores, halves, frames, length = layout.cores, layout.halves, layout.frames, layout.length
    shares, probes = refs[: cores * halves], refs[cores * halves : (cores + 1) * halves]
    plus, minus, windows, intensity, kept, old_piece, inner = refs[(cores + 1) * halves :]
    upper, lower, twin, core = layout.place()
    region = twin * layout.lowers + lower
    plus_table, minus_table = (plus[0], plus[1]), (minus[0], minus[1])
    rows = pl.ds(pl.multiple_of(region * layout.piece, layout.piece), layout.piece)
    for frame in range(frames):
        lead = offsets[region * frames + frame, 0] % layout.band
        for step in range(cores):
            strip = shares[step * halves][frame]
            for entry in range(1, halves):
                strip += shares[step * halves + entry][frame]
            inner[:, :, (core + step) % cores] = strip
        for plane in range(2):
            wrapped = inner[plane].reshape(length, length)
            windows[frame, plane] = pltpu.roll(wrapped, (length - lead) % length, 0)
        window_real, window_imag = windows[frame, 0], windows[frame, 1]
        total = jnp.zeros((length, length), single)
        for entry, probe in enumerate(probes):
            goes_back = (twin + entry) % halves == upper
            for local in range(layout.local_modes):
                probe_real, probe_imag = probe[0, local], probe[1, local]
                leaving = jnp.concatenate(
                    [
                        probe_real * window_real - probe_imag * window_imag,
                        probe_real * window_imag + probe_imag * window_real,
                    ],
                    axis=0,
                )
                wave = from_right(beside(from_left(minus_table, leaving)), plus_table)
                total += wave[:, :length] ** 2 + wave[:, length:] ** 2

                @pl.when(goes_back)
                def _():
                    kept[frame, local] = wave
                    for plane in range(2):
                        old_piece[local, plane] = probe[plane, local, rows, :]

        intensity[frame] = total


def gradient_kernel(layout, *refs):
    cores, frames, length = layout.cores, layout.frames, layout.length
    intensities, parts = refs[:cores], refs[cores : 2 * cores]
    windows, own_measured, kept, plus, minus, pieces, other_measured = refs[2 * cores :]
    upper, _, twin, core = layout.place()
    plus_table, minus_table = (plus[0], plus[1]), (minus[0], minus[1])
    cut = (layout.regions, layout.piece, length)
    for frame in range(frames):
        window_real, window_imag = windows[frame, 0], windows[frame, 1]
        intensity = intensities[0][frame]
        for more in intensities[1:]:
            intensity += more[frame]
        for step, part in enumerate(parts):
            other_measured[(core + step) % cores] = part[frame]
        measured = other_measured[...].reshape(length, length)
        measured = jnp.where(upper == twin, own_measured[frame], measured)
        factor = jnp.sqrt(measured) / jnp.sqrt(intensity + intensity_offset) - 1.0
        factors = jnp.concatenate([factor, factor], axis=1)
        channels = [window_real**2 + window_imag**2]
        for local in range(layout.local_modes):
            wave = kept[frame, local] * factors
            change = from_left(plus_table, above(from_right(wave, minus_table)))
            change_real, change_imag = change[:length], change[length:]
            channels.append(window_real * change_real + window_imag * change_imag)
            channels.append(window_real * change_imag - window_imag * change_real)
        for channel, values in enumerate(channels):
            if frame == 0:
                pieces[:, channel] = values.reshape(cut)
            else:
                pieces[:, channel] += values.reshape(cut)


def step_kernel(layout, arrived, old_piece, new_piece):
    total = jnp.sum(arrived[...], axis=0)
    damped = total[0] + probe_damping
    for kept in range(layout.local_modes):
        for plane in range(2):
            gradient = total[1 + 2 * kept + plane]
            new_piece[kept, plane] = old_piece[kept, plane] + gradient / damped


def second_kernel(layout, offsets, *refs):
    cores, frames, length = layout.cores, layout.frames, layout.length
    probes = refs[:cores]
    windows, own_measured, part_measured, plus, minus, left_plus, left_minus = refs[
        cores : cores + 7
    ]
    probe_out, probe_power, *others = refs[cores + 7 :]
    shares, (far, inner) = others[:cores], others[cores:]
    upper, lower, twin, core = layout.place()
    region = twin * layout.lowers + lower
    plus_table, minus_table = (plus[0], plus[1]), (minus[0], minus[1])
    part_minus = (left_minus[0, core], left_minus[1, core])
    part_plus = (left_plus[0, core], left_plus[1, core])
    local = layout.local_modes
    part = layout.part
    rows = pl.ds(pl.multiple_of(core * part, part), part)
    listed = [
        (step, entry, kept)
        for step in range(cores)
        for entry in range(layout.halves)
        for kept in range(local)
    ]

    def probe(step, entry, kept, plane):
        return probes[step][:, entry, kept, plane].reshape(length, length)

    own_entry = (twin + layout.halves - upper) % layout.halves
    for kept in range(local):
        for plane in range(2):
            probe_out[plane, kept] = probes[0][:, own_entry, kept, plane].reshape(length, length)
    power = jnp.zeros((length, length), single)
    for place in listed:
        power += probe(*place, 0) ** 2 + probe(*place, 1) ** 2
    probe_power[...] = power
    for frame in range(frames):
        window_real, window_imag = windows[frame, 0], windows[frame, 1]
        intensity = jnp.zeros((part, length), single)
        for number, place in enumerate(listed):
            probe_real, probe_imag = probe(*place, 0), probe(*place, 1)
            leaving = jnp.concatenate(
                [
                    probe_real * window_real - probe_imag * window_imag,
                    probe_real * window_imag + probe_imag * window_real,
                ],
                axis=0,
            )
            wave = from_right(beside(from_left(part_minus, leaving)), plus_table)
            intensity += wave[:, :length] ** 2 + wave[:, length:] ** 2
            far[number] = wave
        measured = jnp.where(upper == twin, own_measured[frame, rows, :], part_measured[frame])
        factor = jnp.sqrt(measured) / jnp.sqrt(intensity + intensity_offset) - 1.0
        factors = jnp.concatenate([factor, factor], axis=1)
        numer_real = jnp.zeros((length, length), single)
        numer_imag = jnp.zeros((length, length), single)
        for number, place in enumerate(listed):
            change = from_left(part_plus, above(from_right(far[number] * factors, minus_table)))
            change_real, change_imag = change[:length], change[length:]
            probe_real, probe_imag = probe(*place, 0), probe(*place, 1)
            numer_real += probe_real * change_real + probe_imag * change_imag
            numer_imag += probe_real * change_imag - probe_imag * change_real
        lead = offsets[region * frames + frame, 0] % layout.band
        for plane, values in enumerate((numer_real, numer_imag)):
            turned = pltpu.roll(values, lead, 0)
            inner[plane] = turned.reshape(2, layout.halves, cores, layout.share, length)
        for step, share in enumerate(shares):
            share[frame] = inner[:, :, :, (core + cores - step) % cores]


def post_kernel(layout, offsets, owner, *refs):
    shares, out = refs[:-1], refs[-1]
    upper, lower, twin, _ = layout.place()
    region = twin * layout.lowers + lower
    for low in range(layout.lowers):
        band = band_of_block(owner, upper * layout.lowers + low, layout)
        frame, row = jnp.int32(0), offsets[region * layout.frames, 0]
        for extra in range(1, layout.frames):
            candidate = offsets[region * layout.frames + extra, 0]
            anchor = candidate // layout.band
            over = (anchor <= band) & (band <= anchor + 2)
            frame, row = jnp.where(over, extra, frame), jnp.where(over, candidate, row)
        slot = (band - row // layout.band == 1).astype(jnp.int32)
        for target in range(layout.halves):
            for plane in range(2):
                total = shares[0][frame, plane, slot, target]
                for share in shares[1:]:
                    total += share[frame, plane, slot, target]
                out[target * layout.lowers + low, plane] = total


def update_kernel(layout, offsets, owner, arrived, probe_power, rows_in, rows_out, doubled):
    upper, lower, twin, core = layout.place()
    length, share = layout.length, layout.share
    band = band_of_block(owner, upper * layout.lowers + lower, layout)
    first = (twin * layout.cores + core) * share
    rows = lax.broadcasted_iota(jnp.int32, (share, length), 0) + first
    doubled[0] = probe_power[...]
    doubled[1] = probe_power[...]
    powers = doubled.reshape(2 * length, length)
    total = jnp.zeros((3 * share, layout.width), single)
    blank = jnp.zeros((3 * share, layout.width - length), single)
    for region in range(layout.regions):
        row, column = frame_over(offsets, region, band, layout)
        anchor = row // layout.band
        lead = row - anchor * layout.band
        step = band - anchor
        begin = jnp.where(step == 0, lead, jnp.where((step == 1) | (step == 2), 0, layout.band))
        end = jnp.where(step == 2, lead, layout.band)
        inside = (rows >= begin) & (rows < end)
        slot = (step == 1).astype(jnp.int32)
        start = (slot * layout.band + first + length - lead) % length
        near = powers[pl.ds(pl.multiple_of(start // 8 * 8, 8), share + 8), :]
        near = pltpu.roll(near, (share + 8 - start % 8) % (share + 8), 0)[:share]
        terms = jnp.concatenate([arrived[region, 0], arrived[region, 1], near], axis=0)
        kept = jnp.where(jnp.concatenate([inside] * 3, axis=0), terms, 0.0)
        total += pltpu.roll(jnp.concatenate([kept, blank], axis=1), column, 1)
    damped = total[2 * share :] + object_damping
    for plane in range(2):
        rows_out[plane] = rows_in[plane] + total[plane * share : (plane + 1) * share] / damped


def call(kernel, name, operands, outputs, scratch=(), scalar_count=0, after=()):
    shapes = [jax.ShapeDtypeStruct(shape, single) for shape in outputs]
    count = len(operands)

    def inner(*refs):
        kernel(*refs[:count], *refs[count + len(after) :])

    return pl.pallas_call(
        inner,
        name=name,
        out_shape=shapes,
        in_specs=[scalars] * scalar_count
        + [on_chip] * (count - scalar_count)
        + [pl.BlockSpec(memory_space=pl.ANY)] * len(after),
        out_specs=[on_chip] * len(shapes),
        scratch_shapes=[pltpu.VMEM(shape, single) for shape in scratch],
        compiler_params=pltpu.CompilerParams(vmem_limit_bytes=50 * 2**20),
    )(*operands, *after)


def body(measured, probe_modes, object_bands, scan_offsets, band_owner):
    layout = Layout(
        lax.axis_size("region"),
        lax.axis_size("mode"),
        measured.shape[1],
        measured.shape[0],
        probe_modes.shape[1] * lax.axis_size("mode"),
        object_bands.shape[2],
    )
    regions, halves, cores = layout.regions, layout.halves, layout.cores
    length, share, piece, frames = layout.length, layout.share, layout.piece, layout.frames
    local = layout.local_modes
    plus, minus, left_plus, left_minus = fourier_tables(length, cores)
    helper = lax.axis_index("mode")
    core = helper % cores

    strip_rows = lax.dynamic_slice_in_dim(object_bands, core * layout.strip, layout.strip, 1)
    probes = [probe_modes] + [layout.from_twin(probe_modes, step) for step in range(1, halves)]
    cuts, part_measured = call(
        functools.partial(cut_kernel, layout),
        "cut",
        (scan_offsets, band_owner, strip_rows, measured),
        [(layout.lowers, 2, layout.strip, length), (frames, layout.part, length)],
        scalar_count=2,
    )
    if halves > 1:
        pairs = [
            (layout.device(t, l, t, c), layout.device(u, l, t, c))
            for u, l, t, c in layout.everyone()
            if u != t
        ]
        part_measured = lax.ppermute(part_measured, axes, pairs)
    measured_parts = [part_measured]
    for step in range(1, cores):
        measured_parts.append(layout.from_core(part_measured, step))
    cuts = layout.within_row(cuts)
    (chosen,) = call(
        functools.partial(choose_kernel, layout),
        "choose",
        (scan_offsets, band_owner, cuts),
        [(frames, 2, 2, layout.strip, length)],
        scalar_count=2,
        after=(part_measured,),
    )
    parts = [chosen] + [layout.from_upper(chosen, step) for step in range(1, halves)]
    strips = list(parts)
    for step in range(1, cores):
        strips += [layout.from_core(part, step) for part in parts]
    windows, intensity, kept, old_piece = call(
        functools.partial(far_kernel, layout),
        "far",
        (scan_offsets, *strips, *probes, plus, minus),
        [
            (frames, 2, length, length),
            (frames, length, length),
            (frames, local, length, 2 * length),
            (local, 2, piece, length),
        ],
        scratch=[(2, 2, cores, layout.strip, length)],
        scalar_count=1,
    )
    intensities = [intensity] + [layout.from_core(intensity, step) for step in range(1, cores)]
    (pieces,) = call(
        functools.partial(gradient_kernel, layout),
        "gradient",
        (*intensities, *measured_parts, windows, measured, kept, plus, minus),
        [(regions, 1 + 2 * local, piece, length)],
        scratch=[(cores, layout.part, length)],
    )
    pieces = layout.within_cube(pieces)
    (new_piece,) = call(
        functools.partial(step_kernel, layout),
        "step",
        (pieces, old_piece),
        [(local, 2, piece, length)],
    )
    entries = [new_piece] + [layout.from_upper(new_piece, step) for step in range(1, halves)]
    spread = jnp.broadcast_to(jnp.stack(entries)[None], (regions, halves, local, 2, piece, length))
    gathered = layout.within_cube(spread)
    strip = (frames, 2, 2, halves, share, length)
    inner = (2, 2, halves, cores, share, length)
    own_rows = lax.dynamic_slice_in_dim(object_bands, helper * share, share, 1)
    new_probes = [gathered] + [layout.from_core(gathered, step) for step in range(1, cores)]
    probe_out, probe_power, *shares = call(
        functools.partial(second_kernel, layout),
        "second",
        (
            scan_offsets,
            *new_probes,
            windows,
            measured,
            part_measured,
            plus,
            minus,
            left_plus,
            left_minus,
        ),
        [(2, local, length, length), (length, length)] + [strip] * cores,
        scratch=[
            (layout.modes, layout.part, 2 * length),
            inner,
        ],
        scalar_count=1,
    )
    shares = shares[:1] + [
        layout.from_core(sent, step) for step, sent in enumerate(shares[1:], start=1)
    ]
    (posted,) = call(
        functools.partial(post_kernel, layout),
        "post",
        (scan_offsets, band_owner, *shares),
        [(regions, 2, share, length)],
        scalar_count=2,
    )
    posted = layout.within_cube(posted)
    (new_rows,) = call(
        functools.partial(update_kernel, layout),
        "update",
        (scan_offsets, band_owner, posted, probe_power, own_rows),
        [(2, share, layout.width)],
        scratch=[(2, length, length)],
        scalar_count=2,
    )
    object_out = lax.all_gather(new_rows, "mode", axis=1, tiled=True)
    return probe_out, object_out


def solution(mesh):
    in_specs = (
        P("region", None, None),
        P(None, "mode", None, None),
        P(None, "region", None),
        P(),
        P(),
    )
    out_specs = (P(None, "mode", None, None), P(None, "region", None))
    return jax.shard_map(body, mesh=mesh, in_specs=in_specs, out_specs=out_specs, check_vma=False)
```

```python
import functools
import math

import jax
import jax.numpy as jnp
import ml_dtypes
import numpy as np
from jax import lax
from jax.experimental import pallas as pl
from jax.experimental.pallas import tpu as pltpu
from jax.sharding import PartitionSpec as P

intensity_offset = 0.1
probe_damping = 1.0
object_damping = 1.0
half = jnp.bfloat16
single = jnp.float32
axes = ("region", "mode")
on_chip = pl.BlockSpec(memory_space=pltpu.VMEM)
scalars = pl.BlockSpec(memory_space=pltpu.SMEM)


class Layout:
    def __init__(self, regions, helpers, length, frames, modes, width):
        self.regions, self.helpers = regions, helpers
        self.length, self.frames, self.modes, self.width = length, frames, modes, width
        self.halves = 2 if regions % 2 == 0 and helpers % 2 == 0 else 1
        self.lowers, self.cores = regions // self.halves, helpers // self.halves
        self.local_modes = modes // helpers
        self.band = length // 2
        self.share = self.band // helpers
        self.strip = self.band // self.cores
        self.piece = length // regions
        self.part = length // self.cores

    def place(self):
        region, helper = lax.axis_index("region"), lax.axis_index("mode")
        upper, lower = region // self.lowers, region % self.lowers
        twin, core = helper // self.cores, helper % self.cores
        return upper, lower, twin, core

    def device(self, upper, lower, twin, core):
        return (upper * self.lowers + lower) * self.helpers + twin * self.cores + core

    def everyone(self):
        for upper in range(self.halves):
            for lower in range(self.lowers):
                for twin in range(self.halves):
                    for core in range(self.cores):
                        yield upper, lower, twin, core

    def cubes(self):
        return [
            [
                self.device(upper, lower, twin, core)
                for twin in range(self.halves)
                for lower in range(self.lowers)
            ]
            for upper in range(self.halves)
            for core in range(self.cores)
        ]

    def from_upper(self, array, step):
        pairs = [
            (self.device((u + step) % self.halves, l, t, c), self.device(u, l, t, c))
            for u, l, t, c in self.everyone()
        ]
        return lax.ppermute(array, axes, pairs)

    def from_core(self, array, step):
        pairs = [
            (self.device(u, l, t, (c + step) % self.cores), self.device(u, l, t, c))
            for u, l, t, c in self.everyone()
        ]
        return lax.ppermute(array, axes, pairs)

    def from_twin(self, array, step):
        pairs = [
            (self.device(u, l, (t + step) % self.halves, c), self.device(u, l, t, c))
            for u, l, t, c in self.everyone()
        ]
        return lax.ppermute(array, axes, pairs)

    def within_row(self, array):
        rows = [
            [self.device(upper, lower, twin, core) for lower in range(self.lowers)]
            for upper in range(self.halves)
            for twin in range(self.halves)
            for core in range(self.cores)
        ]
        return lax.all_to_all(
            array, axes, split_axis=0, concat_axis=0, tiled=True, axis_index_groups=rows
        )

    def within_cube(self, array):
        return lax.all_to_all(
            array, axes, split_axis=0, concat_axis=0, tiled=True, axis_index_groups=self.cubes()
        )


def fourier_tables(length, cores):
    near = np.arange(length // 2)
    forms = []
    for odd in range(2):
        angles = near[:, None] * (2 * near[None, :] + odd) % length * (2.0 * math.pi / length)
        cosine, sine = np.cos(angles) / math.sqrt(length), np.sin(angles) / math.sqrt(length)
        forms.append(np.block([[cosine, -sine], [sine, cosine]]))
    forward = np.stack(forms)
    parts = []
    for core in range(cores):
        wanted = np.split(np.arange(length), cores)[core] % (length // 2)
        columns = np.concatenate([wanted, length // 2 + wanted])
        parts.append(forms[2 * core // cores][:, columns])
    back_parts = np.stack(parts)

    def pair(table):
        lead = table.astype(ml_dtypes.bfloat16)
        return np.stack([lead, (table - lead.astype(np.float64)).astype(ml_dtypes.bfloat16)])

    return (
        pair(forward),
        pair(forward.swapaxes(1, 2)),
        pair(back_parts.swapaxes(1, 2)),
        pair(back_parts),
    )


def split(values):
    lead = values.astype(half)
    return lead, (values - lead.astype(single)).astype(half)


def dot(left, right):
    return jnp.dot(left, right, preferred_element_type=single)


def from_left(table, values):
    lead, trail = split(values)
    return dot(table[0], lead) + dot(table[1], lead) + dot(table[0], trail)


def from_right(values, table):
    lead, trail = split(values)
    return dot(lead, table[0]) + dot(lead, table[1]) + dot(trail, table[0])


def beside(left, right):
    return jnp.concatenate([left, right], axis=1)


def above(top, bottom):
    return jnp.concatenate([top, bottom], axis=0)


def table_of(tables, number):
    return tables[0, number], tables[1, number]


def columns_forward(real, imag, forward):
    middle = real.shape[1] // 2
    real_left, real_right = real[:, :middle], real[:, middle:]
    imag_left, imag_right = imag[:, :middle], imag[:, middle:]
    even = from_right(beside(real_left + real_right, imag_left + imag_right), table_of(forward, 0))
    odd = from_right(beside(real_left - real_right, imag_left - imag_right), table_of(forward, 1))
    return (
        beside(even[:, :middle], odd[:, :middle]),
        beside(even[:, middle:], odd[:, middle:]),
    )


def columns_back(real, imag, back):
    middle = real.shape[1] // 2
    even = from_right(beside(real[:, :middle], imag[:, :middle]), table_of(back, 0))
    odd = from_right(beside(real[:, middle:], imag[:, middle:]), table_of(back, 1))
    plus, minus = even + odd, even - odd
    return (
        beside(plus[:, :middle], minus[:, :middle]),
        beside(plus[:, middle:], minus[:, middle:]),
    )


def rows_forward(real, imag, back):
    middle = real.shape[0] // 2
    real_top, real_bottom = real[:middle], real[middle:]
    imag_top, imag_bottom = imag[:middle], imag[middle:]
    even = from_left(table_of(back, 0), above(real_top + real_bottom, imag_top + imag_bottom))
    odd = from_left(table_of(back, 1), above(real_top - real_bottom, imag_top - imag_bottom))
    return above(even[:middle], odd[:middle]), above(even[middle:], odd[middle:])


def rows_back(real, imag, forward):
    middle = real.shape[0] // 2
    even = from_left(table_of(forward, 0), above(real[:middle], imag[:middle]))
    odd = from_left(table_of(forward, 1), above(real[middle:], imag[middle:]))
    plus, minus = even + odd, even - odd
    return above(plus[:middle], minus[:middle]), above(plus[middle:], minus[middle:])


def band_of_block(owner, block, layout):
    band = jnp.int32(0)
    for candidate in range(layout.regions):
        band = jnp.where(owner[candidate] == block, candidate, band)
    return band


def frame_over(offsets, region, band, layout):
    row, column = offsets[region * layout.frames, 0], offsets[region * layout.frames, 1]
    for extra in range(1, layout.frames):
        index = region * layout.frames + extra
        anchor = offsets[index, 0] // layout.band
        over = (anchor <= band) & (band <= anchor + 2)
        row = jnp.where(over, offsets[index, 0], row)
        column = jnp.where(over, offsets[index, 1], column)
    return row, column


def cut_kernel(layout, offsets, owner, block, measured, out, sent):
    upper, lower, twin, core = layout.place()
    sent[...] = measured[:, pl.ds(pl.multiple_of(core * layout.part, layout.part), layout.part), :]
    band = band_of_block(owner, upper * layout.lowers + lower, layout)
    values = block[...].reshape(2 * layout.strip, layout.width)
    for target in range(layout.lowers):
        _, column = frame_over(offsets, twin * layout.lowers + target, band, layout)
        shift = (layout.width - column) % layout.width
        moved = pltpu.roll(values, shift, 1)[:, : layout.length]
        out[target] = moved.reshape(2, layout.strip, layout.length)


def choose_kernel(layout, offsets, owner, arrived, out):
    upper, lower, twin, core = layout.place()
    rows = lax.broadcasted_iota(jnp.int32, (layout.strip, layout.length), 0) + core * layout.strip
    for frame in range(layout.frames):
        row = offsets[(twin * layout.lowers + lower) * layout.frames + frame, 0]
        anchor = row // layout.band
        lead = row - anchor * layout.band
        blocks = [owner[anchor + step] for step in range(3)]
        lows = [block % layout.lowers for block in blocks]
        here = [block // layout.lowers == upper for block in blocks]
        for plane in range(2):
            top, middle, bottom = (arrived[low, plane] for low in lows)
            first = jnp.where((rows >= lead) & here[0], top, 0.0)
            out[frame, plane, 0] = jnp.where((rows < lead) & here[2], bottom, first)
            out[frame, plane, 1] = jnp.where(here[1], middle, 0.0)


def far_kernel(layout, offsets, *refs):
    cores, halves, frames, length = layout.cores, layout.halves, layout.frames, layout.length
    shares, probes = refs[: cores * halves], refs[cores * halves : (cores + 1) * halves]
    forward, back, windows, intensity, kept, old_piece, inner = refs[(cores + 1) * halves :]
    upper, lower, twin, core = layout.place()
    region = twin * layout.lowers + lower
    rows = pl.ds(pl.multiple_of(region * layout.piece, layout.piece), layout.piece)
    for frame in range(frames):
        lead = offsets[region * frames + frame, 0] % layout.band
        for step in range(cores):
            strip = shares[step * halves][frame]
            for entry in range(1, halves):
                strip += shares[step * halves + entry][frame]
            inner[:, :, (core + step) % cores] = strip
        for plane in range(2):
            wrapped = inner[plane].reshape(length, length)
            windows[frame, plane] = pltpu.roll(wrapped, (length - lead) % length, 0)
        window_real, window_imag = windows[frame, 0], windows[frame, 1]
        total = jnp.zeros((length, length), single)
        for entry, probe in enumerate(probes):
            goes_back = (twin + entry) % halves == upper
            for local in range(layout.local_modes):
                probe_real, probe_imag = probe[0, local], probe[1, local]
                wave = rows_forward(
                    probe_real * window_real - probe_imag * window_imag,
                    probe_real * window_imag + probe_imag * window_real,
                    back,
                )
                wave_real, wave_imag = columns_forward(*wave, forward)
                total += wave_real**2 + wave_imag**2

                @pl.when(goes_back)
                def _():
                    kept[frame, local, 0] = wave_real
                    kept[frame, local, 1] = wave_imag
                    for plane in range(2):
                        old_piece[local, plane] = probe[plane, local, rows, :]

        intensity[frame] = total


def order_kernel(layout, own_measured, *refs):
    parts, (out, other_measured) = refs[: layout.cores], refs[layout.cores :]
    upper, _, twin, core = layout.place()
    length = layout.length
    rows = lax.broadcasted_iota(jnp.int32, (length, length), 0)
    columns = lax.broadcasted_iota(jnp.int32, (length, length), 1)
    middle = length // 2
    pick_rows = (columns == jnp.where(rows < middle, 2 * rows, 2 * (rows - middle) + 1)).astype(half)
    pick_columns = (rows == jnp.where(columns < middle, 2 * columns, 2 * (columns - middle) + 1)).astype(half)

    def exact(product, values):
        lead, rest = split(values)
        trail = (values - lead.astype(single) - rest.astype(single)).astype(half)
        return (product(lead) + product(rest)) + product(trail)

    for frame in range(layout.frames):
        for step, part in enumerate(parts):
            other_measured[(core + step) % layout.cores] = part[frame]
        measured = other_measured[...].reshape(length, length)
        measured = jnp.sqrt(jnp.where(upper == twin, own_measured[frame], measured))
        measured = exact(lambda values: dot(pick_rows, values), measured)
        out[frame] = exact(lambda values: dot(values, pick_columns), measured)


def gradient_kernel(layout, *refs):
    cores, frames, length = layout.cores, layout.frames, layout.length
    intensities, (roots, windows, kept, forward, back, pieces) = refs[:cores], refs[cores:]
    cut = (layout.regions, layout.piece, length)
    for frame in range(frames):
        window_real, window_imag = windows[frame, 0], windows[frame, 1]
        intensity = intensities[0][frame]
        for more in intensities[1:]:
            intensity += more[frame]
        factor = roots[frame] / jnp.sqrt(intensity + intensity_offset) - 1.0
        channels = [window_real**2 + window_imag**2]
        for local in range(layout.local_modes):
            wave = columns_back(kept[frame, local, 0] * factor, kept[frame, local, 1] * factor, back)
            change_real, change_imag = rows_back(*wave, forward)
            channels.append(window_real * change_real + window_imag * change_imag)
            channels.append(window_real * change_imag - window_imag * change_real)
        for channel, values in enumerate(channels):
            if frame == 0:
                pieces[:, channel] = values.reshape(cut)
            else:
                pieces[:, channel] += values.reshape(cut)


def step_kernel(layout, arrived, old_piece, new_piece):
    total = jnp.sum(arrived[...], axis=0)
    damped = total[0] + probe_damping
    for kept in range(layout.local_modes):
        for plane in range(2):
            gradient = total[1 + 2 * kept + plane]
            new_piece[kept, plane] = old_piece[kept, plane] + gradient / damped


def second_kernel(layout, offsets, *refs):
    cores, frames, length = layout.cores, layout.frames, layout.length
    probes = refs[:cores]
    windows, roots, forward, back, left_forward, left_back = refs[cores : cores + 6]
    probe_out, probe_power, *others = refs[cores + 6 :]
    shares, (far, inner) = others[:cores], others[cores:]
    upper, lower, twin, core = layout.place()
    region = twin * layout.lowers + lower
    local, part, middle = layout.local_modes, layout.part, length // 2
    rows = pl.ds(pl.multiple_of(core * part, part), part)
    sign = jnp.where(2 * core < cores, 1.0, -1.0)
    listed = [
        (step, entry, kept)
        for step in range(cores)
        for entry in range(layout.halves)
        for kept in range(local)
    ]

    def probe(step, entry, kept, plane):
        return probes[step][:, entry, kept, plane].reshape(length, length)

    def fold(values):
        return values[:middle] + sign * values[middle:]

    own_entry = (twin + layout.halves - upper) % layout.halves
    for kept in range(local):
        for plane in range(2):
            probe_out[plane, kept] = probes[0][:, own_entry, kept, plane].reshape(length, length)
    power = jnp.zeros((length, length), single)
    for place in listed:
        power += probe(*place, 0) ** 2 + probe(*place, 1) ** 2
    probe_power[...] = power
    for frame in range(frames):
        window_real, window_imag = windows[frame, 0], windows[frame, 1]
        intensity = jnp.zeros((part, length), single)
        for number, place in enumerate(listed):
            probe_real, probe_imag = probe(*place, 0), probe(*place, 1)
            leaving = above(
                fold(probe_real * window_real - probe_imag * window_imag),
                fold(probe_real * window_imag + probe_imag * window_real),
            )
            wave = from_left(table_of(left_forward, core), leaving)
            wave_real, wave_imag = columns_forward(wave[:part], wave[part:], forward)
            intensity += wave_real**2 + wave_imag**2
            far[number, 0] = wave_real
            far[number, 1] = wave_imag
        factor = roots[frame, rows, :] / jnp.sqrt(intensity + intensity_offset) - 1.0
        numer_real = jnp.zeros((length, length), single)
        numer_imag = jnp.zeros((length, length), single)
        for number, place in enumerate(listed):
            wave_real, wave_imag = columns_back(far[number, 0] * factor, far[number, 1] * factor, back)
            change = from_left(table_of(left_back, core), above(wave_real, wave_imag))
            change_real = above(change[:middle], sign * change[:middle])
            change_imag = above(change[middle:], sign * change[middle:])
            probe_real, probe_imag = probe(*place, 0), probe(*place, 1)
            numer_real += probe_real * change_real + probe_imag * change_imag
            numer_imag += probe_real * change_imag - probe_imag * change_real
        lead = offsets[region * frames + frame, 0] % layout.band
        for plane, values in enumerate((numer_real, numer_imag)):
            turned = pltpu.roll(values, lead, 0)
            inner[plane] = turned.reshape(2, layout.halves, cores, layout.share, length)
        for step, share in enumerate(shares):
            share[frame] = inner[:, :, :, (core + cores - step) % cores]


def post_kernel(layout, offsets, owner, *refs):
    shares, out = refs[:-1], refs[-1]
    upper, lower, twin, _ = layout.place()
    region = twin * layout.lowers + lower
    for low in range(layout.lowers):
        band = band_of_block(owner, upper * layout.lowers + low, layout)
        frame, row = jnp.int32(0), offsets[region * layout.frames, 0]
        for extra in range(1, layout.frames):
            candidate = offsets[region * layout.frames + extra, 0]
            anchor = candidate // layout.band
            over = (anchor <= band) & (band <= anchor + 2)
            frame, row = jnp.where(over, extra, frame), jnp.where(over, candidate, row)
        slot = (band - row // layout.band == 1).astype(jnp.int32)
        for target in range(layout.halves):
            for plane in range(2):
                total = shares[0][frame, plane, slot, target]
                for share in shares[1:]:
                    total += share[frame, plane, slot, target]
                out[target * layout.lowers + low, plane] = total


def update_kernel(layout, offsets, owner, arrived, probe_power, block, rows_out, doubled):
    upper, lower, twin, core = layout.place()
    length, share = layout.length, layout.share
    band = band_of_block(owner, upper * layout.lowers + lower, layout)
    first = (twin * layout.cores + core) * share
    rows = lax.broadcasted_iota(jnp.int32, (share, length), 0) + first
    doubled[0] = probe_power[...]
    doubled[1] = probe_power[...]
    powers = doubled.reshape(2 * length, length)
    total = jnp.zeros((3 * share, layout.width), single)
    blank = jnp.zeros((3 * share, layout.width - length), single)
    for region in range(layout.regions):
        row, column = frame_over(offsets, region, band, layout)
        anchor = row // layout.band
        lead = row - anchor * layout.band
        step = band - anchor
        begin = jnp.where(step == 0, lead, jnp.where((step == 1) | (step == 2), 0, layout.band))
        end = jnp.where(step == 2, lead, layout.band)
        inside = (rows >= begin) & (rows < end)
        slot = (step == 1).astype(jnp.int32)
        start = (slot * layout.band + first + length - lead) % length
        near = powers[pl.ds(pl.multiple_of(start // 8 * 8, 8), share + 8), :]
        near = pltpu.roll(near, (share + 8 - start % 8) % (share + 8), 0)[:share]
        terms = jnp.concatenate([arrived[region, 0], arrived[region, 1], near], axis=0)
        kept = jnp.where(jnp.concatenate([inside] * 3, axis=0), terms, 0.0)
        total += pltpu.roll(jnp.concatenate([kept, blank], axis=1), column, 1)
    damped = total[2 * share :] + object_damping
    for plane in range(2):
        old = block[plane, pl.ds(pl.multiple_of(first, share), share), :]
        rows_out[plane] = old + total[plane * share : (plane + 1) * share] / damped


def call(kernel, name, operands, outputs, scratch=(), scalar_count=0, after=()):
    shapes = [jax.ShapeDtypeStruct(shape, single) for shape in outputs]
    count = len(operands)

    def inner(*refs):
        kernel(*refs[:count], *refs[count + len(after) :])

    return pl.pallas_call(
        inner,
        name=name,
        out_shape=shapes,
        in_specs=[scalars] * scalar_count
        + [on_chip] * (count - scalar_count)
        + [pl.BlockSpec(memory_space=pl.ANY)] * len(after),
        out_specs=[on_chip] * len(shapes),
        scratch_shapes=[pltpu.VMEM(shape, single) for shape in scratch],
        compiler_params=pltpu.CompilerParams(vmem_limit_bytes=50 * 2**20),
    )(*operands, *after)


def body(measured, probe_modes, object_bands, scan_offsets, band_owner):
    layout = Layout(
        lax.axis_size("region"),
        lax.axis_size("mode"),
        measured.shape[1],
        measured.shape[0],
        probe_modes.shape[1] * lax.axis_size("mode"),
        object_bands.shape[2],
    )
    regions, halves, cores = layout.regions, layout.halves, layout.cores
    length, share, piece, frames = layout.length, layout.share, layout.piece, layout.frames
    local = layout.local_modes
    forward, back, left_forward, left_back = fourier_tables(length, cores)
    helper = lax.axis_index("mode")
    core = helper % cores

    strip_rows = lax.dynamic_slice_in_dim(object_bands, core * layout.strip, layout.strip, 1)
    probes = [probe_modes] + [layout.from_twin(probe_modes, step) for step in range(1, halves)]
    cuts, part_measured = call(
        functools.partial(cut_kernel, layout),
        "cut",
        (scan_offsets, band_owner, strip_rows, measured),
        [(layout.lowers, 2, layout.strip, length), (frames, layout.part, length)],
        scalar_count=2,
    )
    if halves > 1:
        pairs = [
            (layout.device(t, l, t, c), layout.device(u, l, t, c))
            for u, l, t, c in layout.everyone()
            if u != t
        ]
        part_measured = lax.ppermute(part_measured, axes, pairs)
    measured_parts = [part_measured]
    for step in range(1, cores):
        measured_parts.append(layout.from_core(part_measured, step))
    cuts = layout.within_row(cuts)
    (chosen,) = call(
        functools.partial(choose_kernel, layout),
        "choose",
        (scan_offsets, band_owner, cuts),
        [(frames, 2, 2, layout.strip, length)],
        scalar_count=2,
        after=(part_measured,),
    )
    parts = [chosen] + [layout.from_upper(chosen, step) for step in range(1, halves)]
    strips = list(parts)
    for step in range(1, cores):
        strips += [layout.from_core(part, step) for part in parts]
    windows, intensity, kept, old_piece = call(
        functools.partial(far_kernel, layout),
        "far",
        (scan_offsets, *strips, *probes, forward, back),
        [
            (frames, 2, length, length),
            (frames, length, length),
            (frames, local, 2, length, length),
            (local, 2, piece, length),
        ],
        scratch=[(2, 2, cores, layout.strip, length)],
        scalar_count=1,
    )
    (roots,) = call(
        functools.partial(order_kernel, layout),
        "order",
        (measured, *measured_parts),
        [measured.shape],
        scratch=[(cores, layout.part, length)],
    )
    intensities = [intensity] + [layout.from_core(intensity, step) for step in range(1, cores)]
    (pieces,) = call(
        functools.partial(gradient_kernel, layout),
        "gradient",
        (*intensities, roots, windows, kept, forward, back),
        [(regions, 1 + 2 * local, piece, length)],
    )
    pieces = layout.within_cube(pieces)
    (new_piece,) = call(
        functools.partial(step_kernel, layout),
        "step",
        (pieces, old_piece),
        [(local, 2, piece, length)],
    )
    entries = [new_piece] + [layout.from_upper(new_piece, step) for step in range(1, halves)]
    spread = jnp.broadcast_to(jnp.stack(entries)[None], (regions, halves, local, 2, piece, length))
    gathered = layout.within_cube(spread)
    strip = (frames, 2, 2, halves, share, length)
    inner = (2, 2, halves, cores, share, length)
    new_probes = [gathered] + [layout.from_core(gathered, step) for step in range(1, cores)]
    probe_out, probe_power, *shares = call(
        functools.partial(second_kernel, layout),
        "second",
        (
            scan_offsets,
            *new_probes,
            windows,
            roots,
            forward,
            back,
            left_forward,
            left_back,
        ),
        [(2, local, length, length), (length, length)] + [strip] * cores,
        scratch=[
            (layout.modes, 2, layout.part, length),
            inner,
        ],
        scalar_count=1,
    )
    shares = shares[:1] + [
        layout.from_core(sent, step) for step, sent in enumerate(shares[1:], start=1)
    ]
    (posted,) = call(
        functools.partial(post_kernel, layout),
        "post",
        (scan_offsets, band_owner, *shares),
        [(regions, 2, share, length)],
        scalar_count=2,
    )
    posted = layout.within_cube(posted)
    (new_rows,) = call(
        functools.partial(update_kernel, layout),
        "update",
        (scan_offsets, band_owner, posted, probe_power, object_bands),
        [(2, share, layout.width)],
        scratch=[(2, length, length)],
        scalar_count=2,
    )
    object_out = lax.all_gather(new_rows, "mode", axis=1, tiled=True)
    return probe_out, object_out


def solution(mesh):
    in_specs = (
        P("region", None, None),
        P(None, "mode", None, None),
        P(None, "region", None),
        P(),
        P(),
    )
    out_specs = (P(None, "mode", None, None), P(None, "region", None))
    return jax.shard_map(body, mesh=mesh, in_specs=in_specs, out_specs=out_specs, check_vma=False)
```

```python
import functools
import math

import jax
import jax.numpy as jnp
import ml_dtypes
import numpy as np
from jax import lax
from jax.experimental import pallas as pl
from jax.experimental.pallas import tpu as pltpu
from jax.sharding import PartitionSpec as P

intensity_offset = 0.1
probe_damping = 1.0
object_damping = 1.0
half = jnp.bfloat16
single = jnp.float32
axes = ("region", "mode")
lanes = 128
on_chip = pl.BlockSpec(memory_space=pltpu.VMEM)
scalars = pl.BlockSpec(memory_space=pltpu.SMEM)


class Layout:
    def __init__(self, regions, helpers, length, frames, modes, width):
        self.regions, self.helpers = regions, helpers
        self.length, self.frames, self.modes, self.width = length, frames, modes, width
        self.halves = 2 if regions % 2 == 0 and helpers % 2 == 0 else 1
        self.lowers, self.cores = regions // self.halves, helpers // self.halves
        self.local_modes = modes // helpers
        self.band = length // 2
        self.strip = self.band // self.cores
        self.share = self.band // helpers
        self.piece = length // regions
        self.part = length // self.cores

    def place(self):
        region, helper = lax.axis_index("region"), lax.axis_index("mode")
        upper, lower = region // self.lowers, region % self.lowers
        twin, core = helper // self.cores, helper % self.cores
        return upper, lower, twin, core

    def device(self, upper, lower, twin, core):
        return (upper * self.lowers + lower) * self.helpers + twin * self.cores + core

    def everyone(self):
        for upper in range(self.halves):
            for lower in range(self.lowers):
                for twin in range(self.halves):
                    for core in range(self.cores):
                        yield upper, lower, twin, core

    def cubes(self):
        return [
            [
                self.device(upper, lower, twin, core)
                for twin in range(self.halves)
                for lower in range(self.lowers)
            ]
            for upper in range(self.halves)
            for core in range(self.cores)
        ]

    def from_upper(self, array, step):
        pairs = [
            (self.device((u + step) % self.halves, l, t, c), self.device(u, l, t, c))
            for u, l, t, c in self.everyone()
        ]
        return lax.ppermute(array, axes, pairs)

    def from_core(self, array, step):
        pairs = [
            (self.device(u, l, t, (c + step) % self.cores), self.device(u, l, t, c))
            for u, l, t, c in self.everyone()
        ]
        return lax.ppermute(array, axes, pairs)

    def from_twin(self, array, step):
        pairs = [
            (self.device(u, l, (t + step) % self.halves, c), self.device(u, l, t, c))
            for u, l, t, c in self.everyone()
        ]
        return lax.ppermute(array, axes, pairs)

    def across(self, lower, step):
        if self.lowers & (self.lowers - 1) == 0:
            return lower ^ step
        return (lower + step) % self.lowers

    def to_row(self, array, step):
        pairs = [
            (self.device(u, l, t, c), self.device(u, self.across(l, step), t, c))
            for u, l, t, c in self.everyone()
        ]
        return lax.ppermute(array, axes, pairs)

    def within_cube(self, array):
        return lax.all_to_all(
            array, axes, split_axis=0, concat_axis=0, tiled=True, axis_index_groups=self.cubes()
        )


def fourier_tables(length):
    near = np.arange(length // 2)
    forms = []
    for odd in range(2):
        angles = near[:, None] * (2 * near[None, :] + odd) % length * (2.0 * math.pi / length)
        cosine, sine = np.cos(angles) / math.sqrt(length), np.sin(angles) / math.sqrt(length)
        forms.append(np.block([[cosine, -sine], [sine, cosine]]))
    forward = np.stack(forms)

    def pair(table):
        lead = table.astype(ml_dtypes.bfloat16)
        return np.stack([lead, (table - lead.astype(np.float64)).astype(ml_dtypes.bfloat16)])

    return pair(forward), pair(forward.swapaxes(1, 2))


def split(values):
    lead = values.astype(half)
    return lead, (values - lead.astype(single)).astype(half)


def dot(left, right):
    return jnp.dot(left, right, preferred_element_type=single)


def from_left(table, values):
    lead, trail = split(values)
    return dot(table[0], lead) + dot(table[1], lead) + dot(table[0], trail)


def from_right(values, table):
    lead, trail = split(values)
    return dot(lead, table[0]) + dot(lead, table[1]) + dot(trail, table[0])


def beside(left, right):
    return jnp.concatenate([left, right], axis=1)


def above(top, bottom):
    return jnp.concatenate([top, bottom], axis=0)


def table_of(tables, number):
    return tables[0, number], tables[1, number]


def columns_forward(real, imag, forward):
    middle = real.shape[1] // 2
    real_left, real_right = real[:, :middle], real[:, middle:]
    imag_left, imag_right = imag[:, :middle], imag[:, middle:]
    even = from_right(beside(real_left + real_right, imag_left + imag_right), table_of(forward, 0))
    odd = from_right(beside(real_left - real_right, imag_left - imag_right), table_of(forward, 1))
    return (
        beside(even[:, :middle], odd[:, :middle]),
        beside(even[:, middle:], odd[:, middle:]),
    )


def columns_back(real, imag, back):
    middle = real.shape[1] // 2
    even = from_right(beside(real[:, :middle], imag[:, :middle]), table_of(back, 0))
    odd = from_right(beside(real[:, middle:], imag[:, middle:]), table_of(back, 1))
    plus, minus = even + odd, even - odd
    return (
        beside(plus[:, :middle], minus[:, :middle]),
        beside(plus[:, middle:], minus[:, middle:]),
    )


def rows_forward(real, imag, back):
    middle = real.shape[0] // 2
    real_top, real_bottom = real[:middle], real[middle:]
    imag_top, imag_bottom = imag[:middle], imag[middle:]
    even = from_left(table_of(back, 0), above(real_top + real_bottom, imag_top + imag_bottom))
    odd = from_left(table_of(back, 1), above(real_top - real_bottom, imag_top - imag_bottom))
    return above(even[:middle], odd[:middle]), above(even[middle:], odd[middle:])


def rows_back(real, imag, forward):
    middle = real.shape[0] // 2
    even = from_left(table_of(forward, 0), above(real[:middle], imag[:middle]))
    odd = from_left(table_of(forward, 1), above(real[middle:], imag[middle:]))
    plus, minus = even + odd, even - odd
    return above(plus[:middle], minus[:middle]), above(plus[middle:], minus[middle:])


def band_of_block(owner, block, layout):
    band = jnp.int32(0)
    for candidate in range(layout.regions):
        band = jnp.where(owner[candidate] == block, candidate, band)
    return band


def frame_over(offsets, region, band, layout):
    row, column = offsets[0, region * layout.frames], offsets[1, region * layout.frames]
    for extra in range(1, layout.frames):
        index = region * layout.frames + extra
        anchor = offsets[0, index] // layout.band
        over = (anchor <= band) & (band <= anchor + 2)
        row = jnp.where(over, offsets[0, index], row)
        column = jnp.where(over, offsets[1, index], column)
    return row, column


def cut_kernel(layout, corners, owners, block, measured, *refs):
    outs, (sent, taken, offsets, owner, done) = refs[: layout.lowers], refs[layout.lowers :]
    upper, lower, twin, core = layout.place()
    strip = pl.ds(pl.multiple_of(core * layout.strip, layout.strip), layout.strip)
    part = pl.ds(pl.multiple_of(core * layout.part, layout.part), layout.part)
    copies = [
        pltpu.make_async_copy(corners, offsets, done.at[0]),
        pltpu.make_async_copy(owners, owner, done.at[1]),
        pltpu.make_async_copy(block.at[:, strip, :], taken.at[:, :, : layout.width], done.at[2]),
        pltpu.make_async_copy(measured.at[:, part, :], sent, done.at[3]),
    ]
    for copy in copies:
        copy.start()
    for copy in copies[:3]:
        copy.wait()
    band = band_of_block(owner, upper * layout.lowers + lower, layout)
    tiles = layout.length // lanes
    column_in_tile = lax.broadcasted_iota(jnp.int32, (2 * layout.strip, lanes), 1)
    for step, out in enumerate(outs):
        region = twin * layout.lowers + layout.across(lower, step)
        _, column = frame_over(offsets, region, band, layout)
        shift = column % lanes
        begin = pl.multiple_of(column - shift, lanes)
        kept = column_in_tile < lanes - shift
        turned = []
        for tile in range(tiles + 1):
            values = taken[:, :, pl.ds(begin + tile * lanes, lanes)].reshape(2 * layout.strip, lanes)
            turned.append(pltpu.roll(values, (lanes - shift) % lanes, 1))
        for tile in range(tiles):
            values = jnp.where(kept, turned[tile], turned[tile + 1])
            out[:, :, tile * lanes : (tile + 1) * lanes] = values.reshape(2, layout.strip, lanes)
    copies[3].wait()


def choose_kernel(layout, steps, offsets, owner, *refs):
    arrived, (*before, out) = refs[: len(steps)], refs[len(steps) :]
    upper, lower, twin, core = layout.place()
    rows = lax.broadcasted_iota(jnp.int32, (layout.strip, layout.length), 0) + core * layout.strip
    for frame in range(layout.frames):
        row = offsets[0, (twin * layout.lowers + lower) * layout.frames + frame]
        anchor = row // layout.band
        lead = row - anchor * layout.band
        blocks = [owner[anchor + step] for step in range(3)]
        masks = [rows >= lead, rows >= 0, rows < lead]
        for plane in range(2):
            slots = [ref[frame, plane] for ref in before]
            top, bottom = (slots[0][0], slots[0][1]) if before else (0.0, 0.0)
            for block, mask, slot in zip(blocks, masks, (0, 1, 0)):
                here = block // layout.lowers == upper
                values = top if slot == 0 else bottom
                for step, ref in zip(steps, arrived):
                    came = here & (layout.across(block % layout.lowers, step) == lower)
                    values = jnp.where(mask & came, ref[plane], values)
                top, bottom = (values, bottom) if slot == 0 else (top, values)
            out[frame, plane, 0] = top
            out[frame, plane, 1] = bottom


def leave(probe_real, probe_imag, window_real, window_imag, forward, back):
    wave = rows_forward(
        probe_real * window_real - probe_imag * window_imag,
        probe_real * window_imag + probe_imag * window_real,
        back,
    )
    return columns_forward(*wave, forward)


def come_back(far, factor, forward, back):
    return rows_back(*columns_back(far[0] * factor, far[1] * factor, back), forward)


def far_kernel(layout, offsets, *refs):
    cores, halves, frames, length = layout.cores, layout.halves, layout.frames, layout.length
    shares, probes = refs[: cores * halves], refs[cores * halves : (cores + 1) * halves]
    forward, back, windows, intensity, kept, old_pieces, inner = refs[(cores + 1) * halves :]
    upper, lower, twin, core = layout.place()
    region = twin * layout.lowers + lower
    rows = pl.ds(pl.multiple_of(region * layout.piece, layout.piece), layout.piece)
    for entry, probe in enumerate(probes):
        place = (twin + entry + halves - upper) % halves
        for local in range(layout.local_modes):
            for plane in range(2):
                old_pieces[place, local, plane] = probe[plane, local, rows, :]
    for frame in range(frames):
        lead = offsets[0, region * frames + frame] % layout.band
        for step in range(cores):
            strip = shares[step * halves][frame]
            for entry in range(1, halves):
                strip += shares[step * halves + entry][frame]
            inner[:, :, (core + step) % cores] = strip
        for plane in range(2):
            wrapped = inner[plane].reshape(length, length)
            windows[frame, plane] = pltpu.roll(wrapped, (length - lead) % length, 0)
        window = windows[frame, 0], windows[frame, 1]
        total = jnp.zeros((length, length), single)
        for entry, probe in enumerate(probes):
            for local in range(layout.local_modes):
                wave_real, wave_imag = leave(probe[0, local], probe[1, local], *window, forward, back)
                total += wave_real**2 + wave_imag**2

                @pl.when((twin + entry) % halves == upper)
                def _():
                    kept[frame, local, 0] = wave_real
                    kept[frame, local, 1] = wave_imag

        intensity[frame] = total


def order_kernel(layout, own_measured, *refs):
    parts, (out, other_measured) = refs[: layout.cores], refs[layout.cores :]
    upper, _, twin, core = layout.place()
    length = layout.length
    rows = lax.broadcasted_iota(jnp.int32, (length, length), 0)
    columns = lax.broadcasted_iota(jnp.int32, (length, length), 1)
    middle = length // 2
    pick_rows = (columns == jnp.where(rows < middle, 2 * rows, 2 * (rows - middle) + 1)).astype(half)
    pick_columns = (rows == jnp.where(columns < middle, 2 * columns, 2 * (columns - middle) + 1)).astype(half)

    def exact(product, values):
        lead, rest = split(values)
        trail = (values - lead.astype(single) - rest.astype(single)).astype(half)
        return (product(lead) + product(rest)) + product(trail)

    for frame in range(layout.frames):
        for step, part in enumerate(parts):
            other_measured[(core + step) % layout.cores] = part[frame]
        measured = other_measured[...].reshape(length, length)
        measured = jnp.sqrt(jnp.where(upper == twin, own_measured[frame], measured))
        measured = exact(lambda values: dot(pick_rows, values), measured)
        out[frame] = exact(lambda values: dot(values, pick_columns), measured)


def factor_of(root, intensities, frame):
    total = intensities[0][frame]
    for more in intensities[1:]:
        total += more[frame]
    return root[frame] / jnp.sqrt(total + intensity_offset) - 1.0


def gradient_kernel(layout, *refs):
    cores, frames, length, piece = layout.cores, layout.frames, layout.length, layout.piece
    intensities, (roots, windows, kept, forward, back, pieces) = refs[:cores], refs[cores:]
    upper, _, _, _ = layout.place()
    cut = (layout.regions, piece, length)
    part = piece // layout.halves
    for frame in range(frames):
        window_real, window_imag = windows[frame, 0], windows[frame, 1]
        factor = factor_of(roots, intensities, frame)
        channels = []
        for local in range(layout.local_modes):
            change_real, change_imag = come_back(kept[frame, local], factor, forward, back)
            channels.append(window_real * change_real + window_imag * change_imag)
            channels.append(window_real * change_imag - window_imag * change_real)
        channels = [values.reshape(cut) for values in channels]
        power = (window_real**2 + window_imag**2).reshape(cut)
        sent = power[:, :part]
        for other in range(1, layout.halves):
            sent = jnp.where(upper == other, power[:, other * part : (other + 1) * part], sent)
        first = 0
        for values in (*channels, sent):
            rows = slice(first, first + values.shape[1])
            if frame == 0:
                pieces[:, rows] = values
            else:
                pieces[:, rows] += values
            first += values.shape[1]


def sum_kernel(arrived, total):
    total[...] = jnp.sum(arrived[...], axis=0)


def step_kernel(layout, old_pieces, *refs):
    totals, out = refs[:-1], refs[-1]
    upper, _, _, _ = layout.place()
    halves, piece = layout.halves, layout.piece
    planes = 2 * layout.local_modes
    parts = []
    for place in range(halves):
        power = totals[0][planes * piece :]
        for entry in range(1, halves):
            power = jnp.where((upper + entry) % halves == place, totals[entry][planes * piece :], power)
        parts.append(power)
    damped = jnp.concatenate(parts, axis=0) + probe_damping
    for entry, total in enumerate(totals):
        for local in range(layout.local_modes):
            for plane in range(2):
                first = (2 * local + plane) * piece
                stepped = old_pieces[entry, local, plane] + total[first : first + piece] / damped
                for region in range(layout.regions):
                    out[region, entry, local, plane] = stepped


def new_probe(probes, entry, local, plane):
    values = probes[:, entry, local, plane]
    return values.reshape(values.shape[0] * values.shape[1], values.shape[2])


def again_kernel(layout, probes, windows, forward, back, probe_out, probe_power, intensity, fars):
    upper, _, twin, _ = layout.place()
    own_entry = (twin + layout.halves - upper) % layout.halves
    power = jnp.zeros((layout.length, layout.length), single)
    totals = [jnp.zeros((layout.length, layout.length), single) for _ in range(layout.frames)]
    for entry in range(layout.halves):
        for local in range(layout.local_modes):
            probe = [new_probe(probes, entry, local, plane) for plane in range(2)]
            power += probe[0] ** 2 + probe[1] ** 2
            for frame in range(layout.frames):
                wave_real, wave_imag = leave(*probe, windows[frame, 0], windows[frame, 1], forward, back)
                totals[frame] += wave_real**2 + wave_imag**2
                fars[frame, entry, local, 0] = wave_real
                fars[frame, entry, local, 1] = wave_imag
    probe_power[...] = power
    for frame, total in enumerate(totals):
        intensity[frame] = total
    for local in range(layout.local_modes):
        for plane in range(2):
            probe_out[plane, local] = new_probe(probes, own_entry, local, plane)


def terms_kernel(layout, offsets, *refs):
    cores, halves, frames, length = layout.cores, layout.halves, layout.frames, layout.length
    intensities = refs[:cores]
    roots, probes, fars, forward, back, *shares, inner = refs[cores:]
    upper, lower, twin, core = layout.place()
    region = twin * layout.lowers + lower
    for frame in range(frames):
        factor = factor_of(roots, intensities, frame)
        numer_real = jnp.zeros((length, length), single)
        numer_imag = jnp.zeros((length, length), single)
        for entry in range(halves):
            for local in range(layout.local_modes):
                change_real, change_imag = come_back(fars[frame, entry, local], factor, forward, back)
                probe_real, probe_imag = (new_probe(probes, entry, local, plane) for plane in range(2))
                numer_real += probe_real * change_real + probe_imag * change_imag
                numer_imag += probe_real * change_imag - probe_imag * change_real
        lead = offsets[0, region * frames + frame] % layout.band
        for plane, values in enumerate((numer_real, numer_imag)):
            turned = pltpu.roll(values, lead, 0)
            inner[plane] = turned.reshape(2, halves, cores, layout.share, length)
        for step, share in enumerate(shares):
            share[frame] = inner[:, :, :, (core + cores - step) % cores]


def post_kernel(layout, offsets, owner, *refs):
    shares, out = refs[:-1], refs[-1]
    upper, lower, twin, _ = layout.place()
    region = twin * layout.lowers + lower
    for low in range(layout.lowers):
        band = band_of_block(owner, upper * layout.lowers + low, layout)
        frame, row = jnp.int32(0), offsets[0, region * layout.frames]
        for extra in range(1, layout.frames):
            candidate = offsets[0, region * layout.frames + extra]
            anchor = candidate // layout.band
            over = (anchor <= band) & (band <= anchor + 2)
            frame, row = jnp.where(over, extra, frame), jnp.where(over, candidate, row)
        slot = (band - row // layout.band == 1).astype(jnp.int32)
        for target in range(layout.halves):
            for plane in range(2):
                total = shares[0][frame, plane, slot, target]
                for share in shares[1:]:
                    total += share[frame, plane, slot, target]
                out[target * layout.lowers + low, plane] = total


def update_kernel(layout, offsets, owner, arrived, block, *refs):
    powers, (rows_out, doubled, total) = refs[: layout.cores], refs[layout.cores :]
    upper, lower, twin, core = layout.place()
    length, share = layout.length, layout.share
    band = band_of_block(owner, upper * layout.lowers + lower, layout)
    first = (twin * layout.cores + core) * share
    rows = lax.broadcasted_iota(jnp.int32, (share, length), 0) + first
    power = powers[0][...]
    for more in powers[1:]:
        power += more[...]
    doubled[0] = power
    doubled[1] = power
    wide = doubled.reshape(2 * length, length)
    tiles = length // lanes
    column_in_tile = lax.broadcasted_iota(jnp.int32, (3 * share, lanes), 1)
    total[...] = jnp.zeros_like(total)
    for region in range(layout.regions):
        row, column = frame_over(offsets, region, band, layout)
        anchor = row // layout.band
        lead = row - anchor * layout.band
        step = band - anchor
        begin = jnp.where(step == 0, lead, jnp.where((step == 1) | (step == 2), 0, layout.band))
        end = jnp.where(step == 2, lead, layout.band)
        inside = (rows >= begin) & (rows < end)
        slot = (step == 1).astype(jnp.int32)
        start = (slot * layout.band + first + length - lead) % length
        near = wide[pl.ds(pl.multiple_of(start // 8 * 8, 8), share + 8), :]
        near = pltpu.roll(near, (share + 8 - start % 8) % (share + 8), 0)[:share]
        terms = jnp.concatenate([arrived[region, 0], arrived[region, 1], near], axis=0)
        terms = jnp.where(jnp.concatenate([inside] * 3, axis=0), terms, 0.0)
        shift = column % lanes
        begin = pl.multiple_of(column - shift, lanes)
        spilled = column_in_tile < shift
        turned = [
            pltpu.roll(terms[:, tile * lanes : (tile + 1) * lanes], shift, 1) for tile in range(tiles)
        ]
        for tile in range(tiles + 1):
            first_part = turned[tile] if tile < tiles else 0.0
            second_part = turned[tile - 1] if tile else 0.0
            total[:, pl.ds(begin + tile * lanes, lanes)] += jnp.where(spilled, second_part, first_part)
    damped = total[2 * share :, : layout.width] + object_damping
    for plane in range(2):
        old = block[plane, pl.ds(pl.multiple_of(first, share), share), :]
        rows_out[plane] = old + total[plane * share : (plane + 1) * share, : layout.width] / damped


def call(kernel, name, operands, outputs, scratch=(), scalar_count=0, after=()):
    shapes = [jax.ShapeDtypeStruct(shape, single) for shape in outputs]
    count = len(operands)

    def inner(*refs):
        kernel(*refs[:count], *refs[count + len(after) :])

    return pl.pallas_call(
        inner,
        name=name,
        out_shape=shapes,
        in_specs=[scalars] * scalar_count
        + [on_chip] * (count - scalar_count)
        + [pl.BlockSpec(memory_space=pl.ANY)] * len(after),
        out_specs=[on_chip] * len(shapes),
        scratch_shapes=[pltpu.VMEM(shape, single) for shape in scratch],
        compiler_params=pltpu.CompilerParams(vmem_limit_bytes=28 * 2**20),
    )(*operands, *after)


def body(measured, probe_modes, object_bands, scan_offsets, band_owner):
    layout = Layout(
        lax.axis_size("region"),
        lax.axis_size("mode"),
        measured.shape[1],
        measured.shape[0],
        probe_modes.shape[1] * lax.axis_size("mode"),
        object_bands.shape[2],
    )
    regions, halves, cores = layout.regions, layout.halves, layout.cores
    length, piece, frames = layout.length, layout.piece, layout.frames
    local, strip, share = layout.local_modes, layout.strip, layout.share
    forward, back = fourier_tables(length)
    corners = scan_offsets.T

    def from_cores(array):
        return [array] + [layout.from_core(array, step) for step in range(1, cores)]

    def from_uppers(array):
        return [array] + [layout.from_upper(array, step) for step in range(1, halves)]

    *cuts, part_measured = pl.pallas_call(
        functools.partial(cut_kernel, layout),
        name="cut",
        out_shape=[jax.ShapeDtypeStruct((2, strip, length), single)] * layout.lowers
        + [jax.ShapeDtypeStruct((frames, layout.part, length), single)],
        in_specs=[pl.BlockSpec(memory_space=pltpu.HBM)] * 4,
        out_specs=[on_chip] * (layout.lowers + 1),
        scratch_shapes=[
            pltpu.VMEM((2, strip, layout.width + lanes), single),
            pltpu.SMEM(corners.shape, jnp.int32),
            pltpu.SMEM(band_owner.shape, jnp.int32),
            pltpu.SemaphoreType.DMA((4,)),
        ],
        compiler_params=pltpu.CompilerParams(vmem_limit_bytes=60 * 2**20),
    )(corners, band_owner, object_bands, measured)
    probes = [probe_modes] + [layout.from_twin(probe_modes, step) for step in range(1, halves)]
    if halves > 1:
        pairs = [
            (layout.device(t, l, t, c), layout.device(u, l, t, c))
            for u, l, t, c in layout.everyone()
            if u != t
        ]
        part_measured = lax.ppermute(part_measured, axes, pairs)
    cuts = [cuts[0]] + [layout.to_row(cut, step) for step, cut in enumerate(cuts[1:], start=1)]
    chosen = []
    for steps in ((0,), tuple(range(1, layout.lowers))):
        chosen = call(
            functools.partial(choose_kernel, layout, steps),
            "choose",
            (corners, band_owner, *(cuts[step] for step in steps), *chosen),
            [(frames, 2, 2, strip, length)],
            scalar_count=2,
        )
    (chosen,) = chosen
    measured_parts = from_cores(part_measured)
    (roots,) = call(
        functools.partial(order_kernel, layout),
        "order",
        (measured, *measured_parts),
        [measured.shape],
        scratch=[(cores, layout.part, length)],
    )
    parts = from_uppers(chosen)
    held, roots, *received = lax.optimization_barrier((chosen, roots, *probes[1:]))
    probes = [probe_modes, *received]
    strips = list(parts)
    for step in range(1, cores):
        strips += [layout.from_core(part, step) for part in [held] + parts[1:]]
    windows, intensity, kept, old_pieces = call(
        functools.partial(far_kernel, layout),
        "far",
        (corners, *strips, *probes, forward, back),
        [
            (frames, 2, length, length),
            (frames, length, length),
            (frames, local, 2, length, length),
            (halves, local, 2, piece, length),
        ],
        scratch=[(2, 2, cores, strip, length)],
        scalar_count=1,
    )
    (pieces,) = call(
        functools.partial(gradient_kernel, layout),
        "gradient",
        (*from_cores(intensity), roots, windows, kept, forward, back),
        [(regions, 2 * local * piece + piece // halves, length)],
    )
    pieces = layout.within_cube(pieces)
    (total,) = call(sum_kernel, "sum", (pieces,), [pieces.shape[1:]])
    (spread,) = call(
        functools.partial(step_kernel, layout),
        "step",
        (old_pieces, *from_uppers(total)),
        [(regions, halves, local, 2, piece, length)],
    )
    new_probes = layout.within_cube(spread)
    probe_out, probe_power, intensity, fars = call(
        functools.partial(again_kernel, layout),
        "again",
        (new_probes, windows, forward, back),
        [
            (2, local, length, length),
            (length, length),
            (frames, length, length),
            (frames, halves, local, 2, length, length),
        ],
    )
    shares = call(
        functools.partial(terms_kernel, layout),
        "terms",
        (corners, *from_cores(intensity), roots, new_probes, fars, forward, back),
        [(frames, 2, 2, halves, share, length)] * cores,
        scratch=[(2, 2, halves, cores, share, length)],
        scalar_count=1,
    )
    shares = [shares[0]] + [
        layout.from_core(sent, step) for step, sent in enumerate(shares[1:], start=1)
    ]
    powers = from_cores(probe_power)
    (posted,) = call(
        functools.partial(post_kernel, layout),
        "post",
        (corners, band_owner, *shares),
        [(regions, 2, share, length)],
        scalar_count=2,
        after=powers,
    )
    posted = layout.within_cube(posted)
    (new_rows,) = call(
        functools.partial(update_kernel, layout),
        "update",
        (corners, band_owner, posted, object_bands, *powers),
        [(2, share, layout.width)],
        scratch=[(2, length, length), (3 * share, layout.width + lanes)],
        scalar_count=2,
    )
    object_out = lax.all_gather(new_rows, "mode", axis=1, tiled=True)
    return probe_out, object_out


def solution(mesh):
    in_specs = (
        P("region", None, None),
        P(None, "mode", None, None),
        P(None, "region", None),
        P(),
        P(),
    )
    out_specs = (P(None, "mode", None, None), P(None, "region", None))
    return jax.shard_map(body, mesh=mesh, in_specs=in_specs, out_specs=out_specs, check_vma=False)
```

```python
import functools
import math

import jax
import jax.numpy as jnp
import ml_dtypes
import numpy as np
from jax import lax
from jax.experimental import pallas as pl
from jax.experimental.pallas import tpu as pltpu
from jax.sharding import PartitionSpec as P

intensity_offset = 0.1
probe_damping = 1.0
object_damping = 1.0
half = jnp.bfloat16
single = jnp.float32
axes = ("region", "mode")
lanes = 128
on_chip = pl.BlockSpec(memory_space=pltpu.VMEM)
scalars = pl.BlockSpec(memory_space=pltpu.SMEM)


class Layout:
    def __init__(self, regions, helpers, length, frames, modes, width):
        self.regions, self.helpers = regions, helpers
        self.length, self.frames, self.modes, self.width = length, frames, modes, width
        self.halves = 2 if regions % 2 == 0 and helpers % 2 == 0 else 1
        self.lowers, self.cores = regions // self.halves, helpers // self.halves
        self.local_modes = modes // helpers
        self.band = length // 2
        self.strip = self.band // self.cores
        self.paired = self.lowers & (self.lowers - 1) == 0
        self.piece = length // regions
        self.part = length // self.cores

    def place(self):
        region, helper = lax.axis_index("region"), lax.axis_index("mode")
        upper, lower = region // self.lowers, region % self.lowers
        twin, core = helper // self.cores, helper % self.cores
        return upper, lower, twin, core

    def device(self, upper, lower, twin, core):
        return (upper * self.lowers + lower) * self.helpers + twin * self.cores + core

    def everyone(self):
        for upper in range(self.halves):
            for lower in range(self.lowers):
                for twin in range(self.halves):
                    for core in range(self.cores):
                        yield upper, lower, twin, core

    def cubes(self):
        return [
            [
                self.device(upper, lower, twin, core)
                for twin in range(self.halves)
                for lower in range(self.lowers)
            ]
            for upper in range(self.halves)
            for core in range(self.cores)
        ]

    def from_upper(self, array, step):
        pairs = [
            (self.device((u + step) % self.halves, l, t, c), self.device(u, l, t, c))
            for u, l, t, c in self.everyone()
        ]
        return lax.ppermute(array, axes, pairs)

    def from_core(self, array, step):
        pairs = [
            (self.device(u, l, t, (c + step) % self.cores), self.device(u, l, t, c))
            for u, l, t, c in self.everyone()
        ]
        return lax.ppermute(array, axes, pairs)

    def from_twin(self, array, step):
        pairs = [
            (self.device(u, l, (t + step) % self.halves, c), self.device(u, l, t, c))
            for u, l, t, c in self.everyone()
        ]
        return lax.ppermute(array, axes, pairs)

    def across(self, lower, step):
        if self.paired:
            return lower ^ step
        return (lower + step) % self.lowers

    def to_row(self, array, step):
        pairs = [
            (self.device(u, l, t, c), self.device(u, self.across(l, step), t, c))
            for u, l, t, c in self.everyone()
        ]
        return lax.ppermute(array, axes, pairs)

    def within_cube(self, array):
        return lax.all_to_all(
            array, axes, split_axis=0, concat_axis=0, tiled=True, axis_index_groups=self.cubes()
        )


def fourier_tables(length):
    near = np.arange(length // 2)
    forms = []
    for odd in range(2):
        angles = near[:, None] * (2 * near[None, :] + odd) % length * (2.0 * math.pi / length)
        cosine, sine = np.cos(angles) / math.sqrt(length), np.sin(angles) / math.sqrt(length)
        forms.append(np.block([[cosine, -sine], [sine, cosine]]))
    forward = np.stack(forms)

    def pair(table):
        lead = table.astype(ml_dtypes.bfloat16)
        return np.stack([lead, (table - lead.astype(np.float64)).astype(ml_dtypes.bfloat16)])

    return pair(forward), pair(forward.swapaxes(1, 2))


def split(values):
    lead = values.astype(half)
    return lead, (values - lead.astype(single)).astype(half)


def dot(left, right):
    return jnp.dot(left, right, preferred_element_type=single)


def from_left(table, values):
    lead, trail = split(values)
    return dot(table[0], lead) + dot(table[1], lead) + dot(table[0], trail)


def from_right(values, table):
    lead, trail = split(values)
    return dot(lead, table[0]) + dot(lead, table[1]) + dot(trail, table[0])


def beside(left, right):
    return jnp.concatenate([left, right], axis=1)


def above(top, bottom):
    return jnp.concatenate([top, bottom], axis=0)


def table_of(tables, number):
    return tables[0, number], tables[1, number]


def columns_forward(real, imag, forward):
    middle = real.shape[1] // 2
    real_left, real_right = real[:, :middle], real[:, middle:]
    imag_left, imag_right = imag[:, :middle], imag[:, middle:]
    even = from_right(beside(real_left + real_right, imag_left + imag_right), table_of(forward, 0))
    odd = from_right(beside(real_left - real_right, imag_left - imag_right), table_of(forward, 1))
    return (
        beside(even[:, :middle], odd[:, :middle]),
        beside(even[:, middle:], odd[:, middle:]),
    )


def columns_back(real, imag, back):
    middle = real.shape[1] // 2
    even = from_right(beside(real[:, :middle], imag[:, :middle]), table_of(back, 0))
    odd = from_right(beside(real[:, middle:], imag[:, middle:]), table_of(back, 1))
    plus, minus = even + odd, even - odd
    return (
        beside(plus[:, :middle], minus[:, :middle]),
        beside(plus[:, middle:], minus[:, middle:]),
    )


def rows_forward(real, imag, back):
    middle = real.shape[0] // 2
    real_top, real_bottom = real[:middle], real[middle:]
    imag_top, imag_bottom = imag[:middle], imag[middle:]
    even = from_left(table_of(back, 0), above(real_top + real_bottom, imag_top + imag_bottom))
    odd = from_left(table_of(back, 1), above(real_top - real_bottom, imag_top - imag_bottom))
    return above(even[:middle], odd[:middle]), above(even[middle:], odd[middle:])


def rows_back(real, imag, forward):
    middle = real.shape[0] // 2
    even = from_left(table_of(forward, 0), above(real[:middle], imag[:middle]))
    odd = from_left(table_of(forward, 1), above(real[middle:], imag[middle:]))
    plus, minus = even + odd, even - odd
    return above(plus[:middle], minus[:middle]), above(plus[middle:], minus[middle:])


def band_of_block(owner, block, layout):
    band = jnp.int32(0)
    for candidate in range(layout.regions):
        band = jnp.where(owner[candidate] == block, candidate, band)
    return band


def frame_over(offsets, region, band, layout):
    row, column = offsets[0, region * layout.frames], offsets[1, region * layout.frames]
    for extra in range(1, layout.frames):
        index = region * layout.frames + extra
        anchor = offsets[0, index] // layout.band
        over = (anchor <= band) & (band <= anchor + 2)
        row = jnp.where(over, offsets[0, index], row)
        column = jnp.where(over, offsets[1, index], column)
    return row, column


def cut_kernel(layout, corners, owners, block, measured, *refs):
    outs, (sent, taken, offsets, owner, done) = refs[: layout.lowers], refs[layout.lowers :]
    upper, lower, twin, core = layout.place()
    strip = pl.ds(pl.multiple_of(core * layout.strip, layout.strip), layout.strip)
    part = pl.ds(pl.multiple_of(core * layout.part, layout.part), layout.part)
    copies = [
        pltpu.make_async_copy(corners, offsets, done.at[0]),
        pltpu.make_async_copy(owners, owner, done.at[1]),
        pltpu.make_async_copy(block.at[:, strip, :], taken.at[:, :, : layout.width], done.at[2]),
        pltpu.make_async_copy(measured.at[:, part, :], sent, done.at[3]),
    ]
    for copy in copies:
        copy.start()
    for copy in copies[:3]:
        copy.wait()
    band = band_of_block(owner, upper * layout.lowers + lower, layout)
    tiles = layout.length // lanes
    column_in_tile = lax.broadcasted_iota(jnp.int32, (2 * layout.strip, lanes), 1)
    for step, out in enumerate(outs):
        region = twin * layout.lowers + layout.across(lower, step)
        _, column = frame_over(offsets, region, band, layout)
        shift = column % lanes
        begin = pl.multiple_of(column - shift, lanes)
        kept = column_in_tile < lanes - shift
        turned = []
        for tile in range(tiles + 1):
            values = taken[:, :, pl.ds(begin + tile * lanes, lanes)].reshape(2 * layout.strip, lanes)
            turned.append(pltpu.roll(values, (lanes - shift) % lanes, 1))
        for tile in range(tiles):
            values = jnp.where(kept, turned[tile], turned[tile + 1])
            out[:, :, tile * lanes : (tile + 1) * lanes] = values.reshape(2, layout.strip, lanes)
    copies[3].wait()


def choose_kernel(layout, steps, offsets, owner, *refs):
    arrived, (*before, out) = refs[: len(steps)], refs[len(steps) :]
    upper, lower, twin, core = layout.place()
    rows = lax.broadcasted_iota(jnp.int32, (layout.strip, layout.length), 0) + core * layout.strip
    for frame in range(layout.frames):
        row = offsets[0, (twin * layout.lowers + lower) * layout.frames + frame]
        anchor = row // layout.band
        lead = row - anchor * layout.band
        blocks = [owner[anchor + step] for step in range(3)]
        masks = [rows >= lead, rows >= 0, rows < lead]
        for plane in range(2):
            slots = [ref[frame, plane] for ref in before]
            top, bottom = (slots[0][0], slots[0][1]) if before else (0.0, 0.0)
            for block, mask, slot in zip(blocks, masks, (0, 1, 0)):
                here = block // layout.lowers == upper
                values = top if slot == 0 else bottom
                for step, ref in zip(steps, arrived):
                    came = here & (layout.across(block % layout.lowers, step) == lower)
                    values = jnp.where(mask & came, ref[plane], values)
                top, bottom = (values, bottom) if slot == 0 else (top, values)
            out[frame, plane, 0] = top
            out[frame, plane, 1] = bottom


def side_by_side(stack, rows):
    return jnp.concatenate([stack[at : at + rows] for at in range(0, stack.shape[0], rows)], axis=1)


def one_above_another(row, columns):
    return jnp.concatenate([row[:, at : at + columns] for at in range(0, row.shape[1], columns)], axis=0)


def leave(probes, window_real, window_imag, forward, back):
    length = window_real.shape[0]
    wave = rows_forward(
        jnp.concatenate([real * window_real - imag * window_imag for real, imag in probes], axis=1),
        jnp.concatenate([real * window_imag + imag * window_real for real, imag in probes], axis=1),
        back,
    )
    return columns_forward(*(one_above_another(part, length) for part in wave), forward)


def come_back(far, factor, forward, back):
    length = factor.shape[0]
    factors = jnp.concatenate([factor] * (far.shape[1] // length), axis=0)
    wave = columns_back(far[0] * factors, far[1] * factors, back)
    return rows_back(*(side_by_side(part, length) for part in wave), forward)


def power_of(real, imag, length):
    power = real**2 + imag**2
    return sum(power[at : at + length] for at in range(length, power.shape[0], length)) + power[:length]


def far_kernel(layout, offsets, *refs):
    cores, halves, frames, length = layout.cores, layout.halves, layout.frames, layout.length
    shares, probes = refs[: cores * halves], refs[cores * halves : (cores + 1) * halves]
    forward, back, windows, intensity, kept, old_pieces, inner = refs[(cores + 1) * halves :]
    upper, lower, twin, core = layout.place()
    region = twin * layout.lowers + lower
    rows = pl.ds(pl.multiple_of(region * layout.piece, layout.piece), layout.piece)
    for entry, probe in enumerate(probes):
        place = (twin + entry + halves - upper) % halves
        for local in range(layout.local_modes):
            for plane in range(2):
                old_pieces[place, local, plane] = probe[plane, local, rows, :]
    for frame in range(frames):
        lead = offsets[0, region * frames + frame] % layout.band
        for step in range(cores):
            strip = shares[step * halves][frame]
            for entry in range(1, halves):
                strip += shares[step * halves + entry][frame]
            inner[:, :, (core + step) % cores] = strip
        for plane in range(2):
            wrapped = inner[plane].reshape(length, length)
            windows[frame, plane] = pltpu.roll(wrapped, (length - lead) % length, 0)
        listed = [(probe[0, k], probe[1, k]) for probe in probes for k in range(layout.local_modes)]
        waves = leave(listed, windows[frame, 0], windows[frame, 1], forward, back)
        intensity[frame] = power_of(*waves, length)
        rows_kept = layout.local_modes * length
        for entry in range(halves):

            @pl.when((twin + entry) % halves == upper)
            def _():
                for plane, wave in enumerate(waves):
                    kept[frame, plane] = wave[entry * rows_kept : (entry + 1) * rows_kept]


def order_kernel(layout, own_measured, *refs):
    parts, (out, other_measured) = refs[: layout.cores], refs[layout.cores :]
    upper, _, twin, core = layout.place()
    length = layout.length
    rows = lax.broadcasted_iota(jnp.int32, (length, length), 0)
    columns = lax.broadcasted_iota(jnp.int32, (length, length), 1)
    middle = length // 2
    pick_rows = (columns == jnp.where(rows < middle, 2 * rows, 2 * (rows - middle) + 1)).astype(half)
    pick_columns = (rows == jnp.where(columns < middle, 2 * columns, 2 * (columns - middle) + 1)).astype(half)

    def exact(product, values):
        lead, rest = split(values)
        trail = (values - lead.astype(single) - rest.astype(single)).astype(half)
        return (product(lead) + product(rest)) + product(trail)

    for frame in range(layout.frames):
        for step, part in enumerate(parts):
            other_measured[(core + step) % layout.cores] = part[frame]
        measured = other_measured[...].reshape(length, length)
        measured = jnp.sqrt(jnp.where(upper == twin, own_measured[frame], measured))
        measured = exact(lambda values: dot(pick_rows, values), measured)
        out[frame] = exact(lambda values: dot(values, pick_columns), measured)


def factor_of(root, intensities, frame):
    total = intensities[0][frame]
    for more in intensities[1:]:
        total += more[frame]
    return root[frame] / jnp.sqrt(total + intensity_offset) - 1.0


def gradient_kernel(layout, *refs):
    cores, frames, length, piece = layout.cores, layout.frames, layout.length, layout.piece
    intensities, (roots, windows, kept, forward, back, pieces) = refs[:cores], refs[cores:]
    upper, _, _, _ = layout.place()
    cut = (layout.regions, piece, length)
    part = piece // layout.halves
    for frame in range(frames):
        window_real, window_imag = windows[frame, 0], windows[frame, 1]
        factor = factor_of(roots, intensities, frame)
        channels = []
        changes_real, changes_imag = come_back(kept[frame], factor, forward, back)
        for local in range(layout.local_modes):
            columns = slice(local * length, (local + 1) * length)
            change_real, change_imag = changes_real[:, columns], changes_imag[:, columns]
            channels.append(window_real * change_real + window_imag * change_imag)
            channels.append(window_real * change_imag - window_imag * change_real)
        channels = [values.reshape(cut) for values in channels]
        power = (window_real**2 + window_imag**2).reshape(cut)
        sent = power[:, :part]
        for other in range(1, layout.halves):
            sent = jnp.where(upper == other, power[:, other * part : (other + 1) * part], sent)
        first = 0
        for values in (*channels, sent):
            rows = slice(first, first + values.shape[1])
            if frame == 0:
                pieces[:, rows] = values
            else:
                pieces[:, rows] += values
            first += values.shape[1]


def sum_kernel(arrived, total):
    total[...] = jnp.sum(arrived[...], axis=0)


def step_kernel(layout, old_pieces, *refs):
    totals, out = refs[:-1], refs[-1]
    upper, _, _, _ = layout.place()
    halves, piece = layout.halves, layout.piece
    planes = 2 * layout.local_modes
    parts = []
    for place in range(halves):
        power = totals[0][planes * piece :]
        for entry in range(1, halves):
            power = jnp.where((upper + entry) % halves == place, totals[entry][planes * piece :], power)
        parts.append(power)
    damped = jnp.concatenate(parts, axis=0) + probe_damping
    for entry, total in enumerate(totals):
        for local in range(layout.local_modes):
            for plane in range(2):
                first = (2 * local + plane) * piece
                stepped = old_pieces[entry, local, plane] + total[first : first + piece] / damped
                for region in range(layout.regions):
                    out[region, entry, local, plane] = stepped


def new_probe(probes, entry, local, plane):
    values = probes[:, entry, local, plane]
    return values.reshape(values.shape[0] * values.shape[1], values.shape[2])


def again_kernel(layout, probes, windows, forward, back, probe_out, probe_power, intensity, fars):
    upper, _, twin, _ = layout.place()
    own_entry = (twin + layout.halves - upper) % layout.halves
    listed = [
        [new_probe(probes, entry, local, plane) for plane in range(2)]
        for entry in range(layout.halves)
        for local in range(layout.local_modes)
    ]
    for frame in range(layout.frames):
        waves = leave(listed, windows[frame, 0], windows[frame, 1], forward, back)
        intensity[frame] = power_of(*waves, layout.length)
        for plane, wave in enumerate(waves):
            fars[frame, plane] = wave
    probe_power[...] = sum(real**2 + imag**2 for real, imag in listed)
    for local in range(layout.local_modes):
        for plane in range(2):
            probe_out[plane, local] = new_probe(probes, own_entry, local, plane)


def terms_kernel(layout, offsets, *refs):
    cores, halves, frames, length = layout.cores, layout.halves, layout.frames, layout.length
    intensities = refs[:cores]
    roots, probes, fars, forward, back, *strips, inner = refs[cores:]
    upper, lower, twin, core = layout.place()
    region = twin * layout.lowers + lower
    for frame in range(frames):
        factor = factor_of(roots, intensities, frame)
        changes_real, changes_imag = come_back(fars[frame], factor, forward, back)
        numer_real = jnp.zeros((length, length), single)
        numer_imag = jnp.zeros((length, length), single)
        for entry in range(halves):
            for local in range(layout.local_modes):
                first = (entry * layout.local_modes + local) * length
                change_real = changes_real[:, first : first + length]
                change_imag = changes_imag[:, first : first + length]
                probe_real, probe_imag = (new_probe(probes, entry, local, plane) for plane in range(2))
                numer_real += probe_real * change_real + probe_imag * change_imag
                numer_imag += probe_real * change_imag - probe_imag * change_real
        lead = offsets[0, region * frames + frame] % layout.band
        for plane, values in enumerate((numer_real, numer_imag)):
            inner[plane] = pltpu.roll(values, lead, 0).reshape(2, cores, layout.strip, length)
        for step, strip in enumerate(strips):
            strip[frame] = inner[:, :, (core + cores - step) % cores]


def post_kernel(layout, offsets, owner, *refs):
    strips, outs = refs[: layout.cores], refs[layout.cores :]
    upper, lower, twin, _ = layout.place()
    region = twin * layout.lowers + lower
    for step, out in enumerate(outs):
        block = upper * layout.lowers + layout.across(lower, step)
        band = band_of_block(owner, block, layout)
        frame, row = jnp.int32(0), offsets[0, region * layout.frames]
        for extra in range(1, layout.frames):
            candidate = offsets[0, region * layout.frames + extra]
            anchor = candidate // layout.band
            over = (anchor <= band) & (band <= anchor + 2)
            frame, row = jnp.where(over, extra, frame), jnp.where(over, candidate, row)
        slot = (band - row // layout.band == 1).astype(jnp.int32)
        for plane in range(2):
            total = strips[0][frame, plane, slot]
            for strip in strips[1:]:
                total += strip[frame, plane, slot]
            out[plane] = total


class Cover:
    def __init__(self, layout, offsets, region, band, core):
        row, self.column = frame_over(offsets, region, band, layout)
        anchor = row // layout.band
        self.lead = row - anchor * layout.band
        self.step = band - anchor
        self.first = core * layout.strip
        self.layout = layout

    def inside(self):
        band = self.layout.band
        middle = (self.step == 1) | (self.step == 2)
        begin = jnp.where(self.step == 0, self.lead, jnp.where(middle, 0, band))
        end = jnp.where(self.step == 2, self.lead, band)
        shape = (self.layout.strip, self.layout.length)
        rows = lax.broadcasted_iota(jnp.int32, shape, 0) + self.first
        return (rows >= begin) & (rows < end)

    def start(self):
        slot = (self.step == 1).astype(jnp.int32)
        length = self.layout.length
        return (slot * self.layout.band + self.first + length - self.lead) % length

    def add(self, total, terms):
        tiles = self.layout.length // lanes
        shift = self.column % lanes
        begin = pl.multiple_of(self.column - shift, lanes)
        spilled = lax.broadcasted_iota(jnp.int32, (terms.shape[0], lanes), 1) < shift
        turned = [
            pltpu.roll(terms[:, tile * lanes : (tile + 1) * lanes], shift, 1) for tile in range(tiles)
        ]
        for tile in range(tiles + 1):
            near = turned[tile] if tile < tiles else 0.0
            over = turned[tile - 1] if tile else 0.0
            total[:, pl.ds(begin + tile * lanes, lanes)] += jnp.where(spilled, over, near)


def density_kernel(layout, offsets, owner, *refs):
    powers, (out, doubled, total) = refs[: layout.cores], refs[layout.cores :]
    upper, lower, _, core = layout.place()
    strip, length = layout.strip, layout.length
    band = band_of_block(owner, upper * layout.lowers + lower, layout)
    power = powers[0][...]
    for more in powers[1:]:
        power += more[...]
    doubled[0] = power
    doubled[1] = power
    wide = doubled.reshape(2 * length, length)
    total[...] = jnp.zeros_like(total)
    for region in range(layout.regions):
        cover = Cover(layout, offsets, region, band, core)
        start = cover.start()
        near = wide[pl.ds(pl.multiple_of(start // 8 * 8, 8), strip + 8), :]
        near = pltpu.roll(near, (strip + 8 - start % 8) % (strip + 8), 0)[:strip]
        cover.add(total, jnp.where(cover.inside(), near, 0.0))
    out[...] = total[:, : layout.width] + object_damping


def place_kernel(layout, offsets, owner, *refs):
    arrived, (out, total) = refs[: layout.lowers], refs[layout.lowers :]
    upper, lower, twin, core = layout.place()
    strip = layout.strip
    band = band_of_block(owner, upper * layout.lowers + lower, layout)
    total[...] = jnp.zeros_like(total)
    for step, terms in enumerate(arrived):
        source = layout.across(lower, step if layout.paired else layout.lowers - step)
        cover = Cover(layout, offsets, twin * layout.lowers + source, band, core)
        inside = cover.inside()
        kept = [jnp.where(inside, terms[plane], 0.0) for plane in range(2)]
        cover.add(total, jnp.concatenate(kept, axis=0))
    for plane in range(2):
        out[plane] = total[plane * strip : (plane + 1) * strip, : layout.width]


def update_kernel(layout, density, block, *refs):
    placed, out = refs[:-1], refs[-1]
    _, _, _, core = layout.place()
    rows = pl.ds(pl.multiple_of(core * layout.strip, layout.strip), layout.strip)
    for plane in range(2):
        total = placed[0][plane]
        for more in placed[1:]:
            total += more[plane]
        out[plane] = block[plane, rows, :] + total / density[...]


def join_kernel(layout, *refs):
    strips, out = refs[:-1], refs[-1]
    _, _, _, core = layout.place()
    for step, strip in enumerate(strips):
        first = (core + step) % layout.cores * layout.strip
        out[:, pl.ds(pl.multiple_of(first, layout.strip), layout.strip), :] = strip[...]


def call(kernel, name, operands, outputs, scratch=(), scalar_count=0, after=()):
    shapes = [jax.ShapeDtypeStruct(shape, single) for shape in outputs]
    count = len(operands)

    def inner(*refs):
        kernel(*refs[:count], *refs[count + len(after) :])

    return pl.pallas_call(
        inner,
        name=name,
        out_shape=shapes,
        in_specs=[scalars] * scalar_count
        + [on_chip] * (count - scalar_count)
        + [pl.BlockSpec(memory_space=pl.ANY)] * len(after),
        out_specs=[on_chip] * len(shapes),
        scratch_shapes=[pltpu.VMEM(shape, single) for shape in scratch],
        compiler_params=pltpu.CompilerParams(vmem_limit_bytes=28 * 2**20),
    )(*operands, *after)


def body(measured, probe_modes, object_bands, scan_offsets, band_owner):
    layout = Layout(
        lax.axis_size("region"),
        lax.axis_size("mode"),
        measured.shape[1],
        measured.shape[0],
        probe_modes.shape[1] * lax.axis_size("mode"),
        object_bands.shape[2],
    )
    regions, halves, cores = layout.regions, layout.halves, layout.cores
    length, piece, frames = layout.length, layout.piece, layout.frames
    local, strip = layout.local_modes, layout.strip
    forward, back = fourier_tables(length)
    corners = scan_offsets.T

    def from_cores(array):
        return [array] + [layout.from_core(array, step) for step in range(1, cores)]

    def from_uppers(array):
        return [array] + [layout.from_upper(array, step) for step in range(1, halves)]

    *cuts, part_measured = pl.pallas_call(
        functools.partial(cut_kernel, layout),
        name="cut",
        out_shape=[jax.ShapeDtypeStruct((2, strip, length), single)] * layout.lowers
        + [jax.ShapeDtypeStruct((frames, layout.part, length), single)],
        in_specs=[pl.BlockSpec(memory_space=pltpu.HBM)] * 4,
        out_specs=[on_chip] * (layout.lowers + 1),
        scratch_shapes=[
            pltpu.VMEM((2, strip, layout.width + lanes), single),
            pltpu.SMEM(corners.shape, jnp.int32),
            pltpu.SMEM(band_owner.shape, jnp.int32),
            pltpu.SemaphoreType.DMA((4,)),
        ],
        compiler_params=pltpu.CompilerParams(vmem_limit_bytes=28 * 2**20),
    )(
        *(
            pltpu.with_memory_space_constraint(array, pltpu.HBM)
            for array in (corners, band_owner, object_bands, measured)
        )
    )
    probes = [probe_modes] + [layout.from_twin(probe_modes, step) for step in range(1, halves)]
    if halves > 1:
        pairs = [
            (layout.device(t, l, t, c), layout.device(u, l, t, c))
            for u, l, t, c in layout.everyone()
            if u != t
        ]
        part_measured = lax.ppermute(part_measured, axes, pairs)
    cuts = [cuts[0]] + [layout.to_row(cut, step) for step, cut in enumerate(cuts[1:], start=1)]
    chosen = []
    for steps in ((0,), tuple(range(1, layout.lowers))):
        chosen = call(
            functools.partial(choose_kernel, layout, steps),
            "choose",
            (corners, band_owner, *(cuts[step] for step in steps), *chosen),
            [(frames, 2, 2, strip, length)],
            scalar_count=2,
        )
    (chosen,) = chosen
    measured_parts = from_cores(part_measured)
    (roots,) = call(
        functools.partial(order_kernel, layout),
        "order",
        (measured, *measured_parts),
        [measured.shape],
        scratch=[(cores, layout.part, length)],
    )
    parts = from_uppers(chosen)
    held, roots, *received = lax.optimization_barrier((chosen, roots, *probes[1:]))
    probes = [probe_modes, *received]
    strips = list(parts)
    for step in range(1, cores):
        strips += [layout.from_core(part, step) for part in [held] + parts[1:]]
    windows, intensity, kept, old_pieces = call(
        functools.partial(far_kernel, layout),
        "far",
        (corners, *strips, *probes, forward, back),
        [
            (frames, 2, length, length),
            (frames, length, length),
            (frames, 2, local * length, length),
            (halves, local, 2, piece, length),
        ],
        scratch=[(2, 2, cores, strip, length)],
        scalar_count=1,
    )
    (pieces,) = call(
        functools.partial(gradient_kernel, layout),
        "gradient",
        (*from_cores(intensity), roots, windows, kept, forward, back),
        [(regions, 2 * local * piece + piece // halves, length)],
    )
    pieces = layout.within_cube(pieces)
    (total,) = call(sum_kernel, "sum", (pieces,), [pieces.shape[1:]])
    (spread,) = call(
        functools.partial(step_kernel, layout),
        "step",
        (old_pieces, *from_uppers(total)),
        [(regions, halves, local, 2, piece, length)],
    )
    new_probes = layout.within_cube(spread)
    probe_out, probe_power, intensity, fars = call(
        functools.partial(again_kernel, layout),
        "again",
        (new_probes, windows, forward, back),
        [
            (2, local, length, length),
            (length, length),
            (frames, length, length),
            (frames, 2, halves * local * length, length),
        ],
    )
    strips = call(
        functools.partial(terms_kernel, layout),
        "terms",
        (corners, *from_cores(intensity), roots, new_probes, fars, forward, back),
        [(frames, 2, 2, strip, length)] * cores,
        scratch=[(2, 2, cores, strip, length)],
        scalar_count=1,
    )
    strips = [strips[0]] + [
        layout.from_core(sent, step) for step, sent in enumerate(strips[1:], start=1)
    ]
    posted = call(
        functools.partial(post_kernel, layout),
        "post",
        (corners, band_owner, *strips),
        [(2, strip, length)] * layout.lowers,
        scalar_count=2,
    )
    posted = [posted[0]] + [
        layout.to_row(sent, step) for step, sent in enumerate(posted[1:], start=1)
    ]
    (density,) = call(
        functools.partial(density_kernel, layout),
        "density",
        (corners, band_owner, *from_cores(probe_power)),
        [(strip, layout.width)],
        scratch=[(2, length, length), (strip, layout.width + lanes)],
        scalar_count=2,
    )
    (placed,) = call(
        functools.partial(place_kernel, layout),
        "place",
        (corners, band_owner, *posted),
        [(2, strip, layout.width)],
        scratch=[(2 * strip, layout.width + lanes)],
        scalar_count=2,
    )
    placed = [placed] + [layout.from_twin(placed, step) for step in range(1, halves)]
    (new_rows,) = call(
        functools.partial(update_kernel, layout),
        "update",
        (density, object_bands, *placed),
        [(2, strip, layout.width)],
    )
    (object_out,) = call(
        functools.partial(join_kernel, layout), "join", from_cores(new_rows), [object_bands.shape]
    )
    return probe_out, object_out


def solution(mesh):
    in_specs = (
        P("region", None, None),
        P(None, "mode", None, None),
        P(None, "region", None),
        P(),
        P(),
    )
    out_specs = (P(None, "mode", None, None), P(None, "region", None))
    return jax.shard_map(body, mesh=mesh, in_specs=in_specs, out_specs=out_specs, check_vma=False)
```

```python
import functools
import math

import jax
import jax.numpy as jnp
import ml_dtypes
import numpy as np
from jax import lax
from jax.experimental import pallas as pl
from jax.experimental.pallas import tpu as pltpu
from jax.sharding import PartitionSpec as P

intensity_offset = 0.1
probe_damping = 1.0
object_damping = 1.0
half = jnp.bfloat16
single = jnp.float32
axes = ("region", "mode")
lanes = 128
on_chip = pl.BlockSpec(memory_space=pltpu.VMEM)
scalars = pl.BlockSpec(memory_space=pltpu.SMEM)


class Layout:
    def __init__(self, regions, helpers, length, frames, modes, width):
        self.regions, self.helpers = regions, helpers
        self.length, self.frames, self.modes, self.width = length, frames, modes, width
        self.halves = 2 if regions % 2 == 0 and helpers % 2 == 0 else 1
        self.lowers, self.cores = regions // self.halves, helpers // self.halves
        self.local_modes = modes // helpers
        self.band = length // 2
        self.strip = self.band // self.cores
        self.paired = self.lowers & (self.lowers - 1) == 0
        self.piece = length // regions
        self.part = length // self.cores

    def place(self):
        region, helper = lax.axis_index("region"), lax.axis_index("mode")
        upper, lower = region // self.lowers, region % self.lowers
        twin, core = helper // self.cores, helper % self.cores
        return upper, lower, twin, core

    def device(self, upper, lower, twin, core):
        return (upper * self.lowers + lower) * self.helpers + twin * self.cores + core

    def everyone(self):
        for upper in range(self.halves):
            for lower in range(self.lowers):
                for twin in range(self.halves):
                    for core in range(self.cores):
                        yield upper, lower, twin, core

    def cubes(self):
        return [
            [
                self.device(upper, lower, twin, core)
                for twin in range(self.halves)
                for lower in range(self.lowers)
            ]
            for upper in range(self.halves)
            for core in range(self.cores)
        ]

    def from_upper(self, array, step):
        pairs = [
            (self.device((u + step) % self.halves, l, t, c), self.device(u, l, t, c))
            for u, l, t, c in self.everyone()
        ]
        return lax.ppermute(array, axes, pairs)

    def from_core(self, array, step):
        pairs = [
            (self.device(u, l, t, (c + step) % self.cores), self.device(u, l, t, c))
            for u, l, t, c in self.everyone()
        ]
        return lax.ppermute(array, axes, pairs)

    def from_twin(self, array, step):
        pairs = [
            (self.device(u, l, (t + step) % self.halves, c), self.device(u, l, t, c))
            for u, l, t, c in self.everyone()
        ]
        return lax.ppermute(array, axes, pairs)

    def across(self, lower, step):
        if self.paired:
            return lower ^ step
        return (lower + step) % self.lowers

    def to_row(self, array, step):
        pairs = [
            (self.device(u, l, t, c), self.device(u, self.across(l, step), t, c))
            for u, l, t, c in self.everyone()
        ]
        return lax.ppermute(array, axes, pairs)

    def within_cube(self, array):
        return lax.all_to_all(
            array, axes, split_axis=0, concat_axis=0, tiled=True, axis_index_groups=self.cubes()
        )


def fourier_tables(length):
    near = np.arange(length // 2)
    forms = []
    for odd in range(2):
        angles = near[:, None] * (2 * near[None, :] + odd) % length * (2.0 * math.pi / length)
        cosine, sine = np.cos(angles) / math.sqrt(length), np.sin(angles) / math.sqrt(length)
        forms.append(np.block([[cosine, -sine], [sine, cosine]]))
    forward = np.stack(forms)

    def pair(table):
        lead = table.astype(ml_dtypes.bfloat16)
        return np.stack([lead, (table - lead.astype(np.float64)).astype(ml_dtypes.bfloat16)])

    return pair(forward), pair(forward.swapaxes(1, 2))


def split(values):
    lead = values.astype(half)
    return lead, (values - lead.astype(single)).astype(half)


def dot(left, right):
    return jnp.dot(left, right, preferred_element_type=single)


def from_left(table, values):
    lead, trail = split(values)
    return dot(table[0], lead) + dot(table[1], lead) + dot(table[0], trail)


def from_right(values, table):
    lead, trail = split(values)
    return dot(lead, table[0]) + dot(lead, table[1]) + dot(trail, table[0])


def beside(left, right):
    return jnp.concatenate([left, right], axis=1)


def above(top, bottom):
    return jnp.concatenate([top, bottom], axis=0)


def table_of(tables, number):
    return tables[0, number], tables[1, number]


def columns_forward(real, imag, forward):
    middle = real.shape[1] // 2
    real_left, real_right = real[:, :middle], real[:, middle:]
    imag_left, imag_right = imag[:, :middle], imag[:, middle:]
    even = from_right(beside(real_left + real_right, imag_left + imag_right), table_of(forward, 0))
    odd = from_right(beside(real_left - real_right, imag_left - imag_right), table_of(forward, 1))
    return (
        beside(even[:, :middle], odd[:, :middle]),
        beside(even[:, middle:], odd[:, middle:]),
    )


def columns_back(real, imag, back):
    middle = real.shape[1] // 2
    even = from_right(beside(real[:, :middle], imag[:, :middle]), table_of(back, 0))
    odd = from_right(beside(real[:, middle:], imag[:, middle:]), table_of(back, 1))
    plus, minus = even + odd, even - odd
    return (
        beside(plus[:, :middle], minus[:, :middle]),
        beside(plus[:, middle:], minus[:, middle:]),
    )


def rows_forward(real, imag, back):
    middle = real.shape[0] // 2
    real_top, real_bottom = real[:middle], real[middle:]
    imag_top, imag_bottom = imag[:middle], imag[middle:]
    even = from_left(table_of(back, 0), above(real_top + real_bottom, imag_top + imag_bottom))
    odd = from_left(table_of(back, 1), above(real_top - real_bottom, imag_top - imag_bottom))
    return above(even[:middle], odd[:middle]), above(even[middle:], odd[middle:])


def rows_back(real, imag, forward):
    middle = real.shape[0] // 2
    even = from_left(table_of(forward, 0), above(real[:middle], imag[:middle]))
    odd = from_left(table_of(forward, 1), above(real[middle:], imag[middle:]))
    plus, minus = even + odd, even - odd
    return above(plus[:middle], minus[:middle]), above(plus[middle:], minus[middle:])


def band_of_block(owner, block, layout):
    band = jnp.int32(0)
    for candidate in range(layout.regions):
        band = jnp.where(owner[candidate] == block, candidate, band)
    return band


def frame_over(offsets, region, band, layout):
    row, column = offsets[0, region * layout.frames], offsets[1, region * layout.frames]
    for extra in range(1, layout.frames):
        index = region * layout.frames + extra
        anchor = offsets[0, index] // layout.band
        over = (anchor <= band) & (band <= anchor + 2)
        row = jnp.where(over, offsets[0, index], row)
        column = jnp.where(over, offsets[1, index], column)
    return row, column


def cut_kernel(layout, corners, owners, block, measured, *refs):
    outs, (sent, taken, offsets, owner, done) = refs[: layout.lowers], refs[layout.lowers :]
    upper, lower, twin, core = layout.place()
    strip = pl.ds(pl.multiple_of(core * layout.strip, layout.strip), layout.strip)
    part = pl.ds(pl.multiple_of(core * layout.part, layout.part), layout.part)
    copies = [
        pltpu.make_async_copy(corners, offsets, done.at[0]),
        pltpu.make_async_copy(owners, owner, done.at[1]),
        pltpu.make_async_copy(block.at[:, strip, :], taken.at[:, :, : layout.width], done.at[2]),
        pltpu.make_async_copy(measured.at[:, part, :], sent, done.at[3]),
    ]
    for copy in copies:
        copy.start()
    for copy in copies[:3]:
        copy.wait()
    band = band_of_block(owner, upper * layout.lowers + lower, layout)
    tiles = layout.length // lanes
    column_in_tile = lax.broadcasted_iota(jnp.int32, (2 * layout.strip, lanes), 1)
    for step, out in enumerate(outs):
        region = twin * layout.lowers + layout.across(lower, step)
        _, column = frame_over(offsets, region, band, layout)
        shift = column % lanes
        begin = pl.multiple_of(column - shift, lanes)
        kept = column_in_tile < lanes - shift
        turned = []
        for tile in range(tiles + 1):
            values = taken[:, :, pl.ds(begin + tile * lanes, lanes)].reshape(2 * layout.strip, lanes)
            turned.append(pltpu.roll(values, (lanes - shift) % lanes, 1))
        for tile in range(tiles):
            values = jnp.where(kept, turned[tile], turned[tile + 1])
            out[:, :, tile * lanes : (tile + 1) * lanes] = values.reshape(2, layout.strip, lanes)
    copies[3].wait()


def choose_kernel(layout, steps, offsets, owner, *refs):
    arrived, (*before, out) = refs[: len(steps)], refs[len(steps) :]
    upper, lower, twin, core = layout.place()
    rows = lax.broadcasted_iota(jnp.int32, (layout.strip, layout.length), 0) + core * layout.strip
    for frame in range(layout.frames):
        row = offsets[0, (twin * layout.lowers + lower) * layout.frames + frame]
        anchor = row // layout.band
        lead = row - anchor * layout.band
        blocks = [owner[anchor + step] for step in range(3)]
        masks = [rows >= lead, rows >= 0, rows < lead]
        for plane in range(2):
            slots = [ref[frame, plane] for ref in before]
            top, bottom = (slots[0][0], slots[0][1]) if before else (0.0, 0.0)
            for block, mask, slot in zip(blocks, masks, (0, 1, 0)):
                here = block // layout.lowers == upper
                values = top if slot == 0 else bottom
                for step, ref in zip(steps, arrived):
                    came = here & (layout.across(block % layout.lowers, step) == lower)
                    values = jnp.where(mask & came, ref[plane], values)
                top, bottom = (values, bottom) if slot == 0 else (top, values)
            out[frame, plane, 0] = top
            out[frame, plane, 1] = bottom


def side_by_side(stack, rows):
    return jnp.concatenate([stack[at : at + rows] for at in range(0, stack.shape[0], rows)], axis=1)


def one_above_another(row, columns):
    return jnp.concatenate([row[:, at : at + columns] for at in range(0, row.shape[1], columns)], axis=0)


def leave(probes, window_real, window_imag, forward, back):
    length = window_real.shape[0]
    wave = rows_forward(
        jnp.concatenate([real * window_real - imag * window_imag for real, imag in probes], axis=1),
        jnp.concatenate([real * window_imag + imag * window_real for real, imag in probes], axis=1),
        back,
    )
    return columns_forward(*(one_above_another(part, length) for part in wave), forward)


def come_back(far, factor, forward, back):
    length = factor.shape[0]
    factors = jnp.concatenate([factor] * (far.shape[1] // length), axis=0)
    wave = columns_back(far[0] * factors, far[1] * factors, back)
    return rows_back(*(side_by_side(part, length) for part in wave), forward)


def power_of(real, imag, length):
    power = real**2 + imag**2
    return sum(power[at : at + length] for at in range(length, power.shape[0], length)) + power[:length]


def far_kernel(layout, offsets, *refs):
    cores, halves, frames, length = layout.cores, layout.halves, layout.frames, layout.length
    shares, probes = refs[: cores * halves], refs[cores * halves : (cores + 1) * halves]
    forward, back, windows, intensity, kept, old_pieces, inner = refs[(cores + 1) * halves :]
    upper, lower, twin, core = layout.place()
    region = twin * layout.lowers + lower
    rows = pl.ds(pl.multiple_of(region * layout.piece, layout.piece), layout.piece)
    for entry, probe in enumerate(probes):
        place = (twin + entry + halves - upper) % halves
        for local in range(layout.local_modes):
            for plane in range(2):
                old_pieces[place, local, plane] = probe[plane, local, rows, :]
    for frame in range(frames):
        lead = offsets[0, region * frames + frame] % layout.band
        for step in range(cores):
            strip = shares[step * halves][frame]
            for entry in range(1, halves):
                strip += shares[step * halves + entry][frame]
            inner[:, :, (core + step) % cores] = strip
        for plane in range(2):
            wrapped = inner[plane].reshape(length, length)
            windows[frame, plane] = pltpu.roll(wrapped, (length - lead) % length, 0)
        listed = [(probe[0, k], probe[1, k]) for probe in probes for k in range(layout.local_modes)]
        waves = leave(listed, windows[frame, 0], windows[frame, 1], forward, back)
        intensity[frame] = power_of(*waves, length)
        rows_kept = layout.local_modes * length
        for entry in range(halves):

            @pl.when((twin + entry) % halves == upper)
            def _():
                for plane, wave in enumerate(waves):
                    kept[frame, plane] = wave[entry * rows_kept : (entry + 1) * rows_kept]


def order_kernel(layout, own_measured, *refs):
    parts, (out, other_measured) = refs[: layout.cores], refs[layout.cores :]
    upper, _, twin, core = layout.place()
    length = layout.length
    rows = lax.broadcasted_iota(jnp.int32, (length, length), 0)
    columns = lax.broadcasted_iota(jnp.int32, (length, length), 1)
    middle = length // 2
    pick_rows = (columns == jnp.where(rows < middle, 2 * rows, 2 * (rows - middle) + 1)).astype(half)
    pick_columns = (rows == jnp.where(columns < middle, 2 * columns, 2 * (columns - middle) + 1)).astype(half)

    def exact(product, values):
        lead, rest = split(values)
        trail = (values - lead.astype(single) - rest.astype(single)).astype(half)
        return (product(lead) + product(rest)) + product(trail)

    for frame in range(layout.frames):
        for step, part in enumerate(parts):
            other_measured[(core + step) % layout.cores] = part[frame]
        measured = other_measured[...].reshape(length, length)
        measured = jnp.sqrt(jnp.where(upper == twin, own_measured[frame], measured))
        measured = exact(lambda values: dot(pick_rows, values), measured)
        out[frame] = exact(lambda values: dot(values, pick_columns), measured)


def factor_of(root, intensities, frame):
    total = intensities[0][frame]
    for more in intensities[1:]:
        total += more[frame]
    return root[frame] / jnp.sqrt(total + intensity_offset) - 1.0


def gradient_kernel(layout, *refs):
    cores, frames, length, piece = layout.cores, layout.frames, layout.length, layout.piece
    intensities, (roots, windows, kept, forward, back, pieces) = refs[:cores], refs[cores:]
    upper, _, _, _ = layout.place()
    cut = (layout.regions, piece, length)
    part = piece // layout.halves
    for frame in range(frames):
        window_real, window_imag = windows[frame, 0], windows[frame, 1]
        factor = factor_of(roots, intensities, frame)
        channels = []
        changes_real, changes_imag = come_back(kept[frame], factor, forward, back)
        for local in range(layout.local_modes):
            columns = slice(local * length, (local + 1) * length)
            change_real, change_imag = changes_real[:, columns], changes_imag[:, columns]
            channels.append(window_real * change_real + window_imag * change_imag)
            channels.append(window_real * change_imag - window_imag * change_real)
        channels = [values.reshape(cut) for values in channels]
        power = (window_real**2 + window_imag**2).reshape(cut)
        sent = power[:, :part]
        for other in range(1, layout.halves):
            sent = jnp.where(upper == other, power[:, other * part : (other + 1) * part], sent)
        first = 0
        for values in (*channels, sent):
            rows = slice(first, first + values.shape[1])
            if frame == 0:
                pieces[:, rows] = values
            else:
                pieces[:, rows] += values
            first += values.shape[1]


def sum_kernel(arrived, total):
    total[...] = jnp.sum(arrived[...], axis=0)


def step_kernel(layout, old_pieces, *refs):
    totals, out = refs[:-1], refs[-1]
    upper, _, _, _ = layout.place()
    halves, piece = layout.halves, layout.piece
    planes = 2 * layout.local_modes
    parts = []
    for place in range(halves):
        power = totals[0][planes * piece :]
        for entry in range(1, halves):
            power = jnp.where((upper + entry) % halves == place, totals[entry][planes * piece :], power)
        parts.append(power)
    damped = jnp.concatenate(parts, axis=0) + probe_damping
    for entry, total in enumerate(totals):
        for local in range(layout.local_modes):
            for plane in range(2):
                first = (2 * local + plane) * piece
                stepped = old_pieces[entry, local, plane] + total[first : first + piece] / damped
                for region in range(layout.regions):
                    out[region, entry, local, plane] = stepped


def new_probe(probes, entry, local, plane):
    values = probes[:, entry, local, plane]
    return values.reshape(values.shape[0] * values.shape[1], values.shape[2])


def again_kernel(layout, probes, windows, forward, back, probe_out, probe_power, intensity, fars):
    upper, _, twin, _ = layout.place()
    own_entry = (twin + layout.halves - upper) % layout.halves
    listed = [
        [new_probe(probes, entry, local, plane) for plane in range(2)]
        for entry in range(layout.halves)
        for local in range(layout.local_modes)
    ]
    for frame in range(layout.frames):
        waves = leave(listed, windows[frame, 0], windows[frame, 1], forward, back)
        intensity[frame] = power_of(*waves, layout.length)
        for plane, wave in enumerate(waves):
            fars[frame, plane] = wave
    probe_power[...] = sum(real**2 + imag**2 for real, imag in listed)
    for local in range(layout.local_modes):
        for plane in range(2):
            probe_out[plane, local] = new_probe(probes, own_entry, local, plane)


def terms_kernel(layout, offsets, *refs):
    cores, halves, frames, length = layout.cores, layout.halves, layout.frames, layout.length
    intensities = refs[:cores]
    roots, probes, fars, forward, back, *strips, inner = refs[cores:]
    upper, lower, twin, core = layout.place()
    region = twin * layout.lowers + lower
    for frame in range(frames):
        factor = factor_of(roots, intensities, frame)
        changes_real, changes_imag = come_back(fars[frame], factor, forward, back)
        numer_real = jnp.zeros((length, length), single)
        numer_imag = jnp.zeros((length, length), single)
        for entry in range(halves):
            for local in range(layout.local_modes):
                first = (entry * layout.local_modes + local) * length
                change_real = changes_real[:, first : first + length]
                change_imag = changes_imag[:, first : first + length]
                probe_real, probe_imag = (new_probe(probes, entry, local, plane) for plane in range(2))
                numer_real += probe_real * change_real + probe_imag * change_imag
                numer_imag += probe_real * change_imag - probe_imag * change_real
        lead = offsets[0, region * frames + frame] % layout.band
        for plane, values in enumerate((numer_real, numer_imag)):
            inner[plane] = pltpu.roll(values, lead, 0).reshape(2, cores, layout.strip, length)
        for step, strip in enumerate(strips):
            strip[frame] = inner[:, :, (core + cores - step) % cores]


def post_kernel(layout, offsets, owner, *refs):
    strips, outs = refs[: layout.cores], refs[layout.cores :]
    upper, lower, twin, _ = layout.place()
    region = twin * layout.lowers + lower
    for step, out in enumerate(outs):
        block = upper * layout.lowers + layout.across(lower, step)
        band = band_of_block(owner, block, layout)
        frame, row = jnp.int32(0), offsets[0, region * layout.frames]
        for extra in range(1, layout.frames):
            candidate = offsets[0, region * layout.frames + extra]
            anchor = candidate // layout.band
            over = (anchor <= band) & (band <= anchor + 2)
            frame, row = jnp.where(over, extra, frame), jnp.where(over, candidate, row)
        slot = (band - row // layout.band == 1).astype(jnp.int32)
        for plane in range(2):
            total = strips[0][frame, plane, slot]
            for strip in strips[1:]:
                total += strip[frame, plane, slot]
            out[plane] = total


class Cover:
    def __init__(self, layout, offsets, region, band, core):
        row, self.column = frame_over(offsets, region, band, layout)
        anchor = row // layout.band
        self.lead = row - anchor * layout.band
        self.step = band - anchor
        self.first = core * layout.strip
        self.layout = layout

    def inside(self):
        band = self.layout.band
        middle = (self.step == 1) | (self.step == 2)
        begin = jnp.where(self.step == 0, self.lead, jnp.where(middle, 0, band))
        end = jnp.where(self.step == 2, self.lead, band)
        shape = (self.layout.strip, self.layout.length)
        rows = lax.broadcasted_iota(jnp.int32, shape, 0) + self.first
        return (rows >= begin) & (rows < end)

    def start(self):
        slot = (self.step == 1).astype(jnp.int32)
        length = self.layout.length
        return (slot * self.layout.band + self.first + length - self.lead) % length

    def add(self, total, terms):
        tiles = self.layout.length // lanes
        shift = self.column % lanes
        begin = pl.multiple_of(self.column - shift, lanes)
        spilled = lax.broadcasted_iota(jnp.int32, (terms.shape[0], lanes), 1) < shift
        turned = [
            pltpu.roll(terms[:, tile * lanes : (tile + 1) * lanes], shift, 1) for tile in range(tiles)
        ]
        for tile in range(tiles + 1):
            near = turned[tile] if tile < tiles else 0.0
            over = turned[tile - 1] if tile else 0.0
            total[:, pl.ds(begin + tile * lanes, lanes)] += jnp.where(spilled, over, near)


def density_kernel(layout, offsets, owner, *refs):
    powers, (out, doubled, total) = refs[: layout.cores], refs[layout.cores :]
    upper, lower, _, core = layout.place()
    strip, length = layout.strip, layout.length
    band = band_of_block(owner, upper * layout.lowers + lower, layout)
    power = powers[0][...]
    for more in powers[1:]:
        power += more[...]
    doubled[0] = power
    doubled[1] = power
    wide = doubled.reshape(2 * length, length)
    total[...] = jnp.zeros_like(total)
    for region in range(layout.regions):
        cover = Cover(layout, offsets, region, band, core)
        start = cover.start()
        near = wide[pl.ds(pl.multiple_of(start // 8 * 8, 8), strip + 8), :]
        near = pltpu.roll(near, (strip + 8 - start % 8) % (strip + 8), 0)[:strip]
        cover.add(total, jnp.where(cover.inside(), near, 0.0))
    out[...] = total[:, : layout.width] + object_damping


def place_kernel(layout, offsets, owner, *refs):
    arrived, (out, total) = refs[: layout.lowers], refs[layout.lowers :]
    upper, lower, twin, core = layout.place()
    strip = layout.strip
    band = band_of_block(owner, upper * layout.lowers + lower, layout)
    total[...] = jnp.zeros_like(total)
    for step, terms in enumerate(arrived):
        source = layout.across(lower, step if layout.paired else layout.lowers - step)
        cover = Cover(layout, offsets, twin * layout.lowers + source, band, core)
        inside = cover.inside()
        kept = [jnp.where(inside, terms[plane], 0.0) for plane in range(2)]
        cover.add(total, jnp.concatenate(kept, axis=0))
    for plane in range(2):
        out[plane] = total[plane * strip : (plane + 1) * strip, : layout.width]


def update_kernel(layout, density, block, *refs):
    placed, out = refs[:-1], refs[-1]
    _, _, _, core = layout.place()
    rows = pl.ds(pl.multiple_of(core * layout.strip, layout.strip), layout.strip)
    for plane in range(2):
        total = placed[0][plane]
        for more in placed[1:]:
            total += more[plane]
        out[plane] = block[plane, rows, :] + total / density[...]


def join_kernel(layout, *refs):
    strips, out = refs[:-1], refs[-1]
    _, _, _, core = layout.place()
    for step, strip in enumerate(strips):
        first = (core + step) % layout.cores * layout.strip
        out[:, pl.ds(pl.multiple_of(first, layout.strip), layout.strip), :] = strip[...]


def call(kernel, name, operands, outputs, scratch=(), scalar_count=0, after=()):
    shapes = [jax.ShapeDtypeStruct(shape, single) for shape in outputs]
    count = len(operands)

    def inner(*refs):
        kernel(*refs[:count], *refs[count + len(after) :])

    return pl.pallas_call(
        inner,
        name=name,
        out_shape=shapes,
        in_specs=[scalars] * scalar_count
        + [on_chip] * (count - scalar_count)
        + [pl.BlockSpec(memory_space=pl.ANY)] * len(after),
        out_specs=[on_chip] * len(shapes),
        scratch_shapes=[pltpu.VMEM(shape, single) for shape in scratch],
        compiler_params=pltpu.CompilerParams(vmem_limit_bytes=28 * 2**20),
    )(*operands, *after)


def body(measured, probe_modes, object_bands, scan_offsets, band_owner):
    layout = Layout(
        lax.axis_size("region"),
        lax.axis_size("mode"),
        measured.shape[1],
        measured.shape[0],
        probe_modes.shape[1] * lax.axis_size("mode"),
        object_bands.shape[2],
    )
    regions, halves, cores = layout.regions, layout.halves, layout.cores
    length, piece, frames = layout.length, layout.piece, layout.frames
    local, strip = layout.local_modes, layout.strip
    forward, back = fourier_tables(length)
    corners = scan_offsets.T

    def from_cores(array):
        return [array] + [layout.from_core(array, step) for step in range(1, cores)]

    def from_uppers(array):
        return [array] + [layout.from_upper(array, step) for step in range(1, halves)]

    *cuts, part_measured = pl.pallas_call(
        functools.partial(cut_kernel, layout),
        name="cut",
        out_shape=[jax.ShapeDtypeStruct((2, strip, length), single)] * layout.lowers
        + [jax.ShapeDtypeStruct((frames, layout.part, length), single)],
        in_specs=[pl.BlockSpec(memory_space=pltpu.HBM)] * 4,
        out_specs=[on_chip] * (layout.lowers + 1),
        scratch_shapes=[
            pltpu.VMEM((2, strip, layout.width + lanes), single),
            pltpu.SMEM(corners.shape, jnp.int32),
            pltpu.SMEM(band_owner.shape, jnp.int32),
            pltpu.SemaphoreType.DMA((4,)),
        ],
        compiler_params=pltpu.CompilerParams(vmem_limit_bytes=28 * 2**20),
    )(
        *(
            pltpu.with_memory_space_constraint(array, pltpu.HBM)
            for array in (corners, band_owner, object_bands, measured)
        )
    )
    probes = [probe_modes] + [layout.from_twin(probe_modes, step) for step in range(1, halves)]
    if halves > 1:
        pairs = [
            (layout.device(t, l, t, c), layout.device(u, l, t, c))
            for u, l, t, c in layout.everyone()
            if u != t
        ]
        part_measured = lax.ppermute(part_measured, axes, pairs)
    cuts = [cuts[0]] + [layout.to_row(cut, step) for step, cut in enumerate(cuts[1:], start=1)]
    chosen = []
    for steps in ((0,), tuple(range(1, layout.lowers))):
        chosen = call(
            functools.partial(choose_kernel, layout, steps),
            "choose",
            (corners, band_owner, *(cuts[step] for step in steps), *chosen),
            [(frames, 2, 2, strip, length)],
            scalar_count=2,
        )
    (chosen,) = chosen
    measured_parts = from_cores(part_measured)
    (roots,) = call(
        functools.partial(order_kernel, layout),
        "order",
        (measured, *measured_parts),
        [measured.shape],
        scratch=[(cores, layout.part, length)],
    )
    parts = from_uppers(chosen)
    held, roots = lax.optimization_barrier((chosen, roots))
    strips = list(parts)
    for step in range(1, cores):
        strips += [layout.from_core(part, step) for part in [held] + parts[1:]]
    windows, intensity, kept, old_pieces = call(
        functools.partial(far_kernel, layout),
        "far",
        (corners, *strips, *probes, forward, back),
        [
            (frames, 2, length, length),
            (frames, length, length),
            (frames, 2, local * length, length),
            (halves, local, 2, piece, length),
        ],
        scratch=[(2, 2, cores, strip, length)],
        scalar_count=1,
    )
    (pieces,) = call(
        functools.partial(gradient_kernel, layout),
        "gradient",
        (*from_cores(intensity), roots, windows, kept, forward, back),
        [(regions, 2 * local * piece + piece // halves, length)],
    )
    pieces = layout.within_cube(pieces)
    (total,) = call(sum_kernel, "sum", (pieces,), [pieces.shape[1:]])
    (spread,) = call(
        functools.partial(step_kernel, layout),
        "step",
        (old_pieces, *from_uppers(total)),
        [(regions, halves, local, 2, piece, length)],
    )
    new_probes = layout.within_cube(spread)
    probe_out, probe_power, intensity, fars = call(
        functools.partial(again_kernel, layout),
        "again",
        (new_probes, windows, forward, back),
        [
            (2, local, length, length),
            (length, length),
            (frames, length, length),
            (frames, 2, halves * local * length, length),
        ],
    )
    strips = call(
        functools.partial(terms_kernel, layout),
        "terms",
        (corners, *from_cores(intensity), roots, new_probes, fars, forward, back),
        [(frames, 2, 2, strip, length)] * cores,
        scratch=[(2, 2, cores, strip, length)],
        scalar_count=1,
    )
    strips = [strips[0]] + [
        layout.from_core(sent, step) for step, sent in enumerate(strips[1:], start=1)
    ]
    posted = call(
        functools.partial(post_kernel, layout),
        "post",
        (corners, band_owner, *strips),
        [(2, strip, length)] * layout.lowers,
        scalar_count=2,
    )
    posted = [posted[0]] + [
        layout.to_row(sent, step) for step, sent in enumerate(posted[1:], start=1)
    ]
    (density,) = call(
        functools.partial(density_kernel, layout),
        "density",
        (corners, band_owner, *from_cores(probe_power)),
        [(strip, layout.width)],
        scratch=[(2, length, length), (strip, layout.width + lanes)],
        scalar_count=2,
    )
    (placed,) = call(
        functools.partial(place_kernel, layout),
        "place",
        (corners, band_owner, *posted),
        [(2, strip, layout.width)],
        scratch=[(2 * strip, layout.width + lanes)],
        scalar_count=2,
    )
    placed = [placed] + [layout.from_twin(placed, step) for step in range(1, halves)]
    (new_rows,) = call(
        functools.partial(update_kernel, layout),
        "update",
        (density, object_bands, *placed),
        [(2, strip, layout.width)],
    )
    (object_out,) = call(
        functools.partial(join_kernel, layout), "join", from_cores(new_rows), [object_bands.shape]
    )
    return probe_out, object_out


def solution(mesh):
    in_specs = (
        P("region", None, None),
        P(None, "mode", None, None),
        P(None, "region", None),
        P(),
        P(),
    )
    out_specs = (P(None, "mode", None, None), P(None, "region", None))
    return jax.shard_map(body, mesh=mesh, in_specs=in_specs, out_specs=out_specs, check_vma=False)
```

```python
import functools
import math

import jax
import jax.numpy as jnp
import ml_dtypes
import numpy as np
from jax import lax
from jax.experimental import pallas as pl
from jax.experimental.pallas import tpu as pltpu
from jax.sharding import PartitionSpec as P

intensity_offset = 0.1
probe_damping = 1.0
object_damping = 1.0
half = jnp.bfloat16
single = jnp.float32
axes = ("region", "mode")
lanes = 128
on_chip = pl.BlockSpec(memory_space=pltpu.VMEM)
scalars = pl.BlockSpec(memory_space=pltpu.SMEM)


class Layout:
    def __init__(self, regions, helpers, length, frames, modes, width):
        self.regions, self.helpers = regions, helpers
        self.length, self.frames, self.modes, self.width = length, frames, modes, width
        self.halves = 2 if regions % 2 == 0 and helpers % 2 == 0 else 1
        self.lowers, self.cores = regions // self.halves, helpers // self.halves
        self.local_modes = modes // helpers
        self.band = length // 2
        self.strip = self.band // self.cores
        self.paired = self.lowers & (self.lowers - 1) == 0
        self.piece = length // regions
        self.part = length // self.cores

    def place(self):
        region, helper = lax.axis_index("region"), lax.axis_index("mode")
        upper, lower = region // self.lowers, region % self.lowers
        twin, core = helper // self.cores, helper % self.cores
        return upper, lower, twin, core

    def device(self, upper, lower, twin, core):
        return (upper * self.lowers + lower) * self.helpers + twin * self.cores + core

    def everyone(self):
        for upper in range(self.halves):
            for lower in range(self.lowers):
                for twin in range(self.halves):
                    for core in range(self.cores):
                        yield upper, lower, twin, core

    def cubes(self):
        return [
            [
                self.device(upper, lower, twin, core)
                for twin in range(self.halves)
                for lower in range(self.lowers)
            ]
            for upper in range(self.halves)
            for core in range(self.cores)
        ]

    def from_upper(self, array, step):
        pairs = [
            (self.device((u + step) % self.halves, l, t, c), self.device(u, l, t, c))
            for u, l, t, c in self.everyone()
        ]
        return lax.ppermute(array, axes, pairs)

    def from_core(self, array, step):
        pairs = [
            (self.device(u, l, t, (c + step) % self.cores), self.device(u, l, t, c))
            for u, l, t, c in self.everyone()
        ]
        return lax.ppermute(array, axes, pairs)

    def from_twin(self, array, step):
        pairs = [
            (self.device(u, l, (t + step) % self.halves, c), self.device(u, l, t, c))
            for u, l, t, c in self.everyone()
        ]
        return lax.ppermute(array, axes, pairs)

    def across(self, lower, step):
        if self.paired:
            return lower ^ step
        return (lower + step) % self.lowers

    def to_row(self, array, step):
        pairs = [
            (self.device(u, l, t, c), self.device(u, self.across(l, step), t, c))
            for u, l, t, c in self.everyone()
        ]
        return lax.ppermute(array, axes, pairs)

    def within_cube(self, array):
        return lax.all_to_all(
            array, axes, split_axis=0, concat_axis=0, tiled=True, axis_index_groups=self.cubes()
        )


def fourier_tables(length):
    near = np.arange(length // 2)
    forms = []
    for odd in range(2):
        angles = near[:, None] * (2 * near[None, :] + odd) % length * (2.0 * math.pi / length)
        cosine, sine = np.cos(angles) / math.sqrt(length), np.sin(angles) / math.sqrt(length)
        forms.append(np.block([[cosine, -sine], [sine, cosine]]))
    forward = np.stack(forms)

    def pair(table):
        lead = table.astype(ml_dtypes.bfloat16)
        return np.stack([lead, (table - lead.astype(np.float64)).astype(ml_dtypes.bfloat16)])

    return pair(forward), pair(forward.swapaxes(1, 2))


def split(values):
    lead = values.astype(half)
    return lead, (values - lead.astype(single)).astype(half)


def dot(left, right):
    return jnp.dot(left, right, preferred_element_type=single)


def from_left(table, values):
    lead, trail = split(values)
    return dot(table[0], lead) + dot(table[1], lead) + dot(table[0], trail)


def from_right(values, table):
    lead, trail = split(values)
    return dot(lead, table[0]) + dot(lead, table[1]) + dot(trail, table[0])


def beside(left, right):
    return jnp.concatenate([left, right], axis=1)


def above(top, bottom):
    return jnp.concatenate([top, bottom], axis=0)


def table_of(tables, number):
    return tables[0, number], tables[1, number]


def columns_forward(real, imag, forward):
    middle = real.shape[1] // 2
    real_left, real_right = real[:, :middle], real[:, middle:]
    imag_left, imag_right = imag[:, :middle], imag[:, middle:]
    even = from_right(beside(real_left + real_right, imag_left + imag_right), table_of(forward, 0))
    odd = from_right(beside(real_left - real_right, imag_left - imag_right), table_of(forward, 1))
    return (
        beside(even[:, :middle], odd[:, :middle]),
        beside(even[:, middle:], odd[:, middle:]),
    )


def columns_back(real, imag, back):
    middle = real.shape[1] // 2
    even = from_right(beside(real[:, :middle], imag[:, :middle]), table_of(back, 0))
    odd = from_right(beside(real[:, middle:], imag[:, middle:]), table_of(back, 1))
    plus, minus = even + odd, even - odd
    return (
        beside(plus[:, :middle], minus[:, :middle]),
        beside(plus[:, middle:], minus[:, middle:]),
    )


def rows_forward(real, imag, back):
    middle = real.shape[0] // 2
    real_top, real_bottom = real[:middle], real[middle:]
    imag_top, imag_bottom = imag[:middle], imag[middle:]
    even = from_left(table_of(back, 0), above(real_top + real_bottom, imag_top + imag_bottom))
    odd = from_left(table_of(back, 1), above(real_top - real_bottom, imag_top - imag_bottom))
    return above(even[:middle], odd[:middle]), above(even[middle:], odd[middle:])


def rows_back(real, imag, forward):
    middle = real.shape[0] // 2
    even = from_left(table_of(forward, 0), above(real[:middle], imag[:middle]))
    odd = from_left(table_of(forward, 1), above(real[middle:], imag[middle:]))
    plus, minus = even + odd, even - odd
    return above(plus[:middle], minus[:middle]), above(plus[middle:], minus[middle:])


def band_of_block(owner, block, layout):
    band = jnp.int32(0)
    for candidate in range(layout.regions):
        band = jnp.where(owner[candidate] == block, candidate, band)
    return band


def frame_over(offsets, region, band, layout):
    row, column = offsets[0, region * layout.frames], offsets[1, region * layout.frames]
    for extra in range(1, layout.frames):
        index = region * layout.frames + extra
        anchor = offsets[0, index] // layout.band
        over = (anchor <= band) & (band <= anchor + 2)
        row = jnp.where(over, offsets[0, index], row)
        column = jnp.where(over, offsets[1, index], column)
    return row, column


def cut_kernel(layout, corners, owners, block, measured, *refs):
    outs, (sent, taken, offsets, owner, done) = refs[: layout.lowers], refs[layout.lowers :]
    upper, lower, twin, core = layout.place()
    strip = pl.ds(pl.multiple_of(core * layout.strip, layout.strip), layout.strip)
    part = pl.ds(pl.multiple_of(core * layout.part, layout.part), layout.part)
    copies = [
        pltpu.make_async_copy(corners, offsets, done.at[0]),
        pltpu.make_async_copy(owners, owner, done.at[1]),
        pltpu.make_async_copy(block.at[:, strip, :], taken.at[:, :, : layout.width], done.at[2]),
        pltpu.make_async_copy(measured.at[:, part, :], sent, done.at[3]),
    ]
    for copy in copies:
        copy.start()
    for copy in copies[:3]:
        copy.wait()
    band = band_of_block(owner, upper * layout.lowers + lower, layout)
    tiles = layout.length // lanes
    column_in_tile = lax.broadcasted_iota(jnp.int32, (2 * layout.strip, lanes), 1)
    for step, out in enumerate(outs):
        region = twin * layout.lowers + layout.across(lower, step)
        _, column = frame_over(offsets, region, band, layout)
        shift = column % lanes
        begin = pl.multiple_of(column - shift, lanes)
        kept = column_in_tile < lanes - shift
        turned = []
        for tile in range(tiles + 1):
            values = taken[:, :, pl.ds(begin + tile * lanes, lanes)].reshape(2 * layout.strip, lanes)
            turned.append(pltpu.roll(values, (lanes - shift) % lanes, 1))
        for tile in range(tiles):
            values = jnp.where(kept, turned[tile], turned[tile + 1])
            out[:, :, tile * lanes : (tile + 1) * lanes] = values.reshape(2, layout.strip, lanes)
    copies[3].wait()


def choose_kernel(layout, steps, offsets, owner, *refs):
    arrived, (*before, out) = refs[: len(steps)], refs[len(steps) :]
    upper, lower, twin, core = layout.place()
    rows = lax.broadcasted_iota(jnp.int32, (layout.strip, layout.length), 0) + core * layout.strip
    for frame in range(layout.frames):
        row = offsets[0, (twin * layout.lowers + lower) * layout.frames + frame]
        anchor = row // layout.band
        lead = row - anchor * layout.band
        blocks = [owner[anchor + step] for step in range(3)]
        masks = [rows >= lead, rows >= 0, rows < lead]
        for plane in range(2):
            slots = [ref[frame, plane] for ref in before]
            top, bottom = (slots[0][0], slots[0][1]) if before else (0.0, 0.0)
            for block, mask, slot in zip(blocks, masks, (0, 1, 0)):
                here = block // layout.lowers == upper
                values = top if slot == 0 else bottom
                for step, ref in zip(steps, arrived):
                    came = here & (layout.across(block % layout.lowers, step) == lower)
                    values = jnp.where(mask & came, ref[plane], values)
                top, bottom = (values, bottom) if slot == 0 else (top, values)
            out[frame, plane, 0] = top
            out[frame, plane, 1] = bottom


def side_by_side(stack, rows):
    return jnp.concatenate([stack[at : at + rows] for at in range(0, stack.shape[0], rows)], axis=1)


def one_above_another(row, columns):
    return jnp.concatenate([row[:, at : at + columns] for at in range(0, row.shape[1], columns)], axis=0)


def leave(probes, window_real, window_imag, forward, back):
    length = window_real.shape[0]
    wave = rows_forward(
        jnp.concatenate([real * window_real - imag * window_imag for real, imag in probes], axis=1),
        jnp.concatenate([real * window_imag + imag * window_real for real, imag in probes], axis=1),
        back,
    )
    return columns_forward(*(one_above_another(part, length) for part in wave), forward)


def come_back(far, factor, forward, back):
    length = factor.shape[0]
    factors = jnp.concatenate([factor] * (far.shape[1] // length), axis=0)
    wave = columns_back(far[0] * factors, far[1] * factors, back)
    return rows_back(*(side_by_side(part, length) for part in wave), forward)


def power_of(real, imag, length):
    power = real**2 + imag**2
    return sum(power[at : at + length] for at in range(length, power.shape[0], length)) + power[:length]


def order_kernel(layout, own_measured, *refs):
    parts, (out, other_measured) = refs[: layout.cores], refs[layout.cores :]
    upper, _, twin, core = layout.place()
    length = layout.length
    rows = lax.broadcasted_iota(jnp.int32, (length, length), 0)
    columns = lax.broadcasted_iota(jnp.int32, (length, length), 1)
    middle = length // 2
    pick_rows = (columns == jnp.where(rows < middle, 2 * rows, 2 * (rows - middle) + 1)).astype(half)
    pick_columns = (rows == jnp.where(columns < middle, 2 * columns, 2 * (columns - middle) + 1)).astype(half)

    def exact(product, values):
        lead, rest = split(values)
        trail = (values - lead.astype(single) - rest.astype(single)).astype(half)
        return (product(lead) + product(rest)) + product(trail)

    for frame in range(layout.frames):
        for step, part in enumerate(parts):
            other_measured[(core + step) % layout.cores] = part[frame]
        measured = other_measured[...].reshape(length, length)
        measured = jnp.sqrt(jnp.where(upper == twin, own_measured[frame], measured))
        measured = exact(lambda values: dot(pick_rows, values), measured)
        out[frame] = exact(lambda values: dot(values, pick_columns), measured)


def factor_of(root, intensity):
    return root / jnp.sqrt(intensity + intensity_offset) - 1.0


def first_kernel(layout, offsets, *refs):
    cores, halves, frames, length = layout.cores, layout.halves, layout.frames, layout.length
    count = cores * halves
    shares, probes, refs = refs[:count], refs[count : 2 * count], refs[2 * count :]
    roots, forward, back, windows, pieces, old_pieces, inner, far = refs
    upper, lower, twin, core = layout.place()
    region = twin * layout.lowers + lower
    local, piece = layout.local_modes, layout.piece
    rows = pl.ds(pl.multiple_of(region * piece, piece), piece)
    for entry, probe in enumerate(probes[:halves]):
        place = (twin + entry + halves - upper) % halves
        for k in range(local):
            for plane in range(2):
                old_pieces[place, k, plane] = probe[plane, k, rows, :]
    goes_back = (upper + halves - twin) % halves * local * length
    kept = pl.ds(pl.multiple_of(goes_back, length), local * length)
    cut = (layout.regions, piece, length)
    part = piece // halves
    for frame in range(frames):
        lead = offsets[0, region * frames + frame] % layout.band
        for step in range(cores):
            strip = shares[step * halves][frame]
            for entry in range(1, halves):
                strip += shares[step * halves + entry][frame]
            inner[:, :, (core + step) % cores] = strip
        for plane in range(2):
            wrapped = inner[plane].reshape(length, length)
            windows[frame, plane] = pltpu.roll(wrapped, (length - lead) % length, 0)
        window_real, window_imag = windows[frame, 0], windows[frame, 1]
        listed = [(probe[0, k], probe[1, k]) for probe in probes for k in range(local)]
        waves = leave(listed, window_real, window_imag, forward, back)
        for plane, wave in enumerate(waves):
            far[plane] = wave[: halves * local * length]
        factor = factor_of(roots[frame], power_of(*waves, length))
        changes_real, changes_imag = come_back(far[:, kept, :], factor, forward, back)
        channels = []
        for k in range(local):
            columns = slice(k * length, (k + 1) * length)
            change_real, change_imag = changes_real[:, columns], changes_imag[:, columns]
            channels.append(window_real * change_real + window_imag * change_imag)
            channels.append(window_real * change_imag - window_imag * change_real)
        channels = [values.reshape(cut) for values in channels]
        power = (window_real**2 + window_imag**2).reshape(cut)
        sent = power[:, :part]
        for other in range(1, halves):
            sent = jnp.where(upper == other, power[:, other * part : (other + 1) * part], sent)
        first = 0
        for values in (*channels, sent):
            taken = slice(first, first + values.shape[1])
            if frame == 0:
                pieces[:, taken] = values
            else:
                pieces[:, taken] += values
            first += values.shape[1]


def sum_kernel(arrived, total):
    total[...] = jnp.sum(arrived[...], axis=0)


def step_kernel(layout, old_pieces, *refs):
    totals, out = refs[:-1], refs[-1]
    upper, _, _, _ = layout.place()
    halves, piece = layout.halves, layout.piece
    planes = 2 * layout.local_modes
    parts = []
    for place in range(halves):
        power = totals[0][planes * piece :]
        for entry in range(1, halves):
            power = jnp.where((upper + entry) % halves == place, totals[entry][planes * piece :], power)
        parts.append(power)
    damped = jnp.concatenate(parts, axis=0) + probe_damping
    for entry, total in enumerate(totals):
        for local in range(layout.local_modes):
            for plane in range(2):
                first = (2 * local + plane) * piece
                stepped = old_pieces[entry, local, plane] + total[first : first + piece] / damped
                for region in range(layout.regions):
                    out[region, entry, local, plane] = stepped


def new_probe(probes, entry, local, plane):
    values = probes[:, entry, local, plane]
    return values.reshape(values.shape[0] * values.shape[1], values.shape[2])


def again_kernel(layout, probes, windows, forward, back, probe_out, probe_power, intensity, fars):
    upper, _, twin, _ = layout.place()
    own_entry = (twin + layout.halves - upper) % layout.halves
    listed = [
        [new_probe(probes, entry, local, plane) for plane in range(2)]
        for entry in range(layout.halves)
        for local in range(layout.local_modes)
    ]
    for frame in range(layout.frames):
        waves = leave(listed, windows[frame, 0], windows[frame, 1], forward, back)
        intensity[frame] = power_of(*waves, layout.length)
        for plane, wave in enumerate(waves):
            fars[frame, plane] = wave
    probe_power[...] = sum(real**2 + imag**2 for real, imag in listed)
    for local in range(layout.local_modes):
        for plane in range(2):
            probe_out[plane, local] = new_probe(probes, own_entry, local, plane)


def terms_kernel(layout, offsets, *refs):
    cores, halves, frames, length = layout.cores, layout.halves, layout.frames, layout.length
    intensities = refs[:cores]
    roots, probes, fars, forward, back, *strips, inner = refs[cores:]
    upper, lower, twin, core = layout.place()
    region = twin * layout.lowers + lower
    for frame in range(frames):
        intensity = intensities[0][frame]
        for more in intensities[1:]:
            intensity += more[frame]
        factor = factor_of(roots[frame], intensity)
        changes_real, changes_imag = come_back(fars[frame], factor, forward, back)
        numer_real = jnp.zeros((length, length), single)
        numer_imag = jnp.zeros((length, length), single)
        for entry in range(halves):
            for local in range(layout.local_modes):
                first = (entry * layout.local_modes + local) * length
                change_real = changes_real[:, first : first + length]
                change_imag = changes_imag[:, first : first + length]
                probe_real, probe_imag = (new_probe(probes, entry, local, plane) for plane in range(2))
                numer_real += probe_real * change_real + probe_imag * change_imag
                numer_imag += probe_real * change_imag - probe_imag * change_real
        lead = offsets[0, region * frames + frame] % layout.band
        for plane, values in enumerate((numer_real, numer_imag)):
            inner[plane] = pltpu.roll(values, lead, 0).reshape(2, cores, layout.strip, length)
        for step, strip in enumerate(strips):
            strip[frame] = inner[:, :, (core + cores - step) % cores]


def post_kernel(layout, offsets, owner, *refs):
    strips, outs = refs[: layout.cores], refs[layout.cores :]
    upper, lower, twin, _ = layout.place()
    region = twin * layout.lowers + lower
    for step, out in enumerate(outs):
        block = upper * layout.lowers + layout.across(lower, step)
        band = band_of_block(owner, block, layout)
        frame, row = jnp.int32(0), offsets[0, region * layout.frames]
        for extra in range(1, layout.frames):
            candidate = offsets[0, region * layout.frames + extra]
            anchor = candidate // layout.band
            over = (anchor <= band) & (band <= anchor + 2)
            frame, row = jnp.where(over, extra, frame), jnp.where(over, candidate, row)
        slot = (band - row // layout.band == 1).astype(jnp.int32)
        for plane in range(2):
            total = strips[0][frame, plane, slot]
            for strip in strips[1:]:
                total += strip[frame, plane, slot]
            out[plane] = total


class Cover:
    def __init__(self, layout, offsets, region, band, core):
        row, self.column = frame_over(offsets, region, band, layout)
        anchor = row // layout.band
        self.lead = row - anchor * layout.band
        self.step = band - anchor
        self.first = core * layout.strip
        self.layout = layout

    def inside(self):
        band = self.layout.band
        middle = (self.step == 1) | (self.step == 2)
        begin = jnp.where(self.step == 0, self.lead, jnp.where(middle, 0, band))
        end = jnp.where(self.step == 2, self.lead, band)
        shape = (self.layout.strip, self.layout.length)
        rows = lax.broadcasted_iota(jnp.int32, shape, 0) + self.first
        return (rows >= begin) & (rows < end)

    def start(self):
        slot = (self.step == 1).astype(jnp.int32)
        length = self.layout.length
        return (slot * self.layout.band + self.first + length - self.lead) % length

    def add(self, total, terms):
        tiles = self.layout.length // lanes
        shift = self.column % lanes
        begin = pl.multiple_of(self.column - shift, lanes)
        spilled = lax.broadcasted_iota(jnp.int32, (terms.shape[0], lanes), 1) < shift
        turned = [
            pltpu.roll(terms[:, tile * lanes : (tile + 1) * lanes], shift, 1) for tile in range(tiles)
        ]
        for tile in range(tiles + 1):
            near = turned[tile] if tile < tiles else 0.0
            over = turned[tile - 1] if tile else 0.0
            total[:, pl.ds(begin + tile * lanes, lanes)] += jnp.where(spilled, over, near)


def density_kernel(layout, offsets, owner, *refs):
    powers, (out, doubled, total) = refs[: layout.cores], refs[layout.cores :]
    upper, lower, _, core = layout.place()
    strip, length = layout.strip, layout.length
    band = band_of_block(owner, upper * layout.lowers + lower, layout)
    power = powers[0][...]
    for more in powers[1:]:
        power += more[...]
    doubled[0] = power
    doubled[1] = power
    wide = doubled.reshape(2 * length, length)
    total[...] = jnp.zeros_like(total)
    for region in range(layout.regions):
        cover = Cover(layout, offsets, region, band, core)
        start = cover.start()
        near = wide[pl.ds(pl.multiple_of(start // 8 * 8, 8), strip + 8), :]
        near = pltpu.roll(near, (strip + 8 - start % 8) % (strip + 8), 0)[:strip]
        cover.add(total, jnp.where(cover.inside(), near, 0.0))
    out[...] = total[:, : layout.width] + object_damping


def place_kernel(layout, offsets, owner, *refs):
    arrived, (out, total) = refs[: layout.lowers], refs[layout.lowers :]
    upper, lower, twin, core = layout.place()
    strip = layout.strip
    band = band_of_block(owner, upper * layout.lowers + lower, layout)
    total[...] = jnp.zeros_like(total)
    for step, terms in enumerate(arrived):
        source = layout.across(lower, step if layout.paired else layout.lowers - step)
        cover = Cover(layout, offsets, twin * layout.lowers + source, band, core)
        inside = cover.inside()
        kept = [jnp.where(inside, terms[plane], 0.0) for plane in range(2)]
        cover.add(total, jnp.concatenate(kept, axis=0))
    for plane in range(2):
        out[plane] = total[plane * strip : (plane + 1) * strip, : layout.width]


def update_kernel(layout, density, block, *refs):
    placed, out = refs[:-1], refs[-1]
    _, _, _, core = layout.place()
    rows = pl.ds(pl.multiple_of(core * layout.strip, layout.strip), layout.strip)
    for plane in range(2):
        total = placed[0][plane]
        for more in placed[1:]:
            total += more[plane]
        out[plane] = block[plane, rows, :] + total / density[...]


def join_kernel(layout, *refs):
    strips, out = refs[:-1], refs[-1]
    _, _, _, core = layout.place()
    for step, strip in enumerate(strips):
        first = (core + step) % layout.cores * layout.strip
        out[:, pl.ds(pl.multiple_of(first, layout.strip), layout.strip), :] = strip[...]


def call(kernel, name, operands, outputs, scratch=(), scalar_count=0, after=()):
    shapes = [jax.ShapeDtypeStruct(shape, single) for shape in outputs]
    count = len(operands)

    def inner(*refs):
        kernel(*refs[:count], *refs[count + len(after) :])

    return pl.pallas_call(
        inner,
        name=name,
        out_shape=shapes,
        in_specs=[scalars] * scalar_count
        + [on_chip] * (count - scalar_count)
        + [pl.BlockSpec(memory_space=pl.ANY)] * len(after),
        out_specs=[on_chip] * len(shapes),
        scratch_shapes=[pltpu.VMEM(shape, single) for shape in scratch],
        compiler_params=pltpu.CompilerParams(vmem_limit_bytes=28 * 2**20),
    )(*operands, *after)


def body(measured, probe_modes, object_bands, scan_offsets, band_owner):
    layout = Layout(
        lax.axis_size("region"),
        lax.axis_size("mode"),
        measured.shape[1],
        measured.shape[0],
        probe_modes.shape[1] * lax.axis_size("mode"),
        object_bands.shape[2],
    )
    regions, halves, cores = layout.regions, layout.halves, layout.cores
    length, piece, frames = layout.length, layout.piece, layout.frames
    local, strip = layout.local_modes, layout.strip
    forward, back = fourier_tables(length)
    corners = scan_offsets.T

    def from_cores(array):
        return [array] + [layout.from_core(array, step) for step in range(1, cores)]

    def from_uppers(array):
        return [array] + [layout.from_upper(array, step) for step in range(1, halves)]

    *cuts, part_measured = pl.pallas_call(
        functools.partial(cut_kernel, layout),
        name="cut",
        out_shape=[jax.ShapeDtypeStruct((2, strip, length), single)] * layout.lowers
        + [jax.ShapeDtypeStruct((frames, layout.part, length), single)],
        in_specs=[pl.BlockSpec(memory_space=pltpu.HBM)] * 4,
        out_specs=[on_chip] * (layout.lowers + 1),
        scratch_shapes=[
            pltpu.VMEM((2, strip, layout.width + lanes), single),
            pltpu.SMEM(corners.shape, jnp.int32),
            pltpu.SMEM(band_owner.shape, jnp.int32),
            pltpu.SemaphoreType.DMA((4,)),
        ],
        compiler_params=pltpu.CompilerParams(vmem_limit_bytes=28 * 2**20),
    )(
        *(
            pltpu.with_memory_space_constraint(array, pltpu.HBM)
            for array in (corners, band_owner, object_bands, measured)
        )
    )
    probes = [probe_modes] + [layout.from_twin(probe_modes, step) for step in range(1, halves)]
    if halves > 1:
        pairs = [
            (layout.device(t, l, t, c), layout.device(u, l, t, c))
            for u, l, t, c in layout.everyone()
            if u != t
        ]
        part_measured = lax.ppermute(part_measured, axes, pairs)
    cuts = [cuts[0]] + [layout.to_row(cut, step) for step, cut in enumerate(cuts[1:], start=1)]
    chosen = []
    for steps in ((0,), tuple(range(1, layout.lowers))):
        chosen = call(
            functools.partial(choose_kernel, layout, steps),
            "choose",
            (corners, band_owner, *(cuts[step] for step in steps), *chosen),
            [(frames, 2, 2, strip, length)],
            scalar_count=2,
        )
    (chosen,) = chosen
    measured_parts = from_cores(part_measured)
    (roots,) = call(
        functools.partial(order_kernel, layout),
        "order",
        (measured, *measured_parts),
        [measured.shape],
        scratch=[(cores, layout.part, length)],
    )
    parts = from_uppers(chosen)
    held, roots = lax.optimization_barrier((chosen, roots))
    strips = list(parts)
    for step in range(1, cores):
        strips += [layout.from_core(part, step) for part in [held] + parts[1:]]
    every_probe = list(probes)
    for step in range(1, cores):
        every_probe += [layout.from_core(probe, step) for probe in probes]
    windows, pieces, old_pieces = call(
        functools.partial(first_kernel, layout),
        "first",
        (corners, *strips, *every_probe, roots, forward, back),
        [
            (frames, 2, length, length),
            (regions, 2 * local * piece + piece // halves, length),
            (halves, local, 2, piece, length),
        ],
        scratch=[
            (2, 2, cores, strip, length),
            (2, halves * local * length, length),
        ],
        scalar_count=1,
    )
    pieces = layout.within_cube(pieces)
    (total,) = call(sum_kernel, "sum", (pieces,), [pieces.shape[1:]])
    (spread,) = call(
        functools.partial(step_kernel, layout),
        "step",
        (old_pieces, *from_uppers(total)),
        [(regions, halves, local, 2, piece, length)],
    )
    new_probes = layout.within_cube(spread)
    probe_out, probe_power, intensity, fars = call(
        functools.partial(again_kernel, layout),
        "again",
        (new_probes, windows, forward, back),
        [
            (2, local, length, length),
            (length, length),
            (frames, length, length),
            (frames, 2, halves * local * length, length),
        ],
    )
    strips = call(
        functools.partial(terms_kernel, layout),
        "terms",
        (corners, *from_cores(intensity), roots, new_probes, fars, forward, back),
        [(frames, 2, 2, strip, length)] * cores,
        scratch=[(2, 2, cores, strip, length)],
        scalar_count=1,
    )
    strips = [strips[0]] + [
        layout.from_core(sent, step) for step, sent in enumerate(strips[1:], start=1)
    ]
    posted = call(
        functools.partial(post_kernel, layout),
        "post",
        (corners, band_owner, *strips),
        [(2, strip, length)] * layout.lowers,
        scalar_count=2,
    )
    posted = [posted[0]] + [
        layout.to_row(sent, step) for step, sent in enumerate(posted[1:], start=1)
    ]
    (density,) = call(
        functools.partial(density_kernel, layout),
        "density",
        (corners, band_owner, *from_cores(probe_power)),
        [(strip, layout.width)],
        scratch=[(2, length, length), (strip, layout.width + lanes)],
        scalar_count=2,
    )
    (placed,) = call(
        functools.partial(place_kernel, layout),
        "place",
        (corners, band_owner, *posted),
        [(2, strip, layout.width)],
        scratch=[(2 * strip, layout.width + lanes)],
        scalar_count=2,
    )
    placed = [placed] + [layout.from_twin(placed, step) for step in range(1, halves)]
    (new_rows,) = call(
        functools.partial(update_kernel, layout),
        "update",
        (density, object_bands, *placed),
        [(2, strip, layout.width)],
    )
    (object_out,) = call(
        functools.partial(join_kernel, layout), "join", from_cores(new_rows), [object_bands.shape]
    )
    return probe_out, object_out


def solution(mesh):
    in_specs = (
        P("region", None, None),
        P(None, "mode", None, None),
        P(None, "region", None),
        P(),
        P(),
    )
    out_specs = (P(None, "mode", None, None), P(None, "region", None))
    return jax.shard_map(body, mesh=mesh, in_specs=in_specs, out_specs=out_specs, check_vma=False)
```

```python
import functools
import math

import jax
import jax.numpy as jnp
import ml_dtypes
import numpy as np
from jax import lax
from jax.experimental import pallas as pl
from jax.experimental.pallas import tpu as pltpu
from jax.sharding import PartitionSpec as P

intensity_offset = 0.1
probe_damping = 1.0
object_damping = 1.0
half = jnp.bfloat16
single = jnp.float32
axes = ("region", "mode")
lanes = 128
on_chip = pl.BlockSpec(memory_space=pltpu.VMEM)


class Layout:
    def __init__(self, regions, helpers, length, frames, modes, width):
        self.regions, self.helpers = regions, helpers
        self.length, self.frames, self.modes, self.width = length, frames, modes, width
        self.halves = 2 if regions % 2 == 0 and helpers % 2 == 0 else 1
        self.lowers, self.cores = regions // self.halves, helpers // self.halves
        self.local_modes = modes // helpers
        self.band = length // 2
        self.strip = self.band // self.cores
        self.paired = self.lowers & (self.lowers - 1) == 0
        self.piece = length // regions
        self.part = length // self.cores

    def place(self):
        region, helper = lax.axis_index("region"), lax.axis_index("mode")
        upper, lower = region // self.lowers, region % self.lowers
        twin, core = helper // self.cores, helper % self.cores
        return upper, lower, twin, core

    def device(self, upper, lower, twin, core):
        return (upper * self.lowers + lower) * self.helpers + twin * self.cores + core

    def everyone(self):
        for upper in range(self.halves):
            for lower in range(self.lowers):
                for twin in range(self.halves):
                    for core in range(self.cores):
                        yield upper, lower, twin, core

    def cubes(self):
        return [
            [
                self.device(upper, lower, twin, core)
                for twin in range(self.halves)
                for lower in range(self.lowers)
            ]
            for upper in range(self.halves)
            for core in range(self.cores)
        ]

    def from_upper(self, array, step):
        pairs = [
            (self.device((u + step) % self.halves, l, t, c), self.device(u, l, t, c))
            for u, l, t, c in self.everyone()
        ]
        return lax.ppermute(array, axes, pairs)

    def from_core(self, array, step):
        pairs = [
            (self.device(u, l, t, (c + step) % self.cores), self.device(u, l, t, c))
            for u, l, t, c in self.everyone()
        ]
        return lax.ppermute(array, axes, pairs)

    def from_twin(self, array, step):
        pairs = [
            (self.device(u, l, (t + step) % self.halves, c), self.device(u, l, t, c))
            for u, l, t, c in self.everyone()
        ]
        return lax.ppermute(array, axes, pairs)

    def across(self, lower, step):
        if self.paired:
            return lower ^ step
        return (lower + step) % self.lowers

    def to_row(self, array, step):
        pairs = [
            (self.device(u, l, t, c), self.device(u, self.across(l, step), t, c))
            for u, l, t, c in self.everyone()
        ]
        return lax.ppermute(array, axes, pairs)

    def within_cube(self, array):
        return lax.all_to_all(
            array, axes, split_axis=0, concat_axis=0, tiled=True, axis_index_groups=self.cubes()
        )


def fourier_tables(length):
    near = np.arange(length // 2)
    forms = []
    for odd in range(2):
        angles = near[:, None] * (2 * near[None, :] + odd) % length * (2.0 * math.pi / length)
        cosine, sine = np.cos(angles) / math.sqrt(length), np.sin(angles) / math.sqrt(length)
        forms.append(np.block([[cosine, -sine], [sine, cosine]]))
    forward = np.stack(forms)

    def pair(table):
        lead = table.astype(ml_dtypes.bfloat16)
        return np.stack([lead, (table - lead.astype(np.float64)).astype(ml_dtypes.bfloat16)])

    return pair(forward), pair(forward.swapaxes(1, 2))


def split(values):
    lead = values.astype(half)
    return lead, (values - lead.astype(single)).astype(half)


def dot(left, right):
    return jnp.dot(left, right, preferred_element_type=single)


def from_left(table, values):
    lead, trail = split(values)
    return dot(table[0], lead) + dot(table[1], lead) + dot(table[0], trail)


def from_right(values, table):
    lead, trail = split(values)
    return dot(lead, table[0]) + dot(lead, table[1]) + dot(trail, table[0])


def beside(left, right):
    return jnp.concatenate([left, right], axis=1)


def above(top, bottom):
    return jnp.concatenate([top, bottom], axis=0)


def table_of(tables, number):
    return tables[0, number], tables[1, number]


def columns_forward(real, imag, forward):
    middle = real.shape[1] // 2
    real_left, real_right = real[:, :middle], real[:, middle:]
    imag_left, imag_right = imag[:, :middle], imag[:, middle:]
    even = from_right(beside(real_left + real_right, imag_left + imag_right), table_of(forward, 0))
    odd = from_right(beside(real_left - real_right, imag_left - imag_right), table_of(forward, 1))
    return (
        beside(even[:, :middle], odd[:, :middle]),
        beside(even[:, middle:], odd[:, middle:]),
    )


def columns_back(real, imag, back):
    middle = real.shape[1] // 2
    even = from_right(beside(real[:, :middle], imag[:, :middle]), table_of(back, 0))
    odd = from_right(beside(real[:, middle:], imag[:, middle:]), table_of(back, 1))
    plus, minus = even + odd, even - odd
    return (
        beside(plus[:, :middle], minus[:, :middle]),
        beside(plus[:, middle:], minus[:, middle:]),
    )


def rows_forward(real, imag, back):
    middle = real.shape[0] // 2
    real_top, real_bottom = real[:middle], real[middle:]
    imag_top, imag_bottom = imag[:middle], imag[middle:]
    even = from_left(table_of(back, 0), above(real_top + real_bottom, imag_top + imag_bottom))
    odd = from_left(table_of(back, 1), above(real_top - real_bottom, imag_top - imag_bottom))
    return above(even[:middle], odd[:middle]), above(even[middle:], odd[middle:])


def rows_back(real, imag, forward):
    middle = real.shape[0] // 2
    even = from_left(table_of(forward, 0), above(real[:middle], imag[:middle]))
    odd = from_left(table_of(forward, 1), above(real[middle:], imag[middle:]))
    plus, minus = even + odd, even - odd
    return above(plus[:middle], minus[:middle]), above(plus[middle:], minus[middle:])


class Table:
    def __init__(self, ref):
        self.values = ref[...].astype(single)
        self.rows = lax.broadcasted_iota(jnp.int32, self.values.shape, 0)
        self.columns = lax.broadcasted_iota(jnp.int32, self.values.shape, 1)

    def __getitem__(self, place):
        row, column = place if isinstance(place, tuple) else (0, place)
        wanted = (self.rows == row) & (self.columns == column)
        return jnp.sum(jnp.where(wanted, self.values, 0.0)).astype(jnp.int32)


def band_of_block(owner, block, layout):
    band = jnp.int32(0)
    for candidate in range(layout.regions):
        band = jnp.where(owner[candidate] == block, candidate, band)
    return band


def frame_over(offsets, region, band, layout):
    row, column = offsets[0, region * layout.frames], offsets[1, region * layout.frames]
    for extra in range(1, layout.frames):
        index = region * layout.frames + extra
        anchor = offsets[0, index] // layout.band
        over = (anchor <= band) & (band <= anchor + 2)
        row = jnp.where(over, offsets[0, index], row)
        column = jnp.where(over, offsets[1, index], column)
    return row, column


def cut_kernel(layout, corners, owners, block, measured, *refs):
    outs, (sent, taken, offsets, owner, done) = refs[: layout.lowers], refs[layout.lowers :]
    upper, lower, twin, core = layout.place()
    strip = pl.ds(pl.multiple_of(core * layout.strip, layout.strip), layout.strip)
    part = pl.ds(pl.multiple_of(core * layout.part, layout.part), layout.part)
    copies = [
        pltpu.make_async_copy(corners, offsets, done.at[0]),
        pltpu.make_async_copy(owners, owner, done.at[1]),
        pltpu.make_async_copy(block.at[:, strip, :], taken.at[:, :, : layout.width], done.at[2]),
        pltpu.make_async_copy(measured.at[:, part, :], sent, done.at[3]),
    ]
    for copy in copies:
        copy.start()
    for copy in copies[:3]:
        copy.wait()
    band = band_of_block(owner, upper * layout.lowers + lower, layout)
    tiles = layout.length // lanes
    column_in_tile = lax.broadcasted_iota(jnp.int32, (2 * layout.strip, lanes), 1)
    for step, out in enumerate(outs):
        region = twin * layout.lowers + layout.across(lower, step)
        _, column = frame_over(offsets, region, band, layout)
        shift = column % lanes
        begin = pl.multiple_of(column - shift, lanes)
        kept = column_in_tile < lanes - shift
        turned = []
        for tile in range(tiles + 1):
            values = taken[:, :, pl.ds(begin + tile * lanes, lanes)].reshape(2 * layout.strip, lanes)
            turned.append(pltpu.roll(values, (lanes - shift) % lanes, 1))
        for tile in range(tiles):
            values = jnp.where(kept, turned[tile], turned[tile + 1])
            out[:, :, tile * lanes : (tile + 1) * lanes] = values.reshape(2, layout.strip, lanes)
    copies[3].wait()


def choose_kernel(layout, steps, offsets, owner, *refs):
    arrived, (*before, out) = refs[: len(steps)], refs[len(steps) :]
    upper, lower, twin, core = layout.place()
    rows = lax.broadcasted_iota(jnp.int32, (layout.strip, layout.length), 0) + core * layout.strip
    for frame in range(layout.frames):
        row = offsets[0, (twin * layout.lowers + lower) * layout.frames + frame]
        anchor = row // layout.band
        lead = row - anchor * layout.band
        blocks = [owner[anchor + step] for step in range(3)]
        masks = [rows >= lead, rows >= 0, rows < lead]
        for plane in range(2):
            slots = [ref[frame, plane] for ref in before]
            top, bottom = (slots[0][0], slots[0][1]) if before else (0.0, 0.0)
            for block, mask, slot in zip(blocks, masks, (0, 1, 0)):
                here = block // layout.lowers == upper
                values = top if slot == 0 else bottom
                for step, ref in zip(steps, arrived):
                    came = here & (layout.across(block % layout.lowers, step) == lower)
                    values = jnp.where(mask & came, ref[plane], values)
                top, bottom = (values, bottom) if slot == 0 else (top, values)
            out[frame, plane, 0] = top
            out[frame, plane, 1] = bottom


def side_by_side(stack, rows):
    return jnp.concatenate([stack[at : at + rows] for at in range(0, stack.shape[0], rows)], axis=1)


def one_above_another(row, columns):
    return jnp.concatenate([row[:, at : at + columns] for at in range(0, row.shape[1], columns)], axis=0)


def leave(probes, window_real, window_imag, forward, back):
    length = window_real.shape[0]
    wave = rows_forward(
        jnp.concatenate([real * window_real - imag * window_imag for real, imag in probes], axis=1),
        jnp.concatenate([real * window_imag + imag * window_real for real, imag in probes], axis=1),
        back,
    )
    return columns_forward(*(one_above_another(part, length) for part in wave), forward)


def come_back(far, factor, forward, back):
    length = factor.shape[0]
    factors = jnp.concatenate([factor] * (far.shape[1] // length), axis=0)
    wave = columns_back(far[0] * factors, far[1] * factors, back)
    return rows_back(*(side_by_side(part, length) for part in wave), forward)


def power_of(real, imag, length):
    power = real**2 + imag**2
    return sum(power[at : at + length] for at in range(length, power.shape[0], length)) + power[:length]


def order_kernel(layout, own_measured, *refs):
    parts, (out, other_measured) = refs[: layout.cores], refs[layout.cores :]
    upper, _, twin, core = layout.place()
    length = layout.length
    rows = lax.broadcasted_iota(jnp.int32, (length, length), 0)
    columns = lax.broadcasted_iota(jnp.int32, (length, length), 1)
    middle = length // 2
    pick_rows = (columns == jnp.where(rows < middle, 2 * rows, 2 * (rows - middle) + 1)).astype(half)
    pick_columns = (rows == jnp.where(columns < middle, 2 * columns, 2 * (columns - middle) + 1)).astype(half)

    def exact(product, values):
        lead, rest = split(values)
        trail = (values - lead.astype(single) - rest.astype(single)).astype(half)
        return (product(lead) + product(rest)) + product(trail)

    for frame in range(layout.frames):
        for step, part in enumerate(parts):
            other_measured[(core + step) % layout.cores] = part[frame]
        measured = other_measured[...].reshape(length, length)
        measured = jnp.sqrt(jnp.where(upper == twin, own_measured[frame], measured))
        measured = exact(lambda values: dot(pick_rows, values), measured)
        out[frame] = exact(lambda values: dot(values, pick_columns), measured)


def factor_of(root, intensity):
    return root / jnp.sqrt(intensity + intensity_offset) - 1.0


def first_kernel(layout, offsets, *refs):
    cores, halves, frames, length = layout.cores, layout.halves, layout.frames, layout.length
    count = cores * halves
    shares, probes, refs = refs[:count], refs[count : 2 * count], refs[2 * count :]
    roots, forward, back, windows, pieces, old_pieces, inner, far = refs
    upper, lower, twin, core = layout.place()
    region = twin * layout.lowers + lower
    local, piece = layout.local_modes, layout.piece
    rows = pl.ds(pl.multiple_of(region * piece, piece), piece)
    for entry, probe in enumerate(probes[:halves]):
        place = (twin + entry + halves - upper) % halves
        for k in range(local):
            for plane in range(2):
                old_pieces[place, k, plane] = probe[plane, k, rows, :]
    goes_back = (upper + halves - twin) % halves * local * length
    kept = pl.ds(pl.multiple_of(goes_back, length), local * length)
    cut = (layout.regions, piece, length)
    part = piece // halves
    for frame in range(frames):
        lead = offsets[0, region * frames + frame] % layout.band
        for step in range(cores):
            strip = shares[step * halves][frame]
            for entry in range(1, halves):
                strip += shares[step * halves + entry][frame]
            inner[:, :, (core + step) % cores] = strip
        for plane in range(2):
            wrapped = inner[plane].reshape(length, length)
            windows[frame, plane] = pltpu.roll(wrapped, (length - lead) % length, 0)
        window_real, window_imag = windows[frame, 0], windows[frame, 1]
        listed = [(probe[0, k], probe[1, k]) for probe in probes for k in range(local)]
        waves = leave(listed, window_real, window_imag, forward, back)
        for plane, wave in enumerate(waves):
            far[plane] = wave[: halves * local * length]
        factor = factor_of(roots[frame], power_of(*waves, length))
        changes_real, changes_imag = come_back(far[:, kept, :], factor, forward, back)
        channels = []
        for k in range(local):
            columns = slice(k * length, (k + 1) * length)
            change_real, change_imag = changes_real[:, columns], changes_imag[:, columns]
            channels.append(window_real * change_real + window_imag * change_imag)
            channels.append(window_real * change_imag - window_imag * change_real)
        channels = [values.reshape(cut) for values in channels]
        power = (window_real**2 + window_imag**2).reshape(cut)
        sent = power[:, :part]
        for other in range(1, halves):
            sent = jnp.where(upper == other, power[:, other * part : (other + 1) * part], sent)
        first = 0
        for values in (*channels, sent):
            taken = slice(first, first + values.shape[1])
            if frame == 0:
                pieces[:, taken] = values
            else:
                pieces[:, taken] += values
            first += values.shape[1]


def sum_kernel(arrived, total):
    total[...] = jnp.sum(arrived[...], axis=0)


def step_kernel(layout, old_pieces, *refs):
    totals, out = refs[:-1], refs[-1]
    upper, _, _, _ = layout.place()
    halves, piece = layout.halves, layout.piece
    planes = 2 * layout.local_modes
    parts = []
    for place in range(halves):
        power = totals[0][planes * piece :]
        for entry in range(1, halves):
            power = jnp.where((upper + entry) % halves == place, totals[entry][planes * piece :], power)
        parts.append(power)
    damped = jnp.concatenate(parts, axis=0) + probe_damping
    for entry, total in enumerate(totals):
        for local in range(layout.local_modes):
            for plane in range(2):
                first = (2 * local + plane) * piece
                stepped = old_pieces[entry, local, plane] + total[first : first + piece] / damped
                for region in range(layout.regions):
                    out[region, entry, local, plane] = stepped


def new_probe(probes, entry, local, plane):
    values = probes[:, entry, local, plane]
    return values.reshape(values.shape[0] * values.shape[1], values.shape[2])


def probe_kernel(layout, probes, out):
    upper, _, twin, _ = layout.place()
    entry = (twin + layout.halves - upper) % layout.halves
    for local in range(layout.local_modes):
        for plane in range(2):
            out[plane, local] = new_probe(probes, entry, local, plane)


def again_kernel(layout, probes, windows, forward, back, probe_power, intensity, fars):
    listed = [
        [new_probe(probes, entry, local, plane) for plane in range(2)]
        for entry in range(layout.halves)
        for local in range(layout.local_modes)
    ]
    for frame in range(layout.frames):
        waves = leave(listed, windows[frame, 0], windows[frame, 1], forward, back)
        intensity[frame] = power_of(*waves, layout.length)
        for plane, wave in enumerate(waves):
            fars[frame, plane] = wave
    probe_power[...] = sum(real**2 + imag**2 for real, imag in listed)


def terms_kernel(layout, offsets, *refs):
    cores, halves, frames, length = layout.cores, layout.halves, layout.frames, layout.length
    intensities = refs[:cores]
    roots, probes, fars, forward, back, *strips, inner = refs[cores:]
    upper, lower, twin, core = layout.place()
    region = twin * layout.lowers + lower
    for frame in range(frames):
        intensity = intensities[0][frame]
        for more in intensities[1:]:
            intensity += more[frame]
        factor = factor_of(roots[frame], intensity)
        changes_real, changes_imag = come_back(fars[frame], factor, forward, back)
        numer_real = jnp.zeros((length, length), single)
        numer_imag = jnp.zeros((length, length), single)
        for entry in range(halves):
            for local in range(layout.local_modes):
                first = (entry * layout.local_modes + local) * length
                change_real = changes_real[:, first : first + length]
                change_imag = changes_imag[:, first : first + length]
                probe_real, probe_imag = (new_probe(probes, entry, local, plane) for plane in range(2))
                numer_real += probe_real * change_real + probe_imag * change_imag
                numer_imag += probe_real * change_imag - probe_imag * change_real
        lead = offsets[0, region * frames + frame] % layout.band
        for plane, values in enumerate((numer_real, numer_imag)):
            inner[plane] = pltpu.roll(values, lead, 0).reshape(2, cores, layout.strip, length)
        for step, strip in enumerate(strips):
            strip[frame] = inner[:, :, (core + cores - step) % cores]


def post_kernel(layout, offsets, owner, *refs):
    strips, outs = refs[: layout.cores], refs[layout.cores :]
    upper, lower, twin, _ = layout.place()
    region = twin * layout.lowers + lower
    for step, out in enumerate(outs):
        block = upper * layout.lowers + layout.across(lower, step)
        band = band_of_block(owner, block, layout)
        frame, row = jnp.int32(0), offsets[0, region * layout.frames]
        for extra in range(1, layout.frames):
            candidate = offsets[0, region * layout.frames + extra]
            anchor = candidate // layout.band
            over = (anchor <= band) & (band <= anchor + 2)
            frame, row = jnp.where(over, extra, frame), jnp.where(over, candidate, row)
        slot = (band - row // layout.band == 1).astype(jnp.int32)
        for plane in range(2):
            total = strips[0][frame, plane, slot]
            for strip in strips[1:]:
                total += strip[frame, plane, slot]
            out[plane] = total


class Cover:
    def __init__(self, layout, offsets, region, band, core):
        row, self.column = frame_over(offsets, region, band, layout)
        anchor = row // layout.band
        self.lead = row - anchor * layout.band
        self.step = band - anchor
        self.first = core * layout.strip
        self.layout = layout

    def inside(self):
        band = self.layout.band
        middle = (self.step == 1) | (self.step == 2)
        begin = jnp.where(self.step == 0, self.lead, jnp.where(middle, 0, band))
        end = jnp.where(self.step == 2, self.lead, band)
        shape = (self.layout.strip, self.layout.length)
        rows = lax.broadcasted_iota(jnp.int32, shape, 0) + self.first
        return (rows >= begin) & (rows < end)

    def start(self):
        slot = (self.step == 1).astype(jnp.int32)
        length = self.layout.length
        return (slot * self.layout.band + self.first + length - self.lead) % length

    def add(self, total, terms):
        tiles = self.layout.length // lanes
        shift = self.column % lanes
        begin = pl.multiple_of(self.column - shift, lanes)
        spilled = lax.broadcasted_iota(jnp.int32, (terms.shape[0], lanes), 1) < shift
        turned = [
            pltpu.roll(terms[:, tile * lanes : (tile + 1) * lanes], shift, 1) for tile in range(tiles)
        ]
        for tile in range(tiles + 1):
            near = turned[tile] if tile < tiles else 0.0
            over = turned[tile - 1] if tile else 0.0
            total[:, pl.ds(begin + tile * lanes, lanes)] += jnp.where(spilled, over, near)


def density_kernel(layout, offsets, owner, *refs):
    powers, (out, doubled, total) = refs[: layout.cores], refs[layout.cores :]
    upper, lower, _, core = layout.place()
    strip, length = layout.strip, layout.length
    band = band_of_block(owner, upper * layout.lowers + lower, layout)
    power = powers[0][...]
    for more in powers[1:]:
        power += more[...]
    doubled[0] = power
    doubled[1] = power
    wide = doubled.reshape(2 * length, length)
    total[...] = jnp.zeros_like(total)
    for region in range(layout.regions):
        cover = Cover(layout, offsets, region, band, core)
        start = cover.start()
        near = wide[pl.ds(pl.multiple_of(start // 8 * 8, 8), strip + 8), :]
        near = pltpu.roll(near, (strip + 8 - start % 8) % (strip + 8), 0)[:strip]
        cover.add(total, jnp.where(cover.inside(), near, 0.0))
    out[...] = total[:, : layout.width] + object_damping


def place_kernel(layout, offsets, owner, *refs):
    arrived, (out, total) = refs[: layout.lowers], refs[layout.lowers :]
    upper, lower, twin, core = layout.place()
    strip = layout.strip
    band = band_of_block(owner, upper * layout.lowers + lower, layout)
    total[...] = jnp.zeros_like(total)
    for step, terms in enumerate(arrived):
        source = layout.across(lower, step if layout.paired else layout.lowers - step)
        cover = Cover(layout, offsets, twin * layout.lowers + source, band, core)
        inside = cover.inside()
        kept = [jnp.where(inside, terms[plane], 0.0) for plane in range(2)]
        cover.add(total, jnp.concatenate(kept, axis=0))
    for plane in range(2):
        out[plane] = total[plane * strip : (plane + 1) * strip, : layout.width]


def update_kernel(layout, density, block, *refs):
    placed, out = refs[:-1], refs[-1]
    _, _, _, core = layout.place()
    rows = pl.ds(pl.multiple_of(core * layout.strip, layout.strip), layout.strip)
    for plane in range(2):
        total = placed[0][plane]
        for more in placed[1:]:
            total += more[plane]
        out[plane] = block[plane, rows, :] + total / density[...]


def join_kernel(layout, *refs):
    strips, out = refs[:-1], refs[-1]
    _, _, _, core = layout.place()
    for step, strip in enumerate(strips):
        first = (core + step) % layout.cores * layout.strip
        out[:, pl.ds(pl.multiple_of(first, layout.strip), layout.strip), :] = strip[...]


def call(kernel, name, operands, outputs, scratch=(), scalar_count=0, after=()):
    shapes = [jax.ShapeDtypeStruct(shape, single) for shape in outputs]
    count = len(operands)

    def inner(*refs):
        tables = [Table(ref) for ref in refs[:scalar_count]]
        kernel(*tables, *refs[scalar_count:count], *refs[count + len(after) :])

    return pl.pallas_call(
        inner,
        name=name,
        out_shape=shapes,
        in_specs=[on_chip] * count
        + [pl.BlockSpec(memory_space=pl.ANY)] * len(after),
        out_specs=[on_chip] * len(shapes),
        scratch_shapes=[pltpu.VMEM(shape, single) for shape in scratch],
        compiler_params=pltpu.CompilerParams(vmem_limit_bytes=28 * 2**20),
    )(*operands, *after)


def body(measured, probe_modes, object_bands, scan_offsets, band_owner):
    layout = Layout(
        lax.axis_size("region"),
        lax.axis_size("mode"),
        measured.shape[1],
        measured.shape[0],
        probe_modes.shape[1] * lax.axis_size("mode"),
        object_bands.shape[2],
    )
    regions, halves, cores = layout.regions, layout.halves, layout.cores
    length, piece, frames = layout.length, layout.piece, layout.frames
    local, strip = layout.local_modes, layout.strip
    forward, back = fourier_tables(length)
    corners, owners = scan_offsets.T, band_owner[None]

    def from_cores(array):
        return [array] + [layout.from_core(array, step) for step in range(1, cores)]

    def from_uppers(array):
        return [array] + [layout.from_upper(array, step) for step in range(1, halves)]

    *cuts, part_measured = pl.pallas_call(
        functools.partial(cut_kernel, layout),
        name="cut",
        out_shape=[jax.ShapeDtypeStruct((2, strip, length), single)] * layout.lowers
        + [jax.ShapeDtypeStruct((frames, layout.part, length), single)],
        in_specs=[pl.BlockSpec(memory_space=pltpu.HBM)] * 4,
        out_specs=[on_chip] * (layout.lowers + 1),
        scratch_shapes=[
            pltpu.VMEM((2, strip, layout.width + lanes), single),
            pltpu.SMEM(corners.shape, jnp.int32),
            pltpu.SMEM(band_owner.shape, jnp.int32),
            pltpu.SemaphoreType.DMA((4,)),
        ],
        compiler_params=pltpu.CompilerParams(vmem_limit_bytes=28 * 2**20),
    )(
        *(
            pltpu.with_memory_space_constraint(array, pltpu.HBM)
            for array in (corners, band_owner, object_bands, measured)
        )
    )
    probes = [probe_modes] + [layout.from_twin(probe_modes, step) for step in range(1, halves)]
    if halves > 1:
        pairs = [
            (layout.device(t, l, t, c), layout.device(u, l, t, c))
            for u, l, t, c in layout.everyone()
            if u != t
        ]
        part_measured = lax.ppermute(part_measured, axes, pairs)
    cuts = [cuts[0]] + [layout.to_row(cut, step) for step, cut in enumerate(cuts[1:], start=1)]
    chosen = []
    for steps in ((0,), tuple(range(1, layout.lowers))):
        chosen = call(
            functools.partial(choose_kernel, layout, steps),
            "choose",
            (corners, owners, *(cuts[step] for step in steps), *chosen),
            [(frames, 2, 2, strip, length)],
            scalar_count=2,
        )
    (chosen,) = chosen
    measured_parts = from_cores(part_measured)
    (roots,) = call(
        functools.partial(order_kernel, layout),
        "order",
        (measured, *measured_parts),
        [measured.shape],
        scratch=[(cores, layout.part, length)],
    )
    parts = from_uppers(chosen)
    held, roots = lax.optimization_barrier((chosen, roots))
    strips = list(parts)
    for step in range(1, cores):
        strips += [layout.from_core(part, step) for part in [held] + parts[1:]]
    every_probe = list(probes)
    for step in range(1, cores):
        every_probe += [layout.from_core(probe, step) for probe in probes]
    windows, pieces, old_pieces = call(
        functools.partial(first_kernel, layout),
        "first",
        (corners, *strips, *every_probe, roots, forward, back),
        [
            (frames, 2, length, length),
            (regions, 2 * local * piece + piece // halves, length),
            (halves, local, 2, piece, length),
        ],
        scratch=[
            (2, 2, cores, strip, length),
            (2, halves * local * length, length),
        ],
        scalar_count=1,
    )
    pieces = layout.within_cube(pieces)
    (total,) = call(sum_kernel, "sum", (pieces,), [pieces.shape[1:]])
    (spread,) = call(
        functools.partial(step_kernel, layout),
        "step",
        (old_pieces, *from_uppers(total)),
        [(regions, halves, local, 2, piece, length)],
    )
    new_probes = layout.within_cube(spread)
    (probe_out,) = call(
        functools.partial(probe_kernel, layout),
        "probe",
        (new_probes,),
        [(2, local, length, length)],
    )
    probe_power, intensity, fars = call(
        functools.partial(again_kernel, layout),
        "again",
        (new_probes, windows, forward, back),
        [
            (length, length),
            (frames, length, length),
            (frames, 2, halves * local * length, length),
        ],
    )
    strips = call(
        functools.partial(terms_kernel, layout),
        "terms",
        (corners, *from_cores(intensity), roots, new_probes, fars, forward, back),
        [(frames, 2, 2, strip, length)] * cores,
        scratch=[(2, 2, cores, strip, length)],
        scalar_count=1,
    )
    strips = [strips[0]] + [
        layout.from_core(sent, step) for step, sent in enumerate(strips[1:], start=1)
    ]
    posted = call(
        functools.partial(post_kernel, layout),
        "post",
        (corners, owners, *strips),
        [(2, strip, length)] * layout.lowers,
        scalar_count=2,
    )
    posted = [posted[0]] + [
        layout.to_row(sent, step) for step, sent in enumerate(posted[1:], start=1)
    ]
    (density,) = call(
        functools.partial(density_kernel, layout),
        "density",
        (corners, owners, *from_cores(probe_power)),
        [(strip, layout.width)],
        scratch=[(2, length, length), (strip, layout.width + lanes)],
        scalar_count=2,
    )
    (placed,) = call(
        functools.partial(place_kernel, layout),
        "place",
        (corners, owners, *posted),
        [(2, strip, layout.width)],
        scratch=[(2 * strip, layout.width + lanes)],
        scalar_count=2,
    )
    placed = [placed] + [layout.from_twin(placed, step) for step in range(1, halves)]
    (new_rows,) = call(
        functools.partial(update_kernel, layout),
        "update",
        (density, object_bands, *placed),
        [(2, strip, layout.width)],
    )
    (object_out,) = call(
        functools.partial(join_kernel, layout), "join", from_cores(new_rows), [object_bands.shape]
    )
    return probe_out, object_out


def solution(mesh):
    in_specs = (
        P("region", None, None),
        P(None, "mode", None, None),
        P(None, "region", None),
        P(),
        P(),
    )
    out_specs = (P(None, "mode", None, None), P(None, "region", None))
    return jax.shard_map(body, mesh=mesh, in_specs=in_specs, out_specs=out_specs, check_vma=False)
```

```python
import functools
import math

import jax
import jax.numpy as jnp
import ml_dtypes
import numpy as np
from jax import lax
from jax.experimental import pallas as pl
from jax.experimental.pallas import tpu as pltpu
from jax.sharding import PartitionSpec as P

intensity_offset = 0.1
probe_damping = 1.0
object_damping = 1.0
half = jnp.bfloat16
single = jnp.float32
axes = ("region", "mode")
lanes = 128
on_chip = pl.BlockSpec(memory_space=pltpu.VMEM)


class Layout:
    def __init__(self, regions, helpers, length, frames, modes, width):
        self.regions, self.helpers = regions, helpers
        self.length, self.frames, self.modes, self.width = length, frames, modes, width
        self.halves = 2 if regions % 2 == 0 and helpers % 2 == 0 else 1
        self.lowers, self.cores = regions // self.halves, helpers // self.halves
        self.local_modes = modes // helpers
        self.band = length // 2
        self.strip = self.band // self.cores
        self.paired = self.lowers & (self.lowers - 1) == 0
        self.piece = length // regions
        self.part = length // self.cores

    def place(self):
        region, helper = lax.axis_index("region"), lax.axis_index("mode")
        upper, lower = region // self.lowers, region % self.lowers
        twin, core = helper // self.cores, helper % self.cores
        return upper, lower, twin, core

    def device(self, upper, lower, twin, core):
        return (upper * self.lowers + lower) * self.helpers + twin * self.cores + core

    def everyone(self):
        for upper in range(self.halves):
            for lower in range(self.lowers):
                for twin in range(self.halves):
                    for core in range(self.cores):
                        yield upper, lower, twin, core

    def cubes(self):
        return [
            [
                self.device(upper, lower, twin, core)
                for twin in range(self.halves)
                for lower in range(self.lowers)
            ]
            for upper in range(self.halves)
            for core in range(self.cores)
        ]

    def from_upper(self, array, step):
        pairs = [
            (self.device((u + step) % self.halves, l, t, c), self.device(u, l, t, c))
            for u, l, t, c in self.everyone()
        ]
        return lax.ppermute(array, axes, pairs)

    def from_core(self, array, step):
        pairs = [
            (self.device(u, l, t, (c + step) % self.cores), self.device(u, l, t, c))
            for u, l, t, c in self.everyone()
        ]
        return lax.ppermute(array, axes, pairs)

    def from_twin(self, array, step):
        pairs = [
            (self.device(u, l, (t + step) % self.halves, c), self.device(u, l, t, c))
            for u, l, t, c in self.everyone()
        ]
        return lax.ppermute(array, axes, pairs)

    def across(self, lower, step):
        if self.paired:
            return lower ^ step
        return (lower + step) % self.lowers

    def to_row(self, array, step):
        pairs = [
            (self.device(u, l, t, c), self.device(u, self.across(l, step), t, c))
            for u, l, t, c in self.everyone()
        ]
        return lax.ppermute(array, axes, pairs)

    def within_cube(self, array):
        return lax.all_to_all(
            array, axes, split_axis=0, concat_axis=0, tiled=True, axis_index_groups=self.cubes()
        )


def fourier_tables(length):
    near = np.arange(length // 2)
    forms = []
    for odd in range(2):
        angles = near[:, None] * (2 * near[None, :] + odd) % length * (2.0 * math.pi / length)
        cosine, sine = np.cos(angles) / math.sqrt(length), np.sin(angles) / math.sqrt(length)
        forms.append(np.block([[cosine, -sine], [sine, cosine]]))
    forward = np.stack(forms)

    def pair(table):
        lead = table.astype(ml_dtypes.bfloat16)
        return np.stack([lead, (table - lead.astype(np.float64)).astype(ml_dtypes.bfloat16)])

    return pair(forward), pair(forward.swapaxes(1, 2))


def split(values):
    lead = values.astype(half)
    return lead, (values - lead.astype(single)).astype(half)


def dot(left, right):
    return jnp.dot(left, right, preferred_element_type=single)


def from_left(table, values):
    lead, trail = split(values)
    return dot(table[0], lead) + dot(table[1], lead) + dot(table[0], trail)


def from_right(values, table):
    lead, trail = split(values)
    return dot(lead, table[0]) + dot(lead, table[1]) + dot(trail, table[0])


def beside(left, right):
    return jnp.concatenate([left, right], axis=1)


def above(top, bottom):
    return jnp.concatenate([top, bottom], axis=0)


def table_of(tables, number):
    return tables[0, number], tables[1, number]


def columns_forward(real, imag, forward):
    middle = real.shape[1] // 2
    real_left, real_right = real[:, :middle], real[:, middle:]
    imag_left, imag_right = imag[:, :middle], imag[:, middle:]
    even = from_right(beside(real_left + real_right, imag_left + imag_right), table_of(forward, 0))
    odd = from_right(beside(real_left - real_right, imag_left - imag_right), table_of(forward, 1))
    return (
        beside(even[:, :middle], odd[:, :middle]),
        beside(even[:, middle:], odd[:, middle:]),
    )


def columns_back(real, imag, back):
    middle = real.shape[1] // 2
    even = from_right(beside(real[:, :middle], imag[:, :middle]), table_of(back, 0))
    odd = from_right(beside(real[:, middle:], imag[:, middle:]), table_of(back, 1))
    plus, minus = even + odd, even - odd
    return (
        beside(plus[:, :middle], minus[:, :middle]),
        beside(plus[:, middle:], minus[:, middle:]),
    )


def rows_forward(real, imag, back):
    middle = real.shape[0] // 2
    real_top, real_bottom = real[:middle], real[middle:]
    imag_top, imag_bottom = imag[:middle], imag[middle:]
    even = from_left(table_of(back, 0), above(real_top + real_bottom, imag_top + imag_bottom))
    odd = from_left(table_of(back, 1), above(real_top - real_bottom, imag_top - imag_bottom))
    return above(even[:middle], odd[:middle]), above(even[middle:], odd[middle:])


def rows_back(real, imag, forward):
    middle = real.shape[0] // 2
    even = from_left(table_of(forward, 0), above(real[:middle], imag[:middle]))
    odd = from_left(table_of(forward, 1), above(real[middle:], imag[middle:]))
    plus, minus = even + odd, even - odd
    return above(plus[:middle], minus[:middle]), above(plus[middle:], minus[middle:])


class Table:
    def __init__(self, ref):
        self.values = ref[...].astype(single)
        self.rows = lax.broadcasted_iota(jnp.int32, self.values.shape, 0)
        self.columns = lax.broadcasted_iota(jnp.int32, self.values.shape, 1)

    def __getitem__(self, place):
        row, column = place if isinstance(place, tuple) else (0, place)
        wanted = (self.rows == row) & (self.columns == column)
        return jnp.sum(jnp.where(wanted, self.values, 0.0)).astype(jnp.int32)


def band_of_block(owner, block, layout):
    band = jnp.int32(0)
    for candidate in range(layout.regions):
        band = jnp.where(owner[candidate] == block, candidate, band)
    return band


def frame_over(offsets, region, band, layout):
    row, column = offsets[0, region * layout.frames], offsets[1, region * layout.frames]
    for extra in range(1, layout.frames):
        index = region * layout.frames + extra
        anchor = offsets[0, index] // layout.band
        over = (anchor <= band) & (band <= anchor + 2)
        row = jnp.where(over, offsets[0, index], row)
        column = jnp.where(over, offsets[1, index], column)
    return row, column


def cut_kernel(layout, corners, owners, block, measured, *refs):
    outs, (sent, taken, offsets, owner, done) = refs[: layout.lowers], refs[layout.lowers :]
    upper, lower, twin, core = layout.place()
    strip = pl.ds(pl.multiple_of(core * layout.strip, layout.strip), layout.strip)
    part = pl.ds(pl.multiple_of(core * layout.part, layout.part), layout.part)
    copies = [
        pltpu.make_async_copy(corners, offsets, done.at[0]),
        pltpu.make_async_copy(owners, owner, done.at[1]),
        pltpu.make_async_copy(block.at[:, strip, :], taken.at[:, :, : layout.width], done.at[2]),
        pltpu.make_async_copy(measured.at[:, part, :], sent, done.at[3]),
    ]
    for copy in copies:
        copy.start()
    for copy in copies[:3]:
        copy.wait()
    band = band_of_block(owner, upper * layout.lowers + lower, layout)
    tiles = layout.length // lanes
    column_in_tile = lax.broadcasted_iota(jnp.int32, (2 * layout.strip, lanes), 1)
    for step, out in enumerate(outs):
        region = twin * layout.lowers + layout.across(lower, step)
        _, column = frame_over(offsets, region, band, layout)
        shift = column % lanes
        begin = pl.multiple_of(column - shift, lanes)
        kept = column_in_tile < lanes - shift
        turned = []
        for tile in range(tiles + 1):
            values = taken[:, :, pl.ds(begin + tile * lanes, lanes)].reshape(2 * layout.strip, lanes)
            turned.append(pltpu.roll(values, (lanes - shift) % lanes, 1))
        for tile in range(tiles):
            values = jnp.where(kept, turned[tile], turned[tile + 1])
            out[:, :, tile * lanes : (tile + 1) * lanes] = values.reshape(2, layout.strip, lanes)
    copies[3].wait()


def choose_kernel(layout, steps, offsets, owner, *refs):
    arrived, (*before, out) = refs[: len(steps)], refs[len(steps) :]
    upper, lower, twin, core = layout.place()
    rows = lax.broadcasted_iota(jnp.int32, (layout.strip, layout.length), 0) + core * layout.strip
    for frame in range(layout.frames):
        row = offsets[0, (twin * layout.lowers + lower) * layout.frames + frame]
        anchor = row // layout.band
        lead = row - anchor * layout.band
        blocks = [owner[anchor + step] for step in range(3)]
        masks = [rows >= lead, rows >= 0, rows < lead]
        for plane in range(2):
            slots = [ref[frame, plane] for ref in before]
            top, bottom = (slots[0][0], slots[0][1]) if before else (0.0, 0.0)
            for block, mask, slot in zip(blocks, masks, (0, 1, 0)):
                here = block // layout.lowers == upper
                values = top if slot == 0 else bottom
                for step, ref in zip(steps, arrived):
                    came = here & (layout.across(block % layout.lowers, step) == lower)
                    values = jnp.where(mask & came, ref[plane], values)
                top, bottom = (values, bottom) if slot == 0 else (top, values)
            out[frame, plane, 0] = top
            out[frame, plane, 1] = bottom


def side_by_side(stack, rows):
    return jnp.concatenate([stack[at : at + rows] for at in range(0, stack.shape[0], rows)], axis=1)


def one_above_another(row, columns):
    return jnp.concatenate([row[:, at : at + columns] for at in range(0, row.shape[1], columns)], axis=0)


def leave(probes, window_real, window_imag, forward, back):
    length = window_real.shape[0]
    wave = rows_forward(
        jnp.concatenate([real * window_real - imag * window_imag for real, imag in probes], axis=1),
        jnp.concatenate([real * window_imag + imag * window_real for real, imag in probes], axis=1),
        back,
    )
    return columns_forward(*(one_above_another(part, length) for part in wave), forward)


def come_back(far, factor, forward, back):
    length = factor.shape[0]
    factors = jnp.concatenate([factor] * (far.shape[1] // length), axis=0)
    wave = columns_back(far[0] * factors, far[1] * factors, back)
    return rows_back(*(side_by_side(part, length) for part in wave), forward)


def power_of(real, imag, length):
    power = real**2 + imag**2
    return sum(power[at : at + length] for at in range(length, power.shape[0], length)) + power[:length]


def order_kernel(layout, own_measured, *refs):
    parts, (out, other_measured) = refs[: layout.cores], refs[layout.cores :]
    upper, _, twin, core = layout.place()
    length = layout.length
    rows = lax.broadcasted_iota(jnp.int32, (length, length), 0)
    columns = lax.broadcasted_iota(jnp.int32, (length, length), 1)
    middle = length // 2
    pick_rows = (columns == jnp.where(rows < middle, 2 * rows, 2 * (rows - middle) + 1)).astype(half)
    pick_columns = (rows == jnp.where(columns < middle, 2 * columns, 2 * (columns - middle) + 1)).astype(half)

    def exact(product, values):
        lead, rest = split(values)
        trail = (values - lead.astype(single) - rest.astype(single)).astype(half)
        return (product(lead) + product(rest)) + product(trail)

    for frame in range(layout.frames):
        for step, part in enumerate(parts):
            other_measured[(core + step) % layout.cores] = part[frame]
        measured = other_measured[...].reshape(length, length)
        measured = jnp.sqrt(jnp.where(upper == twin, own_measured[frame], measured))
        measured = exact(lambda values: dot(pick_rows, values), measured)
        out[frame] = exact(lambda values: dot(values, pick_columns), measured)


def factor_of(root, intensity):
    return root / jnp.sqrt(intensity + intensity_offset) - 1.0


def first_kernel(layout, offsets, *refs):
    cores, halves, frames, length = layout.cores, layout.halves, layout.frames, layout.length
    count = cores * halves
    shares, probes, refs = refs[:count], refs[count : 2 * count], refs[2 * count :]
    roots, forward, back, windows, pieces, old_pieces, inner, far = refs
    upper, lower, twin, core = layout.place()
    region = twin * layout.lowers + lower
    local, piece = layout.local_modes, layout.piece
    rows = pl.ds(pl.multiple_of(region * piece, piece), piece)
    for entry, probe in enumerate(probes[:halves]):
        place = (twin + entry + halves - upper) % halves
        for k in range(local):
            for plane in range(2):
                old_pieces[place, k, plane] = probe[plane, k, rows, :]
    goes_back = (upper + halves - twin) % halves * local * length
    kept = pl.ds(pl.multiple_of(goes_back, length), local * length)
    cut = (layout.regions, piece, length)
    part = piece // halves
    for frame in range(frames):
        lead = offsets[0, region * frames + frame] % layout.band
        for step in range(cores):
            strip = shares[step * halves][frame]
            for entry in range(1, halves):
                strip += shares[step * halves + entry][frame]
            inner[:, :, (core + step) % cores] = strip
        for plane in range(2):
            wrapped = inner[plane].reshape(length, length)
            windows[frame, plane] = pltpu.roll(wrapped, (length - lead) % length, 0)
        window_real, window_imag = windows[frame, 0], windows[frame, 1]
        listed = [(probe[0, k], probe[1, k]) for probe in probes for k in range(local)]
        waves = leave(listed, window_real, window_imag, forward, back)
        for plane, wave in enumerate(waves):
            far[plane] = wave[: halves * local * length]
        factor = factor_of(roots[frame], power_of(*waves, length))
        changes_real, changes_imag = come_back(far[:, kept, :], factor, forward, back)
        channels = []
        for k in range(local):
            columns = slice(k * length, (k + 1) * length)
            change_real, change_imag = changes_real[:, columns], changes_imag[:, columns]
            channels.append(window_real * change_real + window_imag * change_imag)
            channels.append(window_real * change_imag - window_imag * change_real)
        channels = [values.reshape(cut) for values in channels]
        power = (window_real**2 + window_imag**2).reshape(cut)
        sent = power[:, :part]
        for other in range(1, halves):
            sent = jnp.where(upper == other, power[:, other * part : (other + 1) * part], sent)
        first = 0
        for values in (*channels, sent):
            taken = slice(first, first + values.shape[1])
            if frame == 0:
                pieces[:, taken] = values
            else:
                pieces[:, taken] += values
            first += values.shape[1]


def sum_kernel(arrived, total):
    total[...] = jnp.sum(arrived[...], axis=0)


def step_kernel(layout, old_pieces, *refs):
    totals, out = refs[:-1], refs[-1]
    upper, _, _, _ = layout.place()
    halves, piece = layout.halves, layout.piece
    planes = 2 * layout.local_modes
    parts = []
    for place in range(halves):
        power = totals[0][planes * piece :]
        for entry in range(1, halves):
            power = jnp.where((upper + entry) % halves == place, totals[entry][planes * piece :], power)
        parts.append(power)
    damped = jnp.concatenate(parts, axis=0) + probe_damping
    for entry, total in enumerate(totals):
        for local in range(layout.local_modes):
            for plane in range(2):
                first = (2 * local + plane) * piece
                stepped = old_pieces[entry, local, plane] + total[first : first + piece] / damped
                for region in range(layout.regions):
                    out[region, entry, local, plane] = stepped


def new_probe(probes, entry, local, plane):
    values = probes[:, entry, local, plane]
    return values.reshape(values.shape[0] * values.shape[1], values.shape[2])


def probe_kernel(layout, probes, out):
    upper, _, twin, _ = layout.place()
    entry = (twin + layout.halves - upper) % layout.halves
    for local in range(layout.local_modes):
        for plane in range(2):
            out[plane, local] = new_probe(probes, entry, local, plane)


def again_kernel(layout, probes, windows, forward, back, probe_power, intensity, fars):
    listed = [
        [new_probe(probes, entry, local, plane) for plane in range(2)]
        for entry in range(layout.halves)
        for local in range(layout.local_modes)
    ]
    for frame in range(layout.frames):
        waves = leave(listed, windows[frame, 0], windows[frame, 1], forward, back)
        intensity[frame] = power_of(*waves, layout.length)
        for plane, wave in enumerate(waves):
            fars[frame, plane] = wave
    probe_power[...] = sum(real**2 + imag**2 for real, imag in listed)


def terms_kernel(layout, offsets, *refs):
    cores, halves, frames, length = layout.cores, layout.halves, layout.frames, layout.length
    intensities = refs[:cores]
    roots, probes, fars, forward, back, *strips, inner = refs[cores:]
    upper, lower, twin, core = layout.place()
    region = twin * layout.lowers + lower
    for frame in range(frames):
        intensity = intensities[0][frame]
        for more in intensities[1:]:
            intensity += more[frame]
        factor = factor_of(roots[frame], intensity)
        changes_real, changes_imag = come_back(fars[frame], factor, forward, back)
        numer_real = jnp.zeros((length, length), single)
        numer_imag = jnp.zeros((length, length), single)
        for entry in range(halves):
            for local in range(layout.local_modes):
                first = (entry * layout.local_modes + local) * length
                change_real = changes_real[:, first : first + length]
                change_imag = changes_imag[:, first : first + length]
                probe_real, probe_imag = (new_probe(probes, entry, local, plane) for plane in range(2))
                numer_real += probe_real * change_real + probe_imag * change_imag
                numer_imag += probe_real * change_imag - probe_imag * change_real
        lead = offsets[0, region * frames + frame] % layout.band
        for plane, values in enumerate((numer_real, numer_imag)):
            inner[plane] = pltpu.roll(values, lead, 0).reshape(2, cores, layout.strip, length)
        for step, strip in enumerate(strips):
            strip[frame] = inner[:, :, (core + cores - step) % cores]


def post_kernel(layout, offsets, owner, *refs):
    strips, outs = refs[: layout.cores], refs[layout.cores :]
    upper, lower, twin, _ = layout.place()
    region = twin * layout.lowers + lower
    for step, out in enumerate(outs):
        block = upper * layout.lowers + layout.across(lower, step)
        band = band_of_block(owner, block, layout)
        frame, row = jnp.int32(0), offsets[0, region * layout.frames]
        for extra in range(1, layout.frames):
            candidate = offsets[0, region * layout.frames + extra]
            anchor = candidate // layout.band
            over = (anchor <= band) & (band <= anchor + 2)
            frame, row = jnp.where(over, extra, frame), jnp.where(over, candidate, row)
        slot = (band - row // layout.band == 1).astype(jnp.int32)
        for plane in range(2):
            total = strips[0][frame, plane, slot]
            for strip in strips[1:]:
                total += strip[frame, plane, slot]
            out[plane] = total


class Cover:
    def __init__(self, layout, offsets, region, band, core):
        row, self.column = frame_over(offsets, region, band, layout)
        anchor = row // layout.band
        self.lead = row - anchor * layout.band
        self.step = band - anchor
        self.first = core * layout.strip
        self.layout = layout

    def inside(self):
        band = self.layout.band
        middle = (self.step == 1) | (self.step == 2)
        begin = jnp.where(self.step == 0, self.lead, jnp.where(middle, 0, band))
        end = jnp.where(self.step == 2, self.lead, band)
        shape = (self.layout.strip, self.layout.length)
        rows = lax.broadcasted_iota(jnp.int32, shape, 0) + self.first
        return (rows >= begin) & (rows < end)

    def start(self):
        slot = (self.step == 1).astype(jnp.int32)
        length = self.layout.length
        return (slot * self.layout.band + self.first + length - self.lead) % length

    def add(self, total, terms):
        tiles = self.layout.length // lanes
        shift = self.column % lanes
        begin = pl.multiple_of(self.column - shift, lanes)
        spilled = lax.broadcasted_iota(jnp.int32, (terms.shape[0], lanes), 1) < shift
        turned = [
            pltpu.roll(terms[:, tile * lanes : (tile + 1) * lanes], shift, 1) for tile in range(tiles)
        ]
        for tile in range(tiles + 1):
            near = turned[tile] if tile < tiles else 0.0
            over = turned[tile - 1] if tile else 0.0
            total[:, pl.ds(begin + tile * lanes, lanes)] += jnp.where(spilled, over, near)


def density_kernel(layout, offsets, owner, *refs):
    powers, (out, doubled, total) = refs[: layout.cores], refs[layout.cores :]
    upper, lower, _, core = layout.place()
    strip, length = layout.strip, layout.length
    band = band_of_block(owner, upper * layout.lowers + lower, layout)
    power = powers[0][...]
    for more in powers[1:]:
        power += more[...]
    doubled[:length] = power
    doubled[length:] = power
    total[...] = jnp.zeros_like(total)
    for region in range(layout.regions):
        cover = Cover(layout, offsets, region, band, core)
        start = cover.start()
        near = doubled[pl.ds(pl.multiple_of(start // 8 * 8, 8), strip + 8), :]
        near = pltpu.roll(near, (strip + 8 - start % 8) % (strip + 8), 0)[:strip]
        cover.add(total, jnp.where(cover.inside(), near, 0.0))
    out[...] = total[:, : layout.width] + object_damping


def place_kernel(layout, offsets, owner, *refs):
    arrived, (out, total) = refs[: layout.lowers], refs[layout.lowers :]
    upper, lower, twin, core = layout.place()
    strip = layout.strip
    band = band_of_block(owner, upper * layout.lowers + lower, layout)
    total[...] = jnp.zeros_like(total)
    for step, terms in enumerate(arrived):
        source = layout.across(lower, step if layout.paired else layout.lowers - step)
        cover = Cover(layout, offsets, twin * layout.lowers + source, band, core)
        inside = cover.inside()
        kept = [jnp.where(inside, terms[plane], 0.0) for plane in range(2)]
        cover.add(total, jnp.concatenate(kept, axis=0))
    for plane in range(2):
        out[plane] = total[plane * strip : (plane + 1) * strip, : layout.width]


def update_kernel(layout, density, block, *refs):
    placed, out = refs[:-1], refs[-1]
    _, _, _, core = layout.place()
    rows = pl.ds(pl.multiple_of(core * layout.strip, layout.strip), layout.strip)
    for plane in range(2):
        total = placed[0][plane]
        for more in placed[1:]:
            total += more[plane]
        out[plane] = block[plane, rows, :] + total / density[...]


def join_kernel(layout, *refs):
    strips, out = refs[:-1], refs[-1]
    _, _, _, core = layout.place()
    for step, strip in enumerate(strips):
        first = (core + step) % layout.cores * layout.strip
        out[:, pl.ds(pl.multiple_of(first, layout.strip), layout.strip), :] = strip[...]


def call(kernel, name, operands, outputs, scratch=(), scalar_count=0, after=()):
    shapes = [jax.ShapeDtypeStruct(shape, single) for shape in outputs]
    count = len(operands)

    def inner(*refs):
        tables = [Table(ref) for ref in refs[:scalar_count]]
        kernel(*tables, *refs[scalar_count:count], *refs[count + len(after) :])

    return pl.pallas_call(
        inner,
        name=name,
        out_shape=shapes,
        in_specs=[on_chip] * count
        + [pl.BlockSpec(memory_space=pl.ANY)] * len(after),
        out_specs=[on_chip] * len(shapes),
        scratch_shapes=[pltpu.VMEM(shape, single) for shape in scratch],
        compiler_params=pltpu.CompilerParams(vmem_limit_bytes=28 * 2**20),
    )(*operands, *after)


def body(measured, probe_modes, object_bands, scan_offsets, band_owner):
    layout = Layout(
        lax.axis_size("region"),
        lax.axis_size("mode"),
        measured.shape[1],
        measured.shape[0],
        probe_modes.shape[1] * lax.axis_size("mode"),
        object_bands.shape[2],
    )
    regions, halves, cores = layout.regions, layout.halves, layout.cores
    length, piece, frames = layout.length, layout.piece, layout.frames
    local, strip = layout.local_modes, layout.strip
    forward, back = fourier_tables(length)
    corners, owners = scan_offsets.T, band_owner[None]

    def from_cores(array):
        return [array] + [layout.from_core(array, step) for step in range(1, cores)]

    def from_uppers(array):
        return [array] + [layout.from_upper(array, step) for step in range(1, halves)]

    *cuts, part_measured = pl.pallas_call(
        functools.partial(cut_kernel, layout),
        name="cut",
        out_shape=[jax.ShapeDtypeStruct((2, strip, length), single)] * layout.lowers
        + [jax.ShapeDtypeStruct((frames, layout.part, length), single)],
        in_specs=[pl.BlockSpec(memory_space=pltpu.HBM)] * 4,
        out_specs=[on_chip] * (layout.lowers + 1),
        scratch_shapes=[
            pltpu.VMEM((2, strip, layout.width + lanes), single),
            pltpu.SMEM(corners.shape, jnp.int32),
            pltpu.SMEM(band_owner.shape, jnp.int32),
            pltpu.SemaphoreType.DMA((4,)),
        ],
        compiler_params=pltpu.CompilerParams(vmem_limit_bytes=28 * 2**20),
    )(
        *(
            pltpu.with_memory_space_constraint(array, pltpu.HBM)
            for array in (corners, band_owner, object_bands, measured)
        )
    )
    part_measured, held_probes = lax.optimization_barrier((part_measured, probe_modes))
    probes = [probe_modes] + [layout.from_twin(held_probes, step) for step in range(1, halves)]
    if halves > 1:
        pairs = [
            (layout.device(t, l, t, c), layout.device(u, l, t, c))
            for u, l, t, c in layout.everyone()
            if u != t
        ]
        part_measured = lax.ppermute(part_measured, axes, pairs)
    cuts = [cuts[0]] + [layout.to_row(cut, step) for step, cut in enumerate(cuts[1:], start=1)]
    chosen = []
    for steps in ((0,), tuple(range(1, layout.lowers))):
        chosen = call(
            functools.partial(choose_kernel, layout, steps),
            "choose",
            (corners, owners, *(cuts[step] for step in steps), *chosen),
            [(frames, 2, 2, strip, length)],
            scalar_count=2,
        )
    (chosen,) = chosen
    measured_parts = from_cores(part_measured)
    (roots,) = call(
        functools.partial(order_kernel, layout),
        "order",
        (measured, *measured_parts),
        [measured.shape],
        scratch=[(cores, layout.part, length)],
    )
    parts = from_uppers(chosen)
    held, roots = lax.optimization_barrier((chosen, roots))
    strips = list(parts)
    for step in range(1, cores):
        strips += [layout.from_core(part, step) for part in [held] + parts[1:]]
    every_probe = list(probes)
    for step in range(1, cores):
        every_probe += [layout.from_core(probe, step) for probe in probes]
    windows, pieces, old_pieces = call(
        functools.partial(first_kernel, layout),
        "first",
        (corners, *strips, *every_probe, roots, forward, back),
        [
            (frames, 2, length, length),
            (regions, 2 * local * piece + piece // halves, length),
            (halves, local, 2, piece, length),
        ],
        scratch=[
            (2, 2, cores, strip, length),
            (2, halves * local * length, length),
        ],
        scalar_count=1,
    )
    pieces = layout.within_cube(pieces)
    (total,) = call(sum_kernel, "sum", (pieces,), [pieces.shape[1:]])
    (spread,) = call(
        functools.partial(step_kernel, layout),
        "step",
        (old_pieces, *from_uppers(total)),
        [(regions, halves, local, 2, piece, length)],
    )
    new_probes = layout.within_cube(spread)
    (probe_out,) = call(
        functools.partial(probe_kernel, layout),
        "probe",
        (new_probes,),
        [(2, local, length, length)],
    )
    probe_power, intensity, fars = call(
        functools.partial(again_kernel, layout),
        "again",
        (new_probes, windows, forward, back),
        [
            (length, length),
            (frames, length, length),
            (frames, 2, halves * local * length, length),
        ],
    )
    strips = call(
        functools.partial(terms_kernel, layout),
        "terms",
        (corners, *from_cores(intensity), roots, new_probes, fars, forward, back),
        [(frames, 2, 2, strip, length)] * cores,
        scratch=[(2, 2, cores, strip, length)],
        scalar_count=1,
    )
    strips = [strips[0]] + [
        layout.from_core(sent, step) for step, sent in enumerate(strips[1:], start=1)
    ]
    posted = call(
        functools.partial(post_kernel, layout),
        "post",
        (corners, owners, *strips),
        [(2, strip, length)] * layout.lowers,
        scalar_count=2,
    )
    posted = [posted[0]] + [
        layout.to_row(sent, step) for step, sent in enumerate(posted[1:], start=1)
    ]
    (density,) = call(
        functools.partial(density_kernel, layout),
        "density",
        (corners, owners, *from_cores(probe_power)),
        [(strip, layout.width)],
        scratch=[(2 * length, length), (strip, layout.width + lanes)],
        scalar_count=2,
    )
    (placed,) = call(
        functools.partial(place_kernel, layout),
        "place",
        (corners, owners, *posted),
        [(2, strip, layout.width)],
        scratch=[(2 * strip, layout.width + lanes)],
        scalar_count=2,
    )
    placed = [placed] + [layout.from_twin(placed, step) for step in range(1, halves)]
    (new_rows,) = call(
        functools.partial(update_kernel, layout),
        "update",
        (density, object_bands, *placed),
        [(2, strip, layout.width)],
    )
    (object_out,) = call(
        functools.partial(join_kernel, layout), "join", from_cores(new_rows), [object_bands.shape]
    )
    return probe_out, object_out


def solution(mesh):
    in_specs = (
        P("region", None, None),
        P(None, "mode", None, None),
        P(None, "region", None),
        P(),
        P(),
    )
    out_specs = (P(None, "mode", None, None), P(None, "region", None))
    return jax.shard_map(body, mesh=mesh, in_specs=in_specs, out_specs=out_specs, check_vma=False)
```

```python
import functools
import math

import jax
import jax.numpy as jnp
import ml_dtypes
import numpy as np
from jax import lax
from jax.experimental import pallas as pl
from jax.experimental.pallas import tpu as pltpu
from jax.sharding import PartitionSpec as P

intensity_offset = 0.1
probe_damping = 1.0
object_damping = 1.0
half = jnp.bfloat16
single = jnp.float32
axes = ("region", "mode")
lanes = 128
on_chip = pl.BlockSpec(memory_space=pltpu.VMEM)


class Layout:
    def __init__(self, regions, helpers, length, frames, modes, width):
        self.regions, self.helpers = regions, helpers
        self.length, self.frames, self.modes, self.width = length, frames, modes, width
        self.halves = 2 if regions % 2 == 0 and helpers % 2 == 0 else 1
        self.lowers, self.cores = regions // self.halves, helpers // self.halves
        self.local_modes = modes // helpers
        self.band = length // 2
        self.strip = self.band // self.cores
        self.paired = self.lowers & (self.lowers - 1) == 0
        self.piece = length // regions
        self.part = length // self.cores

    def place(self):
        region, helper = lax.axis_index("region"), lax.axis_index("mode")
        upper, lower = region // self.lowers, region % self.lowers
        twin, core = helper // self.cores, helper % self.cores
        return upper, lower, twin, core

    def device(self, upper, lower, twin, core):
        return (upper * self.lowers + lower) * self.helpers + twin * self.cores + core

    def everyone(self):
        for upper in range(self.halves):
            for lower in range(self.lowers):
                for twin in range(self.halves):
                    for core in range(self.cores):
                        yield upper, lower, twin, core

    def cubes(self):
        return [
            [
                self.device(upper, lower, twin, core)
                for twin in range(self.halves)
                for lower in range(self.lowers)
            ]
            for upper in range(self.halves)
            for core in range(self.cores)
        ]

    def from_upper(self, array, step):
        pairs = [
            (self.device((u + step) % self.halves, l, t, c), self.device(u, l, t, c))
            for u, l, t, c in self.everyone()
        ]
        return lax.ppermute(array, axes, pairs)

    def from_core(self, array, step):
        pairs = [
            (self.device(u, l, t, (c + step) % self.cores), self.device(u, l, t, c))
            for u, l, t, c in self.everyone()
        ]
        return lax.ppermute(array, axes, pairs)

    def from_twin(self, array, step):
        pairs = [
            (self.device(u, l, (t + step) % self.halves, c), self.device(u, l, t, c))
            for u, l, t, c in self.everyone()
        ]
        return lax.ppermute(array, axes, pairs)

    def across(self, lower, step):
        if self.paired:
            return lower ^ step
        return (lower + step) % self.lowers

    def to_row(self, array, step):
        pairs = [
            (self.device(u, l, t, c), self.device(u, self.across(l, step), t, c))
            for u, l, t, c in self.everyone()
        ]
        return lax.ppermute(array, axes, pairs)

    def within_cube(self, array):
        return lax.all_to_all(
            array, axes, split_axis=0, concat_axis=0, tiled=True, axis_index_groups=self.cubes()
        )


def fourier_tables(length):
    near = np.arange(length // 2)
    forms = []
    for odd in range(2):
        angles = near[:, None] * (2 * near[None, :] + odd) % length * (2.0 * math.pi / length)
        cosine, sine = np.cos(angles) / math.sqrt(length), np.sin(angles) / math.sqrt(length)
        forms.append(np.block([[cosine, -sine], [sine, cosine]]))
    forward = np.stack(forms)

    def pair(table):
        lead = table.astype(ml_dtypes.bfloat16)
        return np.stack([lead, (table - lead.astype(np.float64)).astype(ml_dtypes.bfloat16)])

    return pair(forward), pair(forward.swapaxes(1, 2))


def split(values):
    lead = values.astype(half)
    return lead, (values - lead.astype(single)).astype(half)


def dot(left, right):
    return jnp.dot(left, right, preferred_element_type=single)


def from_left(table, values):
    lead, trail = split(values)
    return dot(table[0], lead) + dot(table[1], lead) + dot(table[0], trail)


def from_right(values, table):
    lead, trail = split(values)
    return dot(lead, table[0]) + dot(lead, table[1]) + dot(trail, table[0])


def beside(left, right):
    return jnp.concatenate([left, right], axis=1)


def above(top, bottom):
    return jnp.concatenate([top, bottom], axis=0)


def table_of(tables, number):
    return tables[0, number], tables[1, number]


def columns_forward(real, imag, forward):
    middle = real.shape[1] // 2
    real_left, real_right = real[:, :middle], real[:, middle:]
    imag_left, imag_right = imag[:, :middle], imag[:, middle:]
    even = from_right(beside(real_left + real_right, imag_left + imag_right), table_of(forward, 0))
    odd = from_right(beside(real_left - real_right, imag_left - imag_right), table_of(forward, 1))
    return (
        beside(even[:, :middle], odd[:, :middle]),
        beside(even[:, middle:], odd[:, middle:]),
    )


def columns_back(real, imag, back):
    middle = real.shape[1] // 2
    even = from_right(beside(real[:, :middle], imag[:, :middle]), table_of(back, 0))
    odd = from_right(beside(real[:, middle:], imag[:, middle:]), table_of(back, 1))
    plus, minus = even + odd, even - odd
    return (
        beside(plus[:, :middle], minus[:, :middle]),
        beside(plus[:, middle:], minus[:, middle:]),
    )


def rows_forward(real, imag, back):
    middle = real.shape[0] // 2
    real_top, real_bottom = real[:middle], real[middle:]
    imag_top, imag_bottom = imag[:middle], imag[middle:]
    even = from_left(table_of(back, 0), above(real_top + real_bottom, imag_top + imag_bottom))
    odd = from_left(table_of(back, 1), above(real_top - real_bottom, imag_top - imag_bottom))
    return above(even[:middle], odd[:middle]), above(even[middle:], odd[middle:])


def rows_back(real, imag, forward):
    middle = real.shape[0] // 2
    even = from_left(table_of(forward, 0), above(real[:middle], imag[:middle]))
    odd = from_left(table_of(forward, 1), above(real[middle:], imag[middle:]))
    plus, minus = even + odd, even - odd
    return above(plus[:middle], minus[:middle]), above(plus[middle:], minus[middle:])


class Table:
    def __init__(self, ref):
        self.values = ref[...].astype(single)
        self.rows = lax.broadcasted_iota(jnp.int32, self.values.shape, 0)
        self.columns = lax.broadcasted_iota(jnp.int32, self.values.shape, 1)

    def __getitem__(self, place):
        row, column = place if isinstance(place, tuple) else (0, place)
        wanted = (self.rows == row) & (self.columns == column)
        return jnp.sum(jnp.where(wanted, self.values, 0.0)).astype(jnp.int32)


def band_of_block(owner, block, layout):
    band = jnp.int32(0)
    for candidate in range(layout.regions):
        band = jnp.where(owner[candidate] == block, candidate, band)
    return band


def frame_over(offsets, region, band, layout):
    row, column = offsets[0, region * layout.frames], offsets[1, region * layout.frames]
    for extra in range(1, layout.frames):
        index = region * layout.frames + extra
        anchor = offsets[0, index] // layout.band
        over = (anchor <= band) & (band <= anchor + 2)
        row = jnp.where(over, offsets[0, index], row)
        column = jnp.where(over, offsets[1, index], column)
    return row, column


def cut_kernel(layout, corners, owners, block, measured, *refs):
    outs, (sent, taken, offsets, owner, done) = refs[: layout.lowers], refs[layout.lowers :]
    upper, lower, twin, core = layout.place()
    strip = pl.ds(pl.multiple_of(core * layout.strip, layout.strip), layout.strip)
    part = pl.ds(pl.multiple_of(core * layout.part, layout.part), layout.part)
    copies = [
        pltpu.make_async_copy(corners, offsets, done.at[0]),
        pltpu.make_async_copy(owners, owner, done.at[1]),
        pltpu.make_async_copy(block.at[:, strip, :], taken.at[:, :, : layout.width], done.at[2]),
        pltpu.make_async_copy(measured.at[:, part, :], sent, done.at[3]),
    ]
    for copy in copies:
        copy.start()
    for copy in copies[:3]:
        copy.wait()
    band = band_of_block(owner, upper * layout.lowers + lower, layout)
    tiles = layout.length // lanes
    column_in_tile = lax.broadcasted_iota(jnp.int32, (2 * layout.strip, lanes), 1)
    for step, out in enumerate(outs):
        region = twin * layout.lowers + layout.across(lower, step)
        _, column = frame_over(offsets, region, band, layout)
        shift = column % lanes
        begin = pl.multiple_of(column - shift, lanes)
        kept = column_in_tile < lanes - shift
        turned = []
        for tile in range(tiles + 1):
            values = taken[:, :, pl.ds(begin + tile * lanes, lanes)].reshape(2 * layout.strip, lanes)
            turned.append(pltpu.roll(values, (lanes - shift) % lanes, 1))
        for tile in range(tiles):
            values = jnp.where(kept, turned[tile], turned[tile + 1])
            out[:, :, tile * lanes : (tile + 1) * lanes] = values.reshape(2, layout.strip, lanes)
    copies[3].wait()


def choose_kernel(layout, steps, offsets, owner, *refs):
    arrived, (*before, out) = refs[: len(steps)], refs[len(steps) :]
    upper, lower, twin, core = layout.place()
    rows = lax.broadcasted_iota(jnp.int32, (layout.strip, layout.length), 0) + core * layout.strip
    for frame in range(layout.frames):
        row = offsets[0, (twin * layout.lowers + lower) * layout.frames + frame]
        anchor = row // layout.band
        lead = row - anchor * layout.band
        blocks = [owner[anchor + step] for step in range(3)]
        masks = [rows >= lead, rows >= 0, rows < lead]
        for plane in range(2):
            slots = [ref[frame, plane] for ref in before]
            top, bottom = (slots[0][0], slots[0][1]) if before else (0.0, 0.0)
            for block, mask, slot in zip(blocks, masks, (0, 1, 0)):
                here = block // layout.lowers == upper
                values = top if slot == 0 else bottom
                for step, ref in zip(steps, arrived):
                    came = here & (layout.across(block % layout.lowers, step) == lower)
                    values = jnp.where(mask & came, ref[plane], values)
                top, bottom = (values, bottom) if slot == 0 else (top, values)
            out[frame, plane, 0] = top
            out[frame, plane, 1] = bottom


def side_by_side(stack, rows):
    return jnp.concatenate([stack[at : at + rows] for at in range(0, stack.shape[0], rows)], axis=1)


def one_above_another(row, columns):
    return jnp.concatenate([row[:, at : at + columns] for at in range(0, row.shape[1], columns)], axis=0)


def leave(probes, window_real, window_imag, forward, back):
    length = window_real.shape[0]
    wave = rows_forward(
        jnp.concatenate([real * window_real - imag * window_imag for real, imag in probes], axis=1),
        jnp.concatenate([real * window_imag + imag * window_real for real, imag in probes], axis=1),
        back,
    )
    return columns_forward(*(one_above_another(part, length) for part in wave), forward)


def come_back(far, factor, forward, back):
    length = factor.shape[0]
    factors = jnp.concatenate([factor] * (far.shape[1] // length), axis=0)
    wave = columns_back(far[0] * factors, far[1] * factors, back)
    return rows_back(*(side_by_side(part, length) for part in wave), forward)


def power_of(real, imag, length):
    power = real**2 + imag**2
    return sum(power[at : at + length] for at in range(length, power.shape[0], length)) + power[:length]


def order_kernel(layout, own_measured, *refs):
    parts, (out, other_measured) = refs[: layout.cores], refs[layout.cores :]
    upper, _, twin, core = layout.place()
    length = layout.length
    rows = lax.broadcasted_iota(jnp.int32, (length, length), 0)
    columns = lax.broadcasted_iota(jnp.int32, (length, length), 1)
    middle = length // 2
    pick_rows = (columns == jnp.where(rows < middle, 2 * rows, 2 * (rows - middle) + 1)).astype(half)
    pick_columns = (rows == jnp.where(columns < middle, 2 * columns, 2 * (columns - middle) + 1)).astype(half)

    def exact(product, values):
        lead, rest = split(values)
        trail = (values - lead.astype(single) - rest.astype(single)).astype(half)
        return (product(lead) + product(rest)) + product(trail)

    for frame in range(layout.frames):
        for step, part in enumerate(parts):
            other_measured[(core + step) % layout.cores] = part[frame]
        measured = other_measured[...].reshape(length, length)
        measured = jnp.sqrt(jnp.where(upper == twin, own_measured[frame], measured))
        measured = exact(lambda values: dot(pick_rows, values), measured)
        out[frame] = exact(lambda values: dot(values, pick_columns), measured)


def factor_of(root, intensity):
    return root / jnp.sqrt(intensity + intensity_offset) - 1.0


def first_kernel(layout, offsets, *refs):
    cores, halves, frames, length = layout.cores, layout.halves, layout.frames, layout.length
    count = cores * halves
    shares, probes, refs = refs[:count], refs[count : 2 * count], refs[2 * count :]
    roots, forward, back, windows, pieces, old_pieces, inner, far = refs
    upper, lower, twin, core = layout.place()
    region = twin * layout.lowers + lower
    local, piece = layout.local_modes, layout.piece
    rows = pl.ds(pl.multiple_of(region * piece, piece), piece)
    for entry, probe in enumerate(probes[:halves]):
        place = (twin + entry + halves - upper) % halves
        for k in range(local):
            for plane in range(2):
                old_pieces[place, k, plane] = probe[plane, k, rows, :]
    goes_back = (upper + halves - twin) % halves * local * length
    kept = pl.ds(pl.multiple_of(goes_back, length), local * length)
    cut = (layout.regions, piece, length)
    part = piece // halves
    for frame in range(frames):
        lead = offsets[0, region * frames + frame] % layout.band
        for step in range(cores):
            strip = shares[step * halves][frame]
            for entry in range(1, halves):
                strip += shares[step * halves + entry][frame]
            inner[:, :, (core + step) % cores] = strip
        for plane in range(2):
            wrapped = inner[plane].reshape(length, length)
            windows[frame, plane] = pltpu.roll(wrapped, (length - lead) % length, 0)
        window_real, window_imag = windows[frame, 0], windows[frame, 1]
        listed = [(probe[0, k], probe[1, k]) for probe in probes for k in range(local)]
        waves = leave(listed, window_real, window_imag, forward, back)
        for plane, wave in enumerate(waves):
            far[plane] = wave[: halves * local * length]
        factor = factor_of(roots[frame], power_of(*waves, length))
        changes_real, changes_imag = come_back(far[:, kept, :], factor, forward, back)
        channels = []
        for k in range(local):
            columns = slice(k * length, (k + 1) * length)
            change_real, change_imag = changes_real[:, columns], changes_imag[:, columns]
            channels.append(window_real * change_real + window_imag * change_imag)
            channels.append(window_real * change_imag - window_imag * change_real)
        channels = [values.reshape(cut) for values in channels]
        power = (window_real**2 + window_imag**2).reshape(cut)
        sent = power[:, :part]
        for other in range(1, halves):
            sent = jnp.where(upper == other, power[:, other * part : (other + 1) * part], sent)
        first = 0
        for values in (*channels, sent):
            taken = slice(first, first + values.shape[1])
            if frame == 0:
                pieces[:, taken] = values
            else:
                pieces[:, taken] += values
            first += values.shape[1]


def sum_kernel(arrived, total):
    total[...] = jnp.sum(arrived[...], axis=0)


def step_kernel(layout, old_pieces, *refs):
    totals, out = refs[:-1], refs[-1]
    upper, _, _, _ = layout.place()
    halves, piece = layout.halves, layout.piece
    planes = 2 * layout.local_modes
    parts = []
    for place in range(halves):
        power = totals[0][planes * piece :]
        for entry in range(1, halves):
            power = jnp.where((upper + entry) % halves == place, totals[entry][planes * piece :], power)
        parts.append(power)
    damped = jnp.concatenate(parts, axis=0) + probe_damping
    for entry, total in enumerate(totals):
        for local in range(layout.local_modes):
            for plane in range(2):
                first = (2 * local + plane) * piece
                stepped = old_pieces[entry, local, plane] + total[first : first + piece] / damped
                for region in range(layout.regions):
                    out[region, entry, local, plane] = stepped


def new_probe(probes, entry, local, plane):
    values = probes[:, entry, local, plane]
    return values.reshape(values.shape[0] * values.shape[1], values.shape[2])


def probe_kernel(layout, probes, out):
    upper, _, twin, _ = layout.place()
    entry = (twin + layout.halves - upper) % layout.halves
    for local in range(layout.local_modes):
        for plane in range(2):
            out[plane, local] = new_probe(probes, entry, local, plane)


def again_kernel(layout, probes, windows, forward, back, probe_power, intensity, fars):
    listed = [
        [new_probe(probes, entry, local, plane) for plane in range(2)]
        for entry in range(layout.halves)
        for local in range(layout.local_modes)
    ]
    for frame in range(layout.frames):
        waves = leave(listed, windows[frame, 0], windows[frame, 1], forward, back)
        intensity[frame] = power_of(*waves, layout.length)
        for plane, wave in enumerate(waves):
            fars[frame, plane] = wave
    probe_power[...] = sum(real**2 + imag**2 for real, imag in listed)


def terms_kernel(layout, offsets, *refs):
    cores, halves, frames, length = layout.cores, layout.halves, layout.frames, layout.length
    intensities = refs[:cores]
    roots, probes, fars, forward, back, *strips, inner = refs[cores:]
    upper, lower, twin, core = layout.place()
    region = twin * layout.lowers + lower
    for frame in range(frames):
        intensity = intensities[0][frame]
        for more in intensities[1:]:
            intensity += more[frame]
        factor = factor_of(roots[frame], intensity)
        changes_real, changes_imag = come_back(fars[frame], factor, forward, back)
        numer_real = jnp.zeros((length, length), single)
        numer_imag = jnp.zeros((length, length), single)
        for entry in range(halves):
            for local in range(layout.local_modes):
                first = (entry * layout.local_modes + local) * length
                change_real = changes_real[:, first : first + length]
                change_imag = changes_imag[:, first : first + length]
                probe_real, probe_imag = (new_probe(probes, entry, local, plane) for plane in range(2))
                numer_real += probe_real * change_real + probe_imag * change_imag
                numer_imag += probe_real * change_imag - probe_imag * change_real
        lead = offsets[0, region * frames + frame] % layout.band
        for plane, values in enumerate((numer_real, numer_imag)):
            inner[plane] = pltpu.roll(values, lead, 0).reshape(2, cores, layout.strip, length)
        for step, strip in enumerate(strips):
            strip[frame] = inner[:, :, (core + cores - step) % cores]


def post_kernel(layout, offsets, owner, *refs):
    strips, outs = refs[: layout.cores], refs[layout.cores :]
    upper, lower, twin, _ = layout.place()
    region = twin * layout.lowers + lower
    for step, out in enumerate(outs):
        block = upper * layout.lowers + layout.across(lower, step)
        band = band_of_block(owner, block, layout)
        frame, row = jnp.int32(0), offsets[0, region * layout.frames]
        for extra in range(1, layout.frames):
            candidate = offsets[0, region * layout.frames + extra]
            anchor = candidate // layout.band
            over = (anchor <= band) & (band <= anchor + 2)
            frame, row = jnp.where(over, extra, frame), jnp.where(over, candidate, row)
        slot = (band - row // layout.band == 1).astype(jnp.int32)
        for plane in range(2):
            total = strips[0][frame, plane, slot]
            for strip in strips[1:]:
                total += strip[frame, plane, slot]
            out[plane] = total


class Cover:
    def __init__(self, layout, offsets, region, band, core):
        row, self.column = frame_over(offsets, region, band, layout)
        anchor = row // layout.band
        self.lead = row - anchor * layout.band
        self.step = band - anchor
        self.first = core * layout.strip
        self.layout = layout

    def inside(self):
        band = self.layout.band
        middle = (self.step == 1) | (self.step == 2)
        begin = jnp.where(self.step == 0, self.lead, jnp.where(middle, 0, band))
        end = jnp.where(self.step == 2, self.lead, band)
        shape = (self.layout.strip, self.layout.length)
        rows = lax.broadcasted_iota(jnp.int32, shape, 0) + self.first
        return (rows >= begin) & (rows < end)

    def start(self):
        slot = (self.step == 1).astype(jnp.int32)
        length = self.layout.length
        return (slot * self.layout.band + self.first + length - self.lead) % length

    def add(self, total, terms):
        tiles = self.layout.length // lanes
        shift = self.column % lanes
        begin = pl.multiple_of(self.column - shift, lanes)
        spilled = lax.broadcasted_iota(jnp.int32, (terms.shape[0], lanes), 1) < shift
        turned = [
            pltpu.roll(terms[:, tile * lanes : (tile + 1) * lanes], shift, 1) for tile in range(tiles)
        ]
        for tile in range(tiles + 1):
            near = turned[tile] if tile < tiles else 0.0
            over = turned[tile - 1] if tile else 0.0
            total[:, pl.ds(begin + tile * lanes, lanes)] += jnp.where(spilled, over, near)


def density_kernel(layout, offsets, owner, *refs):
    powers, (out, doubled, total) = refs[: layout.cores], refs[layout.cores :]
    upper, lower, _, core = layout.place()
    strip, length = layout.strip, layout.length
    band = band_of_block(owner, upper * layout.lowers + lower, layout)
    power = powers[0][...]
    for more in powers[1:]:
        power += more[...]
    doubled[:length] = power
    doubled[length:] = power
    total[...] = jnp.zeros_like(total)
    for region in range(layout.regions):
        cover = Cover(layout, offsets, region, band, core)
        start = cover.start()
        near = doubled[pl.ds(pl.multiple_of(start // 8 * 8, 8), strip + 8), :]
        near = pltpu.roll(near, (strip + 8 - start % 8) % (strip + 8), 0)[:strip]
        cover.add(total, jnp.where(cover.inside(), near, 0.0))
    out[...] = total[:, : layout.width] + object_damping


def place_kernel(layout, offsets, owner, *refs):
    arrived, (out, total) = refs[: layout.lowers], refs[layout.lowers :]
    upper, lower, twin, core = layout.place()
    strip = layout.strip
    band = band_of_block(owner, upper * layout.lowers + lower, layout)
    total[...] = jnp.zeros_like(total)
    for step, terms in enumerate(arrived):
        source = layout.across(lower, step if layout.paired else layout.lowers - step)
        cover = Cover(layout, offsets, twin * layout.lowers + source, band, core)
        inside = cover.inside()
        kept = [jnp.where(inside, terms[plane], 0.0) for plane in range(2)]
        cover.add(total, jnp.concatenate(kept, axis=0))
    for plane in range(2):
        out[plane] = total[plane * strip : (plane + 1) * strip, : layout.width]


def update_kernel(layout, density, block, *refs):
    placed, out = refs[:-1], refs[-1]
    _, _, _, core = layout.place()
    rows = pl.ds(pl.multiple_of(core * layout.strip, layout.strip), layout.strip)
    for plane in range(2):
        total = placed[0][plane]
        for more in placed[1:]:
            total += more[plane]
        out[plane] = block[plane, rows, :] + total / density[...]


def join_kernel(layout, first, *refs):
    strips, (out, done) = refs[:-2], refs[-2:]
    _, _, _, core = layout.place()
    copies = []
    for step, strip in enumerate(strips, start=first):
        row = (core + step) % layout.cores * layout.strip
        rows = pl.ds(pl.multiple_of(row, layout.strip), layout.strip)
        copies.append(pltpu.make_async_copy(strip, out.at[:, rows, :], done.at[step]))
    for copy in copies:
        copy.start()
    for copy in copies:
        copy.wait()


def call(kernel, name, operands, outputs, scratch=(), scalar_count=0, after=()):
    shapes = [jax.ShapeDtypeStruct(shape, single) for shape in outputs]
    count = len(operands)

    def inner(*refs):
        tables = [Table(ref) for ref in refs[:scalar_count]]
        kernel(*tables, *refs[scalar_count:count], *refs[count + len(after) :])

    return pl.pallas_call(
        inner,
        name=name,
        out_shape=shapes,
        in_specs=[on_chip] * count
        + [pl.BlockSpec(memory_space=pl.ANY)] * len(after),
        out_specs=[on_chip] * len(shapes),
        scratch_shapes=[pltpu.VMEM(shape, single) for shape in scratch],
        compiler_params=pltpu.CompilerParams(vmem_limit_bytes=28 * 2**20),
    )(*operands, *after)


def body(measured, probe_modes, object_bands, scan_offsets, band_owner):
    layout = Layout(
        lax.axis_size("region"),
        lax.axis_size("mode"),
        measured.shape[1],
        measured.shape[0],
        probe_modes.shape[1] * lax.axis_size("mode"),
        object_bands.shape[2],
    )
    regions, halves, cores = layout.regions, layout.halves, layout.cores
    length, piece, frames = layout.length, layout.piece, layout.frames
    local, strip = layout.local_modes, layout.strip
    forward, back = fourier_tables(length)
    corners, owners = scan_offsets.T, band_owner[None]

    def from_cores(array):
        return [array] + [layout.from_core(array, step) for step in range(1, cores)]

    def from_uppers(array):
        return [array] + [layout.from_upper(array, step) for step in range(1, halves)]

    *cuts, part_measured = pl.pallas_call(
        functools.partial(cut_kernel, layout),
        name="cut",
        out_shape=[jax.ShapeDtypeStruct((2, strip, length), single)] * layout.lowers
        + [jax.ShapeDtypeStruct((frames, layout.part, length), single)],
        in_specs=[pl.BlockSpec(memory_space=pltpu.HBM)] * 4,
        out_specs=[on_chip] * (layout.lowers + 1),
        scratch_shapes=[
            pltpu.VMEM((2, strip, layout.width + lanes), single),
            pltpu.SMEM(corners.shape, jnp.int32),
            pltpu.SMEM(band_owner.shape, jnp.int32),
            pltpu.SemaphoreType.DMA((4,)),
        ],
        compiler_params=pltpu.CompilerParams(vmem_limit_bytes=28 * 2**20),
    )(
        *(
            pltpu.with_memory_space_constraint(array, pltpu.HBM)
            for array in (corners, band_owner, object_bands, measured)
        )
    )
    part_measured, held_probes = lax.optimization_barrier((part_measured, probe_modes))
    probes = [probe_modes] + [layout.from_twin(held_probes, step) for step in range(1, halves)]
    if halves > 1:
        pairs = [
            (layout.device(t, l, t, c), layout.device(u, l, t, c))
            for u, l, t, c in layout.everyone()
            if u != t
        ]
        part_measured = lax.ppermute(part_measured, axes, pairs)
    cuts = [cuts[0]] + [layout.to_row(cut, step) for step, cut in enumerate(cuts[1:], start=1)]
    chosen = []
    for steps in ((0,), tuple(range(1, layout.lowers))):
        chosen = call(
            functools.partial(choose_kernel, layout, steps),
            "choose",
            (corners, owners, *(cuts[step] for step in steps), *chosen),
            [(frames, 2, 2, strip, length)],
            scalar_count=2,
        )
    (chosen,) = chosen
    measured_parts = from_cores(part_measured)
    (roots,) = call(
        functools.partial(order_kernel, layout),
        "order",
        (measured, *measured_parts),
        [measured.shape],
        scratch=[(cores, layout.part, length)],
    )
    parts = from_uppers(chosen)
    held, roots = lax.optimization_barrier((chosen, roots))
    strips = list(parts)
    for step in range(1, cores):
        strips += [layout.from_core(part, step) for part in [held] + parts[1:]]
    every_probe = list(probes)
    for step in range(1, cores):
        every_probe += [layout.from_core(probe, step) for probe in probes]
    windows, pieces, old_pieces = call(
        functools.partial(first_kernel, layout),
        "first",
        (corners, *strips, *every_probe, roots, forward, back),
        [
            (frames, 2, length, length),
            (regions, 2 * local * piece + piece // halves, length),
            (halves, local, 2, piece, length),
        ],
        scratch=[
            (2, 2, cores, strip, length),
            (2, halves * local * length, length),
        ],
        scalar_count=1,
    )
    pieces = layout.within_cube(pieces)
    (total,) = call(sum_kernel, "sum", (pieces,), [pieces.shape[1:]])
    (spread,) = call(
        functools.partial(step_kernel, layout),
        "step",
        (old_pieces, *from_uppers(total)),
        [(regions, halves, local, 2, piece, length)],
    )
    new_probes = layout.within_cube(spread)
    (probe_out,) = call(
        functools.partial(probe_kernel, layout),
        "probe",
        (new_probes,),
        [(2, local, length, length)],
    )
    probe_power, intensity, fars = call(
        functools.partial(again_kernel, layout),
        "again",
        (new_probes, windows, forward, back),
        [
            (length, length),
            (frames, length, length),
            (frames, 2, halves * local * length, length),
        ],
    )
    strips = call(
        functools.partial(terms_kernel, layout),
        "terms",
        (corners, *from_cores(intensity), roots, new_probes, fars, forward, back),
        [(frames, 2, 2, strip, length)] * cores,
        scratch=[(2, 2, cores, strip, length)],
        scalar_count=1,
    )
    strips = [strips[0]] + [
        layout.from_core(sent, step) for step, sent in enumerate(strips[1:], start=1)
    ]
    posted = call(
        functools.partial(post_kernel, layout),
        "post",
        (corners, owners, *strips),
        [(2, strip, length)] * layout.lowers,
        scalar_count=2,
    )
    posted = [posted[0]] + [
        layout.to_row(sent, step) for step, sent in enumerate(posted[1:], start=1)
    ]
    (density,) = call(
        functools.partial(density_kernel, layout),
        "density",
        (corners, owners, *from_cores(probe_power)),
        [(strip, layout.width)],
        scratch=[(2 * length, length), (strip, layout.width + lanes)],
        scalar_count=2,
        after=(probe_out,),
    )
    (placed,) = call(
        functools.partial(place_kernel, layout),
        "place",
        (corners, owners, *posted),
        [(2, strip, layout.width)],
        scratch=[(2 * strip, layout.width + lanes)],
        scalar_count=2,
    )
    placed = [placed] + [layout.from_twin(placed, step) for step in range(1, halves)]
    (new_rows,) = call(
        functools.partial(update_kernel, layout),
        "update",
        (density, object_bands, *placed),
        [(2, strip, layout.width)],
    )
    whole = pl.BlockSpec(memory_space=pl.ANY)
    settings = {
        "name": "join",
        "out_shape": jax.ShapeDtypeStruct(object_bands.shape, single),
        "out_specs": whole,
        "scratch_shapes": [pltpu.SemaphoreType.DMA((cores,))],
        "compiler_params": pltpu.CompilerParams(vmem_limit_bytes=28 * 2**20),
    }
    own, *others = from_cores(new_rows)
    object_out = pl.pallas_call(
        functools.partial(join_kernel, layout, 0), in_specs=[on_chip], **settings
    )(own)
    if others:
        object_out = pl.pallas_call(
            lambda before, *refs: join_kernel(layout, 1, *refs),
            in_specs=[whole] + [on_chip] * len(others),
            input_output_aliases={0: 0},
            **settings,
        )(object_out, *others)
    return probe_out, object_out


def solution(mesh):
    in_specs = (
        P("region", None, None),
        P(None, "mode", None, None),
        P(None, "region", None),
        P(),
        P(),
    )
    out_specs = (P(None, "mode", None, None), P(None, "region", None))
    return jax.shard_map(body, mesh=mesh, in_specs=in_specs, out_specs=out_specs, check_vma=False)
```
